32 devices in a mesh: dp: 2 (over y), seq: 16 (over z, x, core).
Axes of the slice: x: 2, y: 2, z: 4, core: 2. Of those that a mesh axis runs over, the one named last changes fastest.
Arguments:
- block_input: bfloat16 [2, 2048, 2048], P('dp', 'seq'), may hold values from -6 to 6
- attention_gain: bfloat16 [2048], P(('dp', 'seq')), may hold values from 0.5 to 1.5
- query_weight: bfloat16 [2048, 2048], P(('dp', 'seq')), may hold values from -0.125 to 0.125
- keyvalue_weight: bfloat16 [2048, 256], P(('dp', 'seq')), may hold values from -0.125 to 0.125
- output_weight: bfloat16 [2048, 2048], P(('dp', 'seq')), may hold values from -0.5 to 0.5
- feedforward_gain: bfloat16 [2048], P(('dp', 'seq')), may hold values from 0.5 to 1.5
- gate_weight: bfloat16 [2048, 5632], P(('dp', 'seq')), may hold values from -0.125 to 0.125
- up_weight: bfloat16 [2048, 5632], P(('dp', 'seq')), may hold values from -0.125 to 0.125
- down_weight: bfloat16 [2048, 5632], P(('dp', 'seq')), may hold values from -0.078125 to 0.078125
- document_lengths: int32 [2, 32], P('dp'), may hold values from 1 to 1024, 2048 in all within a row
- piece_order: int32 [32], replicated, may hold values from 0 to 31, each once
- output_grad: bfloat16 [2, 2048, 2048], P('dp', 'seq'), may hold values from -6 to 6
- shared_grad: bfloat16 [2, 2048, 256], P('dp', 'seq'), may hold values from -6 to 6
Outputs:
- block_output: bfloat16 [2, 2048, 2048], P('dp', 'seq')
- shared_keyvalue: bfloat16 [2, 2048, 256], P('dp', 'seq')
- input_grad: float32 [2, 2048, 2048], P('dp', 'seq')
- attention_gain_grad: float32 [2048], P(('dp', 'seq'))
- query_weight_grad: float32 [2048, 2048], P(('dp', 'seq'))
- keyvalue_weight_grad: float32 [2048, 256], P(('dp', 'seq'))
- output_weight_grad: float32 [2048, 2048], P(('dp', 'seq'))
- feedforward_gain_grad: float32 [2048], P(('dp', 'seq'))
- gate_weight_grad: float32 [2048, 5632], P(('dp', 'seq'))
- up_weight_grad: float32 [2048, 5632], P(('dp', 'seq'))
- down_weight_grad: float32 [2048, 5632], P(('dp', 'seq'))
The draws below stay inside these ranges and needn't reach their ends.
Inputs may be any that keep to these rules, and one draw needn't show every extreme that they name: `document_lengths`: each row sums to 2048, and its largest entry is 1024. `piece_order`: a permutation: every piece of the stream appears once.
All inputs are finite; a program needn't handle non-finite values.
Results may differ from the reference program's by a relative error of at most 0.015.
Values may be sent and summed in bfloat16 or wider, within the bound.
No kernel may reach another device: no remote copies, remote signals or barrier semaphores. Data moves between devices by JAX's collectives and lax.ppermute only.
A program may use at most 512 MiB of HBM per device.

```python
import math
import jax
import jax.numpy as jnp
import numpy as np
from jax import lax

D = 2048
HEADS = 16
HEAD_DIM = 128
FF = 5632
DOCS = 32
PIECE = 64
PIECES = 32
STREAM = 2048
STREAMS = 2
MOST = 1024


def strengthened(drawn, own_key, source, target, parts, factor):
    owner, partner = [(jnp.arange(drawn.shape[axis_at]) // (drawn.shape[axis_at] // parts)).reshape([-1 if axis == axis_at else 1 for axis in range(drawn.ndim)]) for axis_at in (source, target)]
    chosen = jax.random.permutation(own_key, parts)[partner]
    strong = (owner == chosen) | (owner == (partner + parts // 2) % parts)
    return jnp.where(strong, factor * drawn, drawn)


def steps_of(stream_key, dims, cuts, smallest, top_value):
    factor_of, own = 1.0, jax.random.fold_in(stream_key, 6)
    for axis_at, blocks in cuts:
        heights = jnp.exp(jax.random.uniform(jax.random.fold_in(own, axis_at), (blocks,), jnp.float32, smallest / len(cuts), top_value / len(cuts)))
        factor_of = factor_of * jnp.repeat(heights, dims[axis_at] // blocks).reshape([-1 if axis == axis_at else 1 for axis in range(len(dims))])
    return factor_of


def profile(amount, total, bound, slope):
    weights = [(1 << 20) // math.isqrt(grade ** slope) + 1 for grade in range(2, amount + 1)]
    rest, holding = total - bound - (amount - 1), [1] * (amount - 1)
    while rest > 0:
        candidates = [i for i in range(amount - 1) if holding[i] < bound]
        mass, left = sum([weights[i] for i in candidates]), rest
        for i in candidates:
            addition = min(bound - holding[i], max(1, left * weights[i] // mass), rest)
            holding[i] = holding[i] + addition
            rest = rest - addition
    return np.array([bound] + holding)


def ragged_sizes(rng, number_of, total, most, skew):
    if number_of == 2:
        one = jax.random.randint(rng, (), max(1, total - most), min(most, total - 1) + 1)
        return jnp.stack([one, total - one])
    sizes = jnp.asarray(profile(number_of, total, most, skew), jnp.int32)
    twos = (number_of - 1) // 2
    donor, taker = sizes[1:1 + 2 * twos:2], sizes[2:2 + 2 * twos:2]
    slack = jnp.minimum(donor - 1, most - taker)
    moved = jax.random.randint(jax.random.fold_in(rng, 1), (twos,), 0, 1 << 20) % (slack + 1)
    sizes = sizes.at[1:1 + 2 * twos:2].set(donor - moved).at[2:2 + 2 * twos:2].set(taker + moved)
    return sizes[jax.random.permutation(jax.random.fold_in(rng, 2), number_of)]


def centred(stream_key, extent, width, most, split=(), held_as=jnp.bfloat16):
    values = width * jax.random.normal(stream_key, extent, jnp.float32)
    if split:
        values = values * steps_of(stream_key, extent, split, -0.22, 0.18)
    return jnp.clip(values, -most, most).astype(held_as)


def gaussian_with(stream_key, extent, spread, most, shards, heavy, kind=jnp.bfloat16):
    drawn = spread * jax.random.normal(stream_key, extent, jnp.float32)
    if shards:
        drawn = drawn * steps_of(stream_key, extent, shards, -0.22, 0.18)
    return jnp.clip(strengthened(drawn, jax.random.fold_in(stream_key, 3), *heavy), -most, most).astype(kind)


def setup_inputs(seed: int = 0) -> dict:
    arg_keys = jax.random.split(jax.random.key(seed), 14)
    return {
        "block_input": gaussian_with(arg_keys[0], (STREAMS, STREAM, D), 1.0, 6.0, ((0, 2), (1, 16)), (1, 2, 16, 2.0)),
        "attention_gain": jnp.clip(1.0 + 0.1 * jax.random.normal(arg_keys[1], (D,), jnp.float32), 0.5, 1.5).astype(jnp.bfloat16),
        "query_weight": centred(arg_keys[2], (D, HEADS * HEAD_DIM), D ** -0.5, 0.125, ((0, 32),)),
        "keyvalue_weight": centred(arg_keys[3], (D, 2 * HEAD_DIM), D ** -0.5, 0.125, ((0, 32),)),
        "output_weight": centred(arg_keys[4], (D, HEADS * HEAD_DIM), (HEADS * HEAD_DIM // 16) ** -0.5, 0.5, ((0, 32),)),
        "feedforward_gain": jnp.clip(1.0 + 0.1 * jax.random.normal(arg_keys[5], (D,), jnp.float32), 0.5, 1.5).astype(jnp.bfloat16),
        "gate_weight": centred(arg_keys[6], (D, FF), D ** -0.5, 0.125, ((0, 32),)),
        "up_weight": centred(arg_keys[7], (D, FF), D ** -0.5, 0.125, ((0, 32),)),
        "down_weight": centred(arg_keys[8], (D, FF), FF ** -0.5, 0.078125, ((0, 32),)),
        "document_lengths": jax.vmap(lambda own: ragged_sizes(own, DOCS, STREAM, MOST, 2))(jax.random.split(arg_keys[9], STREAMS)).reshape((STREAMS, DOCS)).astype(jnp.int32),
        "piece_order": jax.random.permutation(arg_keys[10], PIECES).astype(jnp.int32),
        "output_grad": centred(arg_keys[11], (STREAMS, STREAM, D), 1.0, 6.0, ((0, 2), (1, 16))),
        "shared_grad": centred(arg_keys[12], (STREAMS, STREAM, 2 * HEAD_DIM), 1.0, 6.0, ((0, 2), (1, 16))),
    }


EPSILON = 1e-05
HIGHEST = lax.Precision.HIGHEST

@jax.custom_vjp
def low(v):
    return lax.optimization_barrier(v.astype(jnp.bfloat16)).astype(jnp.float32)

@jax.custom_vjp
def low_back(v):
    return v

def low_keep(v):
    return (low(v), None)

def low_pass(kept, grad):
    return (grad,)

def back_keep(v):
    return (v, None)

def back_low(kept, grad):
    return (low(grad),)
low.defvjp(low_keep, low_pass)
low_back.defvjp(back_keep, back_low)

def matmul(left, right):
    return jnp.dot(left, right, precision=HIGHEST)

def matmul_t(left, right):
    return lax.dot_general(left, right, (((1,), (1,)), ((), ())), precision=HIGHEST)

def layout(lengths, order):
    position = (order[:, None] * PIECE + jnp.arange(PIECE, dtype=jnp.int32)[None, :]).reshape(-1).astype(jnp.int32)
    finish = jnp.cumsum(lengths).astype(jnp.int32)
    starts = (finish - lengths).astype(jnp.int32)
    segment = lax.optimization_barrier(jnp.sum((finish[None, :] <= position[:, None]).astype(jnp.int32), axis=1)).astype(jnp.int32)
    begins = lax.optimization_barrier(jnp.max(jnp.where(starts[None, :] <= position[:, None], starts[None, :], 0), axis=1)).astype(jnp.int32)
    return (position, segment, (position - begins).astype(jnp.int32))

def angles(offset):
    half_dim = HEAD_DIM // 2
    frequency = jnp.exp(jnp.arange(half_dim, dtype=jnp.float32) * (-2.0 * math.log(10000.0) / HEAD_DIM))
    phases = offset.astype(jnp.float32)[:, None] * frequency[None, :]
    return (jnp.cos(phases), jnp.sin(phases))

def rotate(vectors, cosine, sine_part):
    half_dim = vectors.shape[-1] // 2
    first_half = vectors[..., :half_dim]
    second_half = vectors[..., half_dim:]
    return jnp.concatenate([first_half * cosine - second_half * sine_part, second_half * cosine + first_half * sine_part], -1)

def attend(query_rot, key_rot, value_low, position, segment):
    row_block = min(256, STREAM)
    block_count = STREAM // row_block
    score_scale = 1.0 / math.sqrt(HEAD_DIM)
    query_blocks = query_rot.reshape(block_count, row_block, HEADS, HEAD_DIM)
    place_blocks = position.reshape(block_count, row_block)
    segment_blocks = segment.reshape(block_count, row_block)

    @jax.checkpoint
    def one_block(block_item):
        query_part, place_part, segment_part = block_item
        scores = low_back(jnp.einsum('bhd,kd->hbk', query_part, key_rot, precision=HIGHEST) * score_scale)
        allowed = (segment_part[:, None] == segment[None, :]) & (position[None, :] <= place_part[:, None])
        scores = jnp.where(allowed[None], scores, -1e+30)
        weights = jax.nn.softmax(scores, axis=-1)
        result = jnp.einsum('hbk,kd->bhd', weights, value_low, precision=HIGHEST)
        return result.reshape(row_block, HEADS * HEAD_DIM)
    return lax.map(one_block, (query_blocks, place_blocks, segment_blocks)).reshape(STREAM, HEADS * HEAD_DIM)

def stream_forward(inputs, gain_one, query_matrix, keyvalue_matrix, output_matrix, gain_two, gate_matrix, up_matrix, down_matrix, position, segment, offset):
    scale_one = lax.rsqrt(lax.optimization_barrier(jnp.mean(inputs * inputs, axis=-1, keepdims=True)) + EPSILON)
    normed_one = low(inputs * scale_one * gain_one)
    query = low_back(matmul(normed_one, query_matrix))
    keyvalue = low_back(matmul(normed_one, keyvalue_matrix))
    cosine, sine_part = angles(offset)
    query_rot = low(rotate(query.reshape(STREAM, HEADS, HEAD_DIM), cosine[:, None, :], sine_part[:, None, :]))
    key_rot = low(rotate(keyvalue[:, :HEAD_DIM], cosine, sine_part))
    value_low = low(keyvalue[:, HEAD_DIM:])
    attended = attend(query_rot, key_rot, value_low, position, segment)
    attended_low = low(low_back(attended))
    hidden = inputs + low_back(matmul_t(attended_low, output_matrix))
    scale_two = lax.rsqrt(lax.optimization_barrier(jnp.mean(hidden * hidden, axis=-1, keepdims=True)) + EPSILON)
    normed_two = low(hidden * scale_two * gain_two)
    gate = low_back(matmul(normed_two, gate_matrix))
    up_part = low_back(matmul(normed_two, up_matrix))
    mixed = low(jax.nn.silu(gate) * up_part)
    result = hidden + matmul_t(mixed, down_matrix)
    return (result, jnp.concatenate([key_rot, value_low], -1))

def reference(block_input, attention_gain, query_weight, keyvalue_weight, output_weight, feedforward_gain, gate_weight, up_weight, down_weight, document_lengths, piece_order, output_grad, shared_grad):
    layouts = [layout(document_lengths[stream], piece_order) for stream in range(STREAMS)]

    def forward(inputs, gain_one, query_matrix, keyvalue_matrix, output_matrix, gain_two, gate_matrix, up_matrix, down_matrix):
        results = [stream_forward(inputs[stream], gain_one, query_matrix, keyvalue_matrix, output_matrix, gain_two, gate_matrix, up_matrix, down_matrix, *layouts[stream]) for stream in range(STREAMS)]
        return (jnp.stack([pair[0] for pair in results]), jnp.stack([pair[1] for pair in results]))
    primals = tuple((array.astype(jnp.float32) for array in (block_input, attention_gain, query_weight, keyvalue_weight, output_weight, feedforward_gain, gate_weight, up_weight, down_weight)))
    (result, shared), pullback = jax.vjp(forward, *primals)
    grads = pullback((output_grad.astype(jnp.float32), shared_grad.astype(jnp.float32)))
    return (result.astype(jnp.bfloat16), shared.astype(jnp.bfloat16), grads[0], grads[1], grads[2], grads[3], grads[4], grads[5], grads[6], grads[7], grads[8])
```

```python
import math

import jax
import jax.numpy as jnp
from jax import lax
from jax.sharding import Mesh
from jax.sharding import PartitionSpec as P

HEAD_DIM = 128
EPSILON = 1e-05
NEGATIVE = -1e30
Z = 4
BF16 = jnp.bfloat16
F32 = jnp.float32


def angles(offset):
    half_dim = HEAD_DIM // 2
    frequency = jnp.exp(
        jnp.arange(half_dim, dtype=F32) * (-2.0 * math.log(10000.0) / HEAD_DIM)
    )
    phases = offset.astype(F32)[:, None] * frequency[None, :]
    return (jnp.cos(phases), jnp.sin(phases))


def rotate(vectors, cosine, sine_part):
    half_dim = vectors.shape[-1] // 2
    first, second = vectors[..., :half_dim], vectors[..., half_dim:]
    return jnp.concatenate(
        [first * cosine - second * sine_part, second * cosine + first * sine_part], -1
    )


def dot(left, right):
    return jnp.dot(left, right, preferred_element_type=F32)


def contract_last(left, right):
    return lax.dot_general(left, right, (((1,), (1,)), ((), ())), preferred_element_type=F32)


def contract_first(left, right):
    return lax.dot_general(left, right, (((0,), (0,)), ((), ())), preferred_element_type=F32)


def norm_back(grad_normed, normed, scale_rows):
    return scale_rows * (
        grad_normed - normed * jnp.mean(grad_normed * normed, axis=-1, keepdims=True)
    )


def swap(value, axis):
    return lax.ppermute(value, axis, [(0, 1), (1, 0)])


def hop(value, k):
    return lax.ppermute(value, "z", [(i, i ^ k) for i in range(Z)])


def pick(stacked, index, axis=0):
    return lax.dynamic_index_in_dim(stacked, index, axis, keepdims=False)


def put(pieces, indices, axis):
    shape = list(pieces[0].shape)
    shape.insert(axis, len(pieces))
    result = jnp.zeros(shape, pieces[0].dtype)
    for piece, index in zip(pieces, indices):
        result = lax.dynamic_update_index_in_dim(result, piece, index, axis)
    return result


def pair(own, other, index, axis=0):
    return jnp.where(
        index == 0, jnp.stack([own, other], axis), jnp.stack([other, own], axis)
    )


def on_device(
    block_input,
    attention_gain,
    query_weight,
    keyvalue_weight,
    output_weight,
    feedforward_gain,
    gate_weight,
    up_weight,
    down_weight,
    document_lengths,
    piece_order,
    output_grad,
    shared_grad,
):
    y, z, m, x, c = (lax.axis_index(a) for a in "yzmxc")
    M = lax.axis_size("m")
    tokens, width = block_input.shape[1:]
    rows = query_weight.shape[0]
    query_width = query_weight.shape[1]
    half_width = query_width // 2
    heads = half_width // HEAD_DIM
    hidden_units = gate_weight.shape[1]
    part = hidden_units // Z
    piece_len = tokens // 2
    others = [z ^ k for k in range(Z)]

    def inward(value):
        value = value.reshape(tokens, 2, Z, M, 2, 2, rows).transpose(0, 5, 1, 4, 3, 2, 6)
        value = jnp.where(c == 0, value, value[:, ::-1])
        value = jnp.where(y == 0, value, value[:, :, ::-1])
        return value.reshape(tokens, width)

    def outward(value):
        value = value.reshape(tokens, 2, 2, 2, M, Z, rows)
        value = jnp.where(y == 0, value, value[:, :, ::-1])
        value = jnp.where(c == 0, value, value[:, ::-1])
        return value.transpose(0, 2, 5, 4, 3, 1, 6).reshape(tokens, width)

    def turn(value):
        parts = value.reshape(tokens, 4, 2, width // 8)
        return jnp.where(x == 0, parts, parts[:, :, ::-1]).reshape(tokens, width)

    def gather_z(value):
        return [value] + [hop(value, k) for k in range(1, Z)]

    def gather_m(value, axis):
        return lax.all_gather(value, "m", axis=axis) if M > 1 else jnp.expand_dims(value, axis)

    def scatter_m(value, axis):
        if M > 1:
            return lax.psum_scatter(value, "m", scatter_dimension=axis)
        return lax.squeeze(value, (axis,))

    finish = jnp.cumsum(document_lengths[0])
    starts = finish - document_lengths[0]

    def places(slots):
        order = piece_order[(slots[:, None] * 2 + jnp.arange(2)[None, :]).reshape(-1)]
        position = (
            order[:, None] * piece_len + jnp.arange(piece_len, dtype=jnp.int32)[None, :]
        ).reshape(-1)
        segment = jnp.sum((finish[None, :] <= position[:, None]).astype(jnp.int32), axis=1)
        begins = jnp.max(
            jnp.where(starts[None, :] <= position[:, None], starts[None, :], 0), axis=1
        )
        return position, segment, position - begins

    def slot(z_at, m_at, x_at, c_at):
        return ((z_at * M + m_at) * 2 + x_at) * 2 + c_at

    query_slots = jnp.stack([slot(z, m, x, c), slot(z, m, 1 - x, c)])
    position, segment, offset = places(query_slots)
    key_slots = jnp.stack(
        [
            slot(z ^ k, m_at, x ^ i, c ^ j)
            for j in range(2)
            for i in range(2)
            for m_at in range(M)
            for k in range(Z)
        ]
    )
    key_position, key_segment, _ = places(key_slots)
    allowed = (key_segment[None, :] == segment[:, None]) & (
        key_position[None, :] <= position[:, None]
    )
    cosine, sine_part = angles(offset)

    gains = jnp.stack([attention_gain, feedforward_gain])
    gains = jnp.pad(gains, ((0, 14), (0, 2 * HEAD_DIM - rows)))
    small = jnp.concatenate([keyvalue_weight, gains])
    small = put(gather_z(small), others, 0)
    small = gather_m(small, 0)
    small_x = swap(small, "x")
    small_y = swap(small, "y")
    small_d = swap(small_x, "y")
    small = jnp.stack([pair(small, small_x, x), pair(small_y, small_d, x)])
    small = jnp.stack([small, swap(small, "c")])
    small = small.reshape(width // rows, rows + 16, 2 * HEAD_DIM)
    keyvalue_full = small[:, :rows].reshape(width, 2 * HEAD_DIM)
    gain_one = small[:, rows, :rows].reshape(1, width).astype(F32)
    gain_two = small[:, rows + 1, :rows].reshape(1, width).astype(F32)

    def gather_heads(weight):
        parts = weight.reshape(rows, 2, half_width).transpose(1, 0, 2)
        got = pair(pick(parts, x), swap(pick(parts, 1 - x), "x"), x)
        got = put(gather_z(got), others, 1)
        got = gather_m(got, 1).reshape(-1, half_width)
        got = jnp.concatenate([got, swap(got, "y")])
        return jnp.concatenate([got, swap(got, "c")])

    def scatter_heads(grad):
        grad = grad.astype(BF16)
        half = width // 2
        grad = grad[:half].astype(F32) + swap(grad[half:], "c").astype(F32)
        quarter = half // 2
        grad = grad[:quarter] + swap(grad[quarter:].astype(BF16), "y").astype(F32)
        grad = scatter_m(grad.reshape(2, M, Z, rows, half_width), 1)
        low = grad.astype(BF16)
        total = pick(grad, z, 1)
        for k in range(1, Z):
            total = total + hop(pick(low, z ^ k, 1), k).astype(F32)
        own = pick(total, x)
        other = swap(pick(total, 1 - x).astype(BF16), "x").astype(F32)
        return pair(own, other, x, 1).reshape(rows, query_width)

    query_full = gather_heads(query_weight)
    output_full = gather_heads(output_weight)

    stacked = jnp.stack([gate_weight, up_weight, down_weight])
    stacked = stacked.reshape(3, rows, Z, part).transpose(2, 0, 1, 3)
    got = [pick(stacked, z)] + [hop(pick(stacked, z ^ k), k) for k in range(1, Z)]
    got = put(got, others, 1)
    got = gather_m(got, 1).reshape(3, width // 8, part)
    got_x = swap(got, "x")
    got_y = swap(got, "y")
    mid = width // 16
    got_da = swap(got_x[:, :mid], "y")
    got_db = swap(got_y[:, mid:], "x")
    pieces = [got, got_x, got_y, got_da, got_db]
    pieces = pieces + [swap(piece, "c") for piece in pieces]
    gate_full, up_full, down_full = (
        jnp.concatenate([piece[i] for piece in pieces]) for i in range(3)
    )

    score_scale = 1.0 / math.sqrt(HEAD_DIM)
    input_mine = inward(block_input[0])
    input_pair = jnp.concatenate([input_mine, swap(input_mine, "x")])
    inputs = input_pair.astype(F32)
    scale_one = lax.rsqrt(jnp.mean(inputs * inputs, axis=-1, keepdims=True) + EPSILON)
    normed_one = inputs * scale_one
    normed_one_low = (normed_one * gain_one).astype(BF16)
    keyvalue_sum = dot(normed_one_low[:tokens], keyvalue_full)
    shared_mine = jnp.concatenate(
        [
            rotate(keyvalue_sum[:, :HEAD_DIM], cosine[:tokens], sine_part[:tokens]),
            keyvalue_sum[:, HEAD_DIM:],
        ],
        -1,
    ).astype(BF16)
    gathered = gather_m(jnp.stack(gather_z(shared_mine)), 0)
    gathered = jnp.stack([gathered, swap(gathered, "x")])
    gathered = jnp.stack([gathered, swap(gathered, "c")])
    gathered = gathered.reshape(-1, 2 * HEAD_DIM)
    key_all, value_all = gathered[:, :HEAD_DIM], gathered[:, HEAD_DIM:]
    query_rot = rotate(
        dot(normed_one_low, query_full).reshape(2 * tokens, heads, HEAD_DIM),
        cosine[:, None, :],
        sine_part[:, None, :],
    ).astype(BF16)
    scores = (
        jnp.einsum("thd,kd->htk", query_rot, key_all, preferred_element_type=F32) * score_scale
    )
    scores = jnp.where(allowed[None], scores, NEGATIVE)
    top = jnp.max(scores, axis=-1, keepdims=True)
    weights = jnp.exp(scores - top)
    total = jnp.sum(weights, axis=-1, keepdims=True)
    log_total = top + jnp.log(total)
    output_heads = (
        jnp.einsum("htk,kd->htd", weights.astype(BF16), value_all, preferred_element_type=F32)
        / total
    )
    attended_low = output_heads.transpose(1, 0, 2).reshape(2 * tokens, half_width).astype(BF16)
    branch = contract_last(attended_low, output_full)
    branch = branch[:tokens] + swap(branch[tokens:].astype(BF16), "x").astype(F32)
    hidden = inputs[:tokens] + branch

    scale_two = lax.rsqrt(jnp.mean(hidden * hidden, axis=-1, keepdims=True) + EPSILON)
    normed_two = hidden * scale_two
    normed_two_low = jnp.concatenate(gather_z(turn((normed_two * gain_two).astype(BF16))))
    grad_mine = inward(output_grad[0])
    grad_low = jnp.concatenate(gather_z(turn(grad_mine)))
    gate_sum = dot(normed_two_low, gate_full)
    up_sum = dot(normed_two_low, up_full)
    sigmoid_gate = jax.nn.sigmoid(gate_sum)
    silu_gate = gate_sum * sigmoid_gate
    mixed_low = (silu_gate * up_sum).astype(BF16)
    grad_mixed = dot(grad_low, down_full)
    grad_gate = (
        grad_mixed * up_sum * sigmoid_gate * (1.0 + gate_sum * (1.0 - sigmoid_gate))
    ).astype(BF16)
    grad_up = (grad_mixed * silu_gate).astype(BF16)

    def scatter_z(value):
        value = value.reshape(Z, tokens, width)
        low = value.astype(BF16)
        result = value[0]
        for k in range(1, Z):
            result = result + hop(low[k], k).astype(F32)
        return turn(result)

    grad_two = scatter_z(contract_last(grad_gate, gate_full) + contract_last(grad_up, up_full))
    feed_out = scatter_z(contract_last(mixed_low, down_full))
    block_output = outward((hidden + feed_out).astype(BF16))[None]
    gain_two_grad = jnp.sum(grad_two * normed_two, axis=0)
    grad_hidden = grad_mine.astype(F32) + norm_back(grad_two * gain_two, normed_two, scale_two)

    grad_hidden_low = grad_hidden.astype(BF16)
    grad_hidden_low = jnp.concatenate([grad_hidden_low, swap(grad_hidden_low, "x")])
    grad_heads = (
        dot(grad_hidden_low, output_full).astype(BF16).reshape(2 * tokens, heads, HEAD_DIM)
    )
    delta = jnp.einsum("thd,htd->ht", grad_heads, output_heads, preferred_element_type=F32)
    scores = (
        jnp.einsum("thd,kd->htk", query_rot, key_all, preferred_element_type=F32) * score_scale
    )
    probs = jnp.where(allowed[None], jnp.exp(scores - log_total), 0.0)
    grad_probs = jnp.einsum("thd,kd->htk", grad_heads, value_all, preferred_element_type=F32)
    grad_scores = (probs * (grad_probs - delta[..., None])).astype(BF16)
    grad_query = jnp.einsum("htk,kd->thd", grad_scores, key_all, preferred_element_type=F32)
    grad_key = jnp.einsum("htk,thd->kd", grad_scores, query_rot, preferred_element_type=F32)
    grad_value = jnp.einsum(
        "htk,thd->kd", probs.astype(BF16), grad_heads, preferred_element_type=F32
    )
    kv_grad = jnp.concatenate([grad_key * score_scale, grad_value], -1)
    half = kv_grad.shape[0] // 2
    kv_grad = kv_grad[:half] + swap(kv_grad[half:].astype(BF16), "c").astype(F32)
    half = half // 2
    kv_grad = kv_grad[:half] + swap(kv_grad[half:].astype(BF16), "x").astype(F32)
    kv_grad = scatter_m(kv_grad.reshape(M, Z, tokens, 2 * HEAD_DIM), 0)
    kv_low = kv_grad.astype(BF16)
    kv_mine = kv_grad[0]
    for k in range(1, Z):
        kv_mine = kv_mine + hop(kv_low[k], k).astype(F32)
    kv_mine = kv_mine + shared_grad[0].astype(F32)
    query_grad_low = (
        rotate(grad_query * score_scale, cosine[:, None, :], -sine_part[:, None, :])
        .reshape(2 * tokens, half_width)
        .astype(BF16)
    )
    keyvalue_grad_low = jnp.concatenate(
        [
            rotate(kv_mine[:, :HEAD_DIM], cosine[:tokens], -sine_part[:tokens]),
            kv_mine[:, HEAD_DIM:],
        ],
        -1,
    ).astype(BF16)
    grad_one = contract_last(query_grad_low, query_full)
    grad_one = grad_one[:tokens] + swap(grad_one[tokens:].astype(BF16), "x").astype(F32)
    grad_one = grad_one + contract_last(keyvalue_grad_low, keyvalue_full)
    normed_mine = normed_one[:tokens]
    gain_one_grad = jnp.sum(grad_one * normed_mine, axis=0)
    input_grad = outward(
        grad_hidden + norm_back(grad_one * gain_one, normed_mine, scale_one[:tokens])
    )[None]

    def scatter_feed(grad):
        grad = grad.astype(BF16)
        half = width // 2
        grad = grad[:half].astype(F32) + swap(grad[half:], "c").astype(F32)
        own, by_x, by_y, by_d = (grad[i * 2 * mid : (i + 1) * 2 * mid] for i in range(4))
        by_d = by_d.astype(BF16)
        from_y = swap(by_d[:mid], "y").astype(F32)
        from_x = swap(by_d[mid:], "x").astype(F32)
        by_x = jnp.concatenate([by_x[:mid] + from_y, by_x[mid:]]).astype(BF16)
        by_y = jnp.concatenate([by_y[:mid], by_y[mid:] + from_x]).astype(BF16)
        own = own + swap(by_x, "x").astype(F32) + swap(by_y, "y").astype(F32)
        own = scatter_m(own.reshape(M, Z, rows, part), 0).astype(BF16)
        got = [pick(own, z)] + [hop(pick(own, z ^ k), k) for k in range(1, Z)]
        return put(got, others, 0).transpose(1, 0, 2).reshape(rows, hidden_units).astype(F32)

    down_weight_grad = scatter_feed(contract_first(grad_low, mixed_low))
    gate_weight_grad = scatter_feed(contract_first(normed_two_low, grad_gate))
    up_weight_grad = scatter_feed(contract_first(normed_two_low, grad_up))
    output_weight_grad = scatter_heads(contract_first(grad_hidden_low, attended_low))
    query_weight_grad = scatter_heads(contract_first(normed_one_low, query_grad_low))

    small_grad = contract_first(normed_one_low[:tokens], keyvalue_grad_low)
    small_gains = jnp.stack([gain_one_grad, gain_two_grad], -1)
    small_gains = jnp.pad(small_gains, ((0, 0), (0, HEAD_DIM - 2)))
    small_grad = jnp.concatenate([small_grad, small_gains], -1)
    half = width // 2
    small_grad = small_grad[:half] + swap(small_grad[half:].astype(BF16), "c").astype(F32)
    half = half // 2
    small_grad = small_grad[:half] + swap(small_grad[half:].astype(BF16), "y").astype(F32)
    small_grad = small_grad.reshape(2, M, Z, rows, 3 * HEAD_DIM)
    small_grad = pick(small_grad, x) + swap(pick(small_grad, 1 - x).astype(BF16), "x").astype(F32)
    small_grad = scatter_m(small_grad, 0)
    small_low = small_grad.astype(BF16)
    small_grad = pick(small_grad, z)
    for k in range(1, Z):
        small_grad = small_grad + hop(pick(small_low, z ^ k), k).astype(F32)
    keyvalue_weight_grad = small_grad[:, : 2 * HEAD_DIM]
    gain_one_mine = small_grad[:, 2 * HEAD_DIM]
    gain_two_mine = small_grad[:, 2 * HEAD_DIM + 1]
    return (
        block_output,
        shared_mine[None],
        input_grad,
        gain_one_mine,
        query_weight_grad,
        keyvalue_weight_grad,
        output_weight_grad,
        gain_two_mine,
        gate_weight_grad,
        up_weight_grad,
        down_weight_grad,
    )


def solution(mesh):
    streams, seq = mesh.shape["dp"], mesh.shape["seq"]
    fine = Mesh(mesh.devices.reshape(streams, Z, seq // (4 * Z), 2, 2), tuple("yzmxc"))
    stream = P("y", ("z", "m", "x", "c"), None)
    vector, matrix = P(tuple("yzmxc")), P(tuple("yzmxc"), None)
    return jax.shard_map(
        on_device,
        mesh=fine,
        in_specs=(
            stream,
            vector,
            matrix,
            matrix,
            matrix,
            vector,
            matrix,
            matrix,
            matrix,
            P("y", None),
            P(),
            stream,
            stream,
        ),
        out_specs=(
            stream,
            stream,
            stream,
            vector,
            matrix,
            matrix,
            matrix,
            vector,
            matrix,
            matrix,
            matrix,
        ),
        check_vma=False,
    )
```

```python
import math

import jax
import jax.numpy as jnp
from jax import lax
from jax.experimental import pallas as pl
from jax.experimental.pallas import tpu as pltpu
from jax.sharding import Mesh
from jax.sharding import PartitionSpec as P

HEAD_DIM = 128
EPSILON = 1e-05
NEGATIVE = -1e30
AXES = "yhlmxc"
BF16 = jnp.bfloat16
F32 = jnp.float32


def angles(offset):
    half_dim = HEAD_DIM // 2
    frequency = jnp.exp(
        jnp.arange(half_dim, dtype=F32) * (-2.0 * math.log(10000.0) / HEAD_DIM)
    )
    phases = offset.astype(F32)[:, None] * frequency[None, :]
    return (jnp.cos(phases), jnp.sin(phases))


def rotate(vectors, cosine, sine_part):
    half_dim = vectors.shape[-1] // 2
    first, second = vectors[..., :half_dim], vectors[..., half_dim:]
    return jnp.concatenate(
        [first * cosine - second * sine_part, second * cosine + first * sine_part], -1
    )


def dot(left, right):
    return jnp.dot(left, right, preferred_element_type=F32)


def contract_last(left, right):
    return lax.dot_general(left, right, (((1,), (1,)), ((), ())), preferred_element_type=F32)


def contract_first(left, right):
    return lax.dot_general(left, right, (((0,), (0,)), ((), ())), preferred_element_type=F32)


def norm_back(grad_normed, normed, scale_rows):
    return scale_rows * (
        grad_normed - normed * jnp.mean(grad_normed * normed, axis=-1, keepdims=True)
    )


def swap(value, axis):
    return lax.ppermute(value, axis, [(0, 1), (1, 0)])


def low(value):
    return value.astype(BF16)


def pick(stacked, index, axis=0):
    return lax.dynamic_index_in_dim(stacked, index, axis, keepdims=False)


def pair(own, other, index, axis=0):
    return jnp.where(
        index == 0, jnp.stack([own, other], axis), jnp.stack([other, own], axis)
    )


def gather_m(value, axis):
    if lax.axis_size("m") > 1:
        return lax.all_gather(value, "m", axis=axis)
    return jnp.expand_dims(value, axis)


def scatter_m(value, axis):
    if lax.axis_size("m") > 1:
        return lax.psum_scatter(value, "m", scatter_dimension=axis)
    return lax.squeeze(value, (axis,))


def fold(total, axis):
    half = total.shape[0] // 2
    return total[:half].astype(F32) + swap(low(total[half:]), axis).astype(F32)


def gather_group(value):
    return lax.all_to_all(jnp.broadcast_to(value, (4, *value.shape)), ("l", "x"), 0, 0)


def scatter_group(value):
    return jnp.sum(lax.all_to_all(low(value), ("l", "x"), 0, 0).astype(F32), axis=0)


LOG2E = math.log2(math.e)
SCALE = 1.0 / math.sqrt(HEAD_DIM)
NT = (((1,), (1,)), ((), ()))
NN = (((1,), (0,)), ((), ()))


def mxu(left, right, dims):
    return lax.dot_general(left, right, dims, preferred_element_type=F32)


def turn(vectors, cosine, sine_part):
    half = HEAD_DIM // 2
    first, second = vectors[:half], vectors[half:]
    return jnp.concatenate(
        [first * cosine - second * sine_part, second * cosine + first * sine_part], 0
    )


def fill_bias(bias, key_place, query_place, query_start):
    keys = bias.shape[0]
    block = 256
    for i in range(keys // block):
        at = key_place[i * block : (i + 1) * block, :]
        fits = (at <= query_place[...]) & (at >= query_start[...])
        bias[i * block : (i + 1) * block, :] = jnp.where(fits, 0.0, NEGATIVE)


def attend_kernel(
    query_sum, key, value_t, cosine, sine_part, key_place, query_place, query_start,
    query_rot, attended, attended_low, lse, bias,
):
    fill_bias(bias, key_place, query_place, query_start)
    for head in range(query_sum.shape[0] // HEAD_DIM):
        at = slice(head * HEAD_DIM, (head + 1) * HEAD_DIM)
        query = turn(query_sum[at, :], cosine[...], sine_part[...]).astype(BF16)
        query_rot[at, :] = query
        scores = mxu(key[...], query, NN) * (SCALE * LOG2E) + bias[...]
        top = jnp.max(scores, axis=0, keepdims=True)
        weights = jnp.exp2(scores - top)
        total = jnp.sum(weights, axis=0, keepdims=True)
        result = mxu(value_t[...], weights.astype(BF16), NN) / total
        attended[at, :] = result
        attended_low[at, :] = result.astype(BF16)
        lse[head : head + 1, :] = top + jnp.log2(total)


def attend_back_kernel(
    query_rot, key, key_t, value, grad, attended, lse, cosine, sine_part, key_place,
    query_place, query_start, query_grad, kv_grad, bias,
):
    fill_bias(bias, key_place, query_place, query_start)
    for head in range(query_rot.shape[0] // HEAD_DIM):
        at = slice(head * HEAD_DIM, (head + 1) * HEAD_DIM)
        query = query_rot[at, :]
        grad_head = grad[at, :]
        delta = jnp.sum(grad_head.astype(F32) * attended[at, :], axis=0, keepdims=True)
        scores = mxu(key[...], query, NN) * (SCALE * LOG2E) + bias[...]
        probs = jnp.exp2(scores - lse[head : head + 1, :])
        grad_probs = mxu(value[...], grad_head, NN)
        grad_scores = (probs * (grad_probs - delta)).astype(BF16)
        key_part = mxu(grad_scores, query, NT) * SCALE
        value_part = mxu(probs.astype(BF16), grad_head, NT)
        if head:
            key_part = key_part + kv_grad[:, :HEAD_DIM]
            value_part = value_part + kv_grad[:, HEAD_DIM:]
        kv_grad[:, :HEAD_DIM] = key_part
        kv_grad[:, HEAD_DIM:] = value_part
        grad_query = mxu(key_t[...], grad_scores, NN) * SCALE
        query_grad[at, :] = turn(grad_query, cosine[...], -sine_part[...]).astype(BF16)


def local_call(kernel, outs, scratch, *args):
    flops = 1 << 32
    return pl.pallas_call(
        kernel,
        out_shape=outs,
        in_specs=[pl.BlockSpec(memory_space=pltpu.VMEM)] * len(args),
        out_specs=[pl.BlockSpec(memory_space=pltpu.VMEM)] * len(outs),
        scratch_shapes=scratch,
        compiler_params=pltpu.CompilerParams(vmem_limit_bytes=48 << 20),
        cost_estimate=pl.CostEstimate(flops=flops, bytes_accessed=1 << 24, transcendentals=1 << 22),
    )(*args)


def on_device(
    block_input,
    attention_gain,
    query_weight,
    keyvalue_weight,
    output_weight,
    feedforward_gain,
    gate_weight,
    up_weight,
    down_weight,
    document_lengths,
    piece_order,
    output_grad,
    shared_grad,
):
    y, h, l, m, x, c = (lax.axis_index(a) for a in AXES)
    M = lax.axis_size("m")
    tokens, width = block_input.shape[1:]
    rows = query_weight.shape[0]
    query_width = query_weight.shape[1]
    half_width = query_width // 2
    heads = half_width // HEAD_DIM
    hidden_units = gate_weight.shape[1]
    part = hidden_units // 4
    piece_len = tokens // 2

    def inward(value):
        value = value.reshape(tokens, 2, 2, 2, M, 2, 2, rows)
        value = value.transpose(0, 6, 1, 2, 4, 3, 5, 7)
        value = jnp.where(c == 0, value, value[:, ::-1])
        value = jnp.where(y == 0, value, value[:, :, ::-1])
        value = jnp.where(h == 0, value, value[:, :, :, ::-1])
        return value.reshape(tokens, width)

    def outward(value):
        value = value.reshape(tokens, 2, 2, 2, M, 2, 2, rows)
        value = jnp.where(h == 0, value, value[:, :, :, ::-1])
        value = jnp.where(y == 0, value, value[:, :, ::-1])
        value = jnp.where(c == 0, value, value[:, ::-1])
        return value.transpose(0, 2, 3, 5, 4, 6, 1, 7).reshape(tokens, width)

    finish = jnp.cumsum(document_lengths[0])
    starts = finish - document_lengths[0]

    def places(slots):
        order = piece_order[(slots[:, None] * 2 + jnp.arange(2)[None, :]).reshape(-1)]
        return (
            order[:, None] * piece_len + jnp.arange(piece_len, dtype=jnp.int32)[None, :]
        ).reshape(-1)

    def slot(h_at, l_at, m_at, x_at, c_at):
        return (((h_at * 2 + l_at) * M + m_at) * 2 + x_at) * 2 + c_at

    position = places(jnp.stack([slot(h, l, m, x, c), slot(h, l, m, 1 - x, c)]))
    begins = jnp.max(
        jnp.where(starts[None, :] <= position[:, None], starts[None, :], 0), axis=1
    )
    key_position = places(
        jnp.stack(
            [
                slot(h ^ i, l ^ j, m_at, x ^ k, c ^ n)
                for n in range(2)
                for k in range(2)
                for j in range(2)
                for m_at in range(M)
                for i in range(2)
            ]
        )
    )[:, None]
    query_place, query_start = position[None, :], begins[None, :]
    cosine, sine_part = angles(position - begins)

    gains = jnp.stack([attention_gain, feedforward_gain])
    gains = jnp.pad(gains, ((0, 14), (0, 2 * HEAD_DIM - rows)))
    small = jnp.concatenate([keyvalue_weight, gains])
    small = jnp.stack([small, swap(small, "h")])
    small = pair(small, swap(small, "l"), l, 1)
    small = pair(small, swap(small, "x"), x, 2)
    small = gather_m(small, 1)
    small = jnp.stack([small, swap(small, "y")])
    small = jnp.stack([small, swap(small, "c")])
    small = small.reshape(width // rows, rows + 16, 2 * HEAD_DIM)
    keyvalue_full = small[:, :rows].reshape(width, 2 * HEAD_DIM)
    gain_one = small[:, rows, :rows].reshape(1, width).astype(F32)
    gain_two = small[:, rows + 1, :rows].reshape(1, width).astype(F32)

    def gather_heads(weight):
        parts = weight.reshape(rows, 2, half_width).transpose(1, 0, 2)
        got = pair(pick(parts, x), swap(pick(parts, 1 - x), "x"), x)
        got = jnp.stack([got, swap(got, "h")])
        got = pair(got, swap(got, "l"), l, 1)
        got = gather_m(got, 1).reshape(-1, half_width)
        got = jnp.concatenate([got, swap(got, "y")])
        return jnp.concatenate([got, swap(got, "c")])

    def scatter_heads(grad):
        grad = fold(fold(low(grad), "c"), "y")
        grad = scatter_m(grad.reshape(2, M, 2, 2, rows, half_width), 1)
        grad = pick(grad, l, 1) + swap(low(pick(grad, 1 - l, 1)), "l").astype(F32)
        grad = grad[0] + swap(low(grad[1]), "h").astype(F32)
        other = swap(low(pick(grad, 1 - x)), "x").astype(F32)
        return pair(pick(grad, x), other, x, 1).reshape(rows, query_width)

    query_full = gather_heads(query_weight)
    output_full = gather_heads(output_weight)

    def gather_feed(weight):
        parts = weight.reshape(rows, 4, part).transpose(1, 0, 2)
        got = lax.all_to_all(parts, ("l", "x"), 0, 0)
        got = gather_m(got, 0).reshape(width // 8, part)
        by_h = swap(got, "h")
        near = jnp.concatenate([got, by_h])
        far = jnp.concatenate([swap(got, "y"), swap(by_h, "y")])
        return jnp.concatenate([near, far, swap(near, "c"), swap(far, "c")])

    def scatter_feed(left, right):
        half, quarter = width // 2, width // 4
        sent = swap(low(contract_first(left[:, half:], right)), "c")
        grad = contract_first(left[:, :half], right) + sent.astype(F32)
        near, far = grad[:quarter], low(grad[quarter:])
        block = width // 8
        by_h = near[block:] + swap(far[block:], "y").astype(F32)
        own = near[:block] + swap(far[:block], "y").astype(F32)
        own = own + swap(low(by_h), "h").astype(F32)
        own = low(scatter_m(own.reshape(M, 4, rows, part), 0))
        got = lax.all_to_all(own, ("l", "x"), 0, 0)
        return got.transpose(1, 0, 2).reshape(rows, hidden_units).astype(F32)

    gate_full = gather_feed(gate_weight)
    up_full = gather_feed(up_weight)
    down_full = gather_feed(down_weight)

    input_mine = inward(block_input[0])
    inputs = jnp.concatenate([input_mine, swap(input_mine, "x")]).astype(F32)
    scale_one = lax.rsqrt(jnp.mean(inputs * inputs, axis=-1, keepdims=True) + EPSILON)
    normed_one = inputs * scale_one
    normed_one_low = low(normed_one * gain_one)
    keyvalue_sum = dot(normed_one_low[:tokens], keyvalue_full)
    shared_mine = low(
        jnp.concatenate(
            [
                rotate(keyvalue_sum[:, :HEAD_DIM], cosine[:tokens], sine_part[:tokens]),
                keyvalue_sum[:, HEAD_DIM:],
            ],
            -1,
        )
    )
    gathered = jnp.stack([shared_mine, swap(shared_mine, "h")])
    gathered = gather_m(gathered, 0)
    for axis in "lxc":
        gathered = jnp.stack([gathered, swap(gathered, axis)])
    gathered = gathered.reshape(-1, 2 * HEAD_DIM)
    stream_len = gathered.shape[0]
    key, value = gathered[:, :HEAD_DIM], gathered[:, HEAD_DIM:]
    query_sum = lax.dot_general(
        query_full, normed_one_low, (((0,), (1,)), ((), ())), preferred_element_type=F32
    )
    cosine_t, sine_t = cosine.T, sine_part.T
    wide = (half_width, 2 * tokens)
    places_used = (key_position, query_place, query_start)
    query_rot, attended, attended_low, lse = local_call(
        attend_kernel,
        [
            jax.ShapeDtypeStruct(wide, BF16),
            jax.ShapeDtypeStruct(wide, F32),
            jax.ShapeDtypeStruct(wide, BF16),
            jax.ShapeDtypeStruct((heads, 2 * tokens), F32),
        ],
        [pltpu.VMEM((stream_len, 2 * tokens), F32)],
        query_sum, key, value.T, cosine_t, sine_t, *places_used,
    )
    branch = lax.dot_general(
        attended_low, output_full, (((0,), (1,)), ((), ())), preferred_element_type=F32
    )
    hidden = inputs[:tokens] + fold(branch, "x")

    scale_two = lax.rsqrt(jnp.mean(hidden * hidden, axis=-1, keepdims=True) + EPSILON)
    normed_two = hidden * scale_two
    grad_mine = inward(output_grad[0])
    grad_low = gather_group(grad_mine).reshape(-1, width)
    normed_two_low = gather_group(low(normed_two * gain_two)).reshape(-1, width)
    gate_sum = dot(normed_two_low, gate_full)
    up_sum = dot(normed_two_low, up_full)
    sigmoid_gate = jax.nn.sigmoid(gate_sum)
    silu_gate = gate_sum * sigmoid_gate
    mixed_low = low(silu_gate * up_sum)
    grad_mixed = dot(grad_low, down_full)
    grad_gate = low(
        grad_mixed * up_sum * sigmoid_gate * (1.0 + gate_sum * (1.0 - sigmoid_gate))
    )
    grad_up = low(grad_mixed * silu_gate)
    blocks = (4, tokens, width)
    grad_two = scatter_group(
        (contract_last(grad_gate, gate_full) + contract_last(grad_up, up_full)).reshape(blocks)
    )
    feed_out = scatter_group(contract_last(mixed_low, down_full).reshape(blocks))
    block_output = outward(low(hidden + feed_out))[None]
    gain_two_grad = jnp.sum(grad_two * normed_two, axis=0)
    grad_hidden = grad_mine.astype(F32) + norm_back(grad_two * gain_two, normed_two, scale_two)

    grad_hidden_low = low(grad_hidden)
    grad_hidden_low = jnp.concatenate([grad_hidden_low, swap(grad_hidden_low, "x")])
    grad_heads = low(
        lax.dot_general(
            output_full, grad_hidden_low, (((0,), (1,)), ((), ())), preferred_element_type=F32
        )
    )
    query_grad_low, kv_grad = local_call(
        attend_back_kernel,
        [
            jax.ShapeDtypeStruct(wide, BF16),
            jax.ShapeDtypeStruct((stream_len, 2 * HEAD_DIM), F32),
        ],
        [pltpu.VMEM((stream_len, 2 * tokens), F32)],
        query_rot, key, key.T, value, grad_heads, attended, lse, cosine_t, sine_t, *places_used,
    )
    for axis in "cxl":
        kv_grad = fold(kv_grad, axis)
    kv_grad = scatter_m(kv_grad.reshape(M, 2 * tokens, 2 * HEAD_DIM), 0)
    kv_mine = fold(kv_grad, "h") + shared_grad[0].astype(F32)
    keyvalue_grad_low = low(
        jnp.concatenate(
            [
                rotate(kv_mine[:, :HEAD_DIM], cosine[:tokens], -sine_part[:tokens]),
                kv_mine[:, HEAD_DIM:],
            ],
            -1,
        )
    )
    grad_one = lax.dot_general(
        query_grad_low, query_full, (((0,), (1,)), ((), ())), preferred_element_type=F32
    )
    grad_one = fold(grad_one, "x") + contract_last(keyvalue_grad_low, keyvalue_full)
    normed_mine = normed_one[:tokens]
    gain_one_grad = jnp.sum(grad_one * normed_mine, axis=0)
    input_grad = outward(
        grad_hidden + norm_back(grad_one * gain_one, normed_mine, scale_one[:tokens])
    )[None]

    down_weight_grad = scatter_feed(grad_low, mixed_low)
    gate_weight_grad = scatter_feed(normed_two_low, grad_gate)
    up_weight_grad = scatter_feed(normed_two_low, grad_up)
    across = (((0,), (1,)), ((), ()))
    output_weight_grad = scatter_heads(
        lax.dot_general(grad_hidden_low, attended_low, across, preferred_element_type=F32)
    )
    query_weight_grad = scatter_heads(
        lax.dot_general(normed_one_low, query_grad_low, across, preferred_element_type=F32)
    )

    small_grad = contract_first(normed_one_low[:tokens], keyvalue_grad_low)
    small_gains = jnp.stack([gain_one_grad, gain_two_grad], -1)
    small_gains = jnp.pad(small_gains, ((0, 0), (0, HEAD_DIM - 2)))
    small_grad = jnp.concatenate([small_grad, small_gains], -1)
    small_grad = fold(fold(small_grad, "c"), "y")
    small_grad = fold(small_grad, "h").reshape(M, 2, 2, rows, 3 * HEAD_DIM)
    small_grad = pick(small_grad, l, 1) + swap(low(pick(small_grad, 1 - l, 1)), "l").astype(F32)
    small_grad = pick(small_grad, x, 1) + swap(low(pick(small_grad, 1 - x, 1)), "x").astype(F32)
    small_grad = scatter_m(small_grad, 0)
    keyvalue_weight_grad = small_grad[:, : 2 * HEAD_DIM]
    gain_one_mine = small_grad[:, 2 * HEAD_DIM]
    gain_two_mine = small_grad[:, 2 * HEAD_DIM + 1]
    return (
        block_output,
        shared_mine[None],
        input_grad,
        gain_one_mine,
        query_weight_grad,
        keyvalue_weight_grad,
        output_weight_grad,
        gain_two_mine,
        gate_weight_grad,
        up_weight_grad,
        down_weight_grad,
    )


def solution(mesh):
    streams, seq = mesh.shape["dp"], mesh.shape["seq"]
    fine = Mesh(mesh.devices.reshape(streams, 2, 2, seq // 16, 2, 2), tuple(AXES))
    stream = P("y", tuple(AXES[1:]), None)
    vector, matrix = P(tuple(AXES)), P(tuple(AXES), None)
    return jax.shard_map(
        on_device,
        mesh=fine,
        in_specs=(
            stream,
            vector,
            matrix,
            matrix,
            matrix,
            vector,
            matrix,
            matrix,
            matrix,
            P("y", None),
            P(),
            stream,
            stream,
        ),
        out_specs=(
            stream,
            stream,
            stream,
            vector,
            matrix,
            matrix,
            matrix,
            vector,
            matrix,
            matrix,
            matrix,
        ),
        check_vma=False,
    )
```

```python
import functools
import math

import jax
import jax.numpy as jnp
from jax import lax
from jax.experimental import pallas as pl
from jax.experimental.pallas import tpu as pltpu
from jax.sharding import Mesh
from jax.sharding import PartitionSpec as P

HEAD_DIM = 128
EPSILON = 1e-05
NEGATIVE = -1e30
AXES = "yhlmxc"
BF16 = jnp.bfloat16
F32 = jnp.float32


def angles(offset):
    half_dim = HEAD_DIM // 2
    frequency = jnp.exp(
        jnp.arange(half_dim, dtype=F32) * (-2.0 * math.log(10000.0) / HEAD_DIM)
    )
    phases = offset.astype(F32)[:, None] * frequency[None, :]
    return (jnp.cos(phases), jnp.sin(phases))


def rotate(vectors, cosine, sine_part):
    half_dim = vectors.shape[-1] // 2
    first, second = vectors[..., :half_dim], vectors[..., half_dim:]
    return jnp.concatenate(
        [first * cosine - second * sine_part, second * cosine + first * sine_part], -1
    )


def dot(left, right):
    return jnp.dot(left, right, preferred_element_type=F32)


def contract_last(left, right):
    return lax.dot_general(left, right, (((1,), (1,)), ((), ())), preferred_element_type=F32)


def contract_first(left, right):
    return lax.dot_general(left, right, (((0,), (0,)), ((), ())), preferred_element_type=F32)


def norm_back(grad_normed, normed, scale_rows):
    return scale_rows * (
        grad_normed - normed * jnp.mean(grad_normed * normed, axis=-1, keepdims=True)
    )


def swap(value, axis):
    return lax.ppermute(value, axis, [(0, 1), (1, 0)])


def low(value):
    return value.astype(BF16)


def after(value, *events):
    return lax.optimization_barrier((value, *events))[0]


def pick(stacked, index, axis=0):
    return lax.dynamic_index_in_dim(stacked, index, axis, keepdims=False)


def pair(own, other, index, axis=0):
    return jnp.where(
        index == 0, jnp.stack([own, other], axis), jnp.stack([other, own], axis)
    )


def gather_m(value, axis):
    if lax.axis_size("m") > 1:
        return lax.all_gather(value, "m", axis=axis)
    return jnp.expand_dims(value, axis)


def scatter_m(value, axis):
    if lax.axis_size("m") > 1:
        return lax.psum_scatter(value, "m", scatter_dimension=axis)
    return lax.squeeze(value, (axis,))


def fold(total, axis):
    half = total.shape[0] // 2
    return total[:half].astype(F32) + swap(low(total[half:]), axis).astype(F32)


def gather_group(value):
    return lax.all_to_all(jnp.broadcast_to(value, (4, *value.shape)), ("l", "x"), 0, 0)


def scatter_group(value):
    return jnp.sum(lax.all_to_all(low(value), ("l", "x"), 0, 0).astype(F32), axis=0)


LOG2E = math.log2(math.e)
SCALE = 1.0 / math.sqrt(HEAD_DIM)
NT = (((1,), (1,)), ((), ()))
NN = (((1,), (0,)), ((), ()))


def mxu(left, right, dims):
    return lax.dot_general(left, right, dims, preferred_element_type=F32)


def turn(vectors, cosine, sine_part):
    half = HEAD_DIM // 2
    first, second = vectors[:half], vectors[half:]
    return jnp.concatenate(
        [first * cosine - second * sine_part, second * cosine + first * sine_part], 0
    )


def fill_bias(bias, key_place, query_place, query_start):
    keys = bias.shape[0]
    block = 256
    for i in range(keys // block):
        at = key_place[i * block : (i + 1) * block, :]
        fits = (at <= query_place[...]) & (at >= query_start[...])
        bias[i * block : (i + 1) * block, :] = jnp.where(fits, 0.0, NEGATIVE)


def attend_kernel(
    query_sum, key, value_t, cosine, sine_part, key_place, query_place, query_start,
    query_rot, attended, attended_low, lse, bias,
):
    fill_bias(bias, key_place, query_place, query_start)

    def one(head, unused):
        at = pl.ds(pl.multiple_of(head * HEAD_DIM, HEAD_DIM), HEAD_DIM)
        query = turn(query_sum[at, :], cosine[...], sine_part[...]).astype(BF16)
        query_rot[at, :] = query
        scores = mxu(key[...], query, NN) * (SCALE * LOG2E) + bias[...]
        top = jnp.max(scores, axis=0, keepdims=True)
        weights = jnp.exp2(scores - top)
        total = jnp.sum(weights, axis=0, keepdims=True)
        result = mxu(value_t[...], weights.astype(BF16), NN) / total
        attended[at, :] = result
        attended_low[at, :] = result.astype(BF16)
        lse[pl.ds(head, 1), :] = top + jnp.log2(total)
        return unused

    each_head(one, query_sum, key)


def each_head(one, heads_ref, key):
    count = heads_ref.shape[0] // HEAD_DIM
    if key.shape[0] > 2048:
        lax.fori_loop(0, count, one, 0)
    else:
        for head in range(count):
            one(head, 0)


def attend_back_kernel(
    query_rot, key, key_t, value, grad, attended, lse, cosine, sine_part, key_place,
    query_place, query_start, query_grad, kv_grad, bias,
):
    fill_bias(bias, key_place, query_place, query_start)
    kv_grad[...] = jnp.zeros_like(kv_grad)

    def one(head, unused):
        at = pl.ds(pl.multiple_of(head * HEAD_DIM, HEAD_DIM), HEAD_DIM)
        query = query_rot[at, :]
        grad_head = grad[at, :]
        delta = jnp.sum(grad_head.astype(F32) * attended[at, :], axis=0, keepdims=True)
        scores = mxu(key[...], query, NN) * (SCALE * LOG2E) + bias[...]
        probs = jnp.exp2(scores - lse[pl.ds(head, 1), :])
        grad_probs = mxu(value[...], grad_head, NN)
        grad_scores = (probs * (grad_probs - delta)).astype(BF16)
        kv_grad[:, :HEAD_DIM] += mxu(grad_scores, query, NT) * SCALE
        kv_grad[:, HEAD_DIM:] += mxu(probs.astype(BF16), grad_head, NT)
        grad_query = mxu(key_t[...], grad_scores, NN) * SCALE
        query_grad[at, :] = turn(grad_query, cosine[...], -sine_part[...]).astype(BF16)
        return unused

    each_head(one, query_rot, key)


def columns_of(width):
    return width // 256, width % 256


def each_block(width, body):
    full, rest = columns_of(width)

    def step(i, unused):
        body(pl.ds(pl.multiple_of(i * 256, 256), 256))
        return unused

    lax.fori_loop(0, full, step, 0)
    if rest:
        body(pl.ds(full * 256, rest))


def load_pieces(pieces, slots, held, sems):
    waits = []
    for slot, (arrays, at) in enumerate(slots):
        copies = [
            pltpu.make_async_copy(pieces[a].at[:, at], held.at[slot, p], sems.at[slot, p])
            for p, a in enumerate(arrays)
        ]
        for copy in copies:
            copy.start()
        waits.append(copies)

    def wait(slot):
        for copy in waits[slot]:
            copy.wait()

    return wait


def feed_kernel(normed, grad, *refs):
    pieces = refs[:16]
    mixed, grad_gate, grad_up, grad_two, held, gate_sum, up_sum, sems = refs[16:]
    both, down = range(8), range(8, 16)
    wait = load_pieces(pieces, [(both, 0), (both, 1), (down, 0)], held, sems)
    width, part = normed.shape[1], mixed.shape[1]

    def block(slot, at):
        return held[slot, :, :, :, at].reshape(width, at.size)

    wait(0)

    def gate_step(at):
        gate_sum[:, at] = mxu(normed[...], block(0, at), NN)

    each_block(part, gate_step)
    wait(1)

    def up_step(at):
        up_sum[:, at] = mxu(normed[...], block(1, at), NN)

    each_block(part, up_step)
    wait(2)

    def down_step(at):
        grad_mixed = mxu(grad[...], block(2, at), NN)
        gate, up = gate_sum[:, at], up_sum[:, at]
        sigmoid_gate = jax.nn.sigmoid(gate)
        silu_gate = gate * sigmoid_gate
        mixed[:, at] = (silu_gate * up).astype(BF16)
        grad_up[:, at] = (grad_mixed * silu_gate).astype(BF16)
        grad_gate[:, at] = (
            grad_mixed * up * sigmoid_gate * (1.0 + gate * (1.0 - sigmoid_gate))
        ).astype(BF16)

    each_block(part, down_step)

    def two_step(p, unused):
        at = pl.ds(pl.multiple_of(p * (width // 8), width // 8), width // 8)
        grad_two[:, at] = (
            mxu(grad_gate[...], held[0, p].reshape(width // 8, part), NT)
            + mxu(grad_up[...], held[1, p].reshape(width // 8, part), NT)
        ).astype(BF16)
        return unused

    lax.fori_loop(0, 8, two_step, 0)


TN = (((0,), (0,)), ((), ()))


def outer(first_block, left, right, result):
    rows = left.shape[1] // 8

    def step(p, unused):
        at = pl.ds(pl.multiple_of((first_block + p) * rows, rows), rows)
        to = pl.ds(pl.multiple_of(p * rows, rows), rows)
        result[to, :] = mxu(left[:, at], right[...], TN).astype(result.dtype)
        return unused

    lax.fori_loop(0, 4, step, 0)


def outer_far_kernel(normed, grad, mixed, grad_gate, grad_up, down_far, gate_far, up_far):
    outer(4, grad, mixed, down_far)
    outer(4, normed, grad_gate, gate_far)
    outer(4, normed, grad_up, up_far)


def outer_near_kernel(normed, grad, mixed, grad_gate, grad_up, *refs):
    pieces = refs[:8]
    down_near, gate_near, up_near, feed, held, sems = refs[8:]
    wait = load_pieces(pieces, [(range(8), 0)], held, sems)
    outer(0, grad, mixed, down_near)
    outer(0, normed, grad_gate, gate_near)
    outer(0, normed, grad_up, up_near)
    wait(0)
    width, part = normed.shape[1], mixed.shape[1]

    def feed_step(p, unused):
        at = pl.ds(pl.multiple_of(p * (width // 8), width // 8), width // 8)
        feed[:, at] = mxu(
            mixed[...], held[0, p].reshape(width // 8, part), NT
        ).astype(BF16)
        return unused

    lax.fori_loop(0, 8, feed_step, 0)


def split_kernel(count, *refs):
    matrices, result, sems = refs[:count], refs[count], refs[count + 1]
    part = result.shape[-1]
    copies = [
        pltpu.make_async_copy(
            matrix.at[:, pl.ds(i * part, part)], result.at[i, j], sems.at[i, j]
        )
        for i in range(4)
        for j, matrix in enumerate(matrices)
    ]
    for copy in copies:
        copy.start()
    for copy in copies:
        copy.wait()


def split(*matrices):
    rows, columns = matrices[0].shape
    count = len(matrices)
    anywhere = pl.BlockSpec(memory_space=pl.ANY)
    return pl.pallas_call(
        functools.partial(split_kernel, count),
        out_shape=jax.ShapeDtypeStruct((4, count, rows, columns // 4), matrices[0].dtype),
        in_specs=[anywhere] * count,
        out_specs=anywhere,
        scratch_shapes=[pltpu.SemaphoreType.DMA((4, count))],
        cost_estimate=pl.CostEstimate(flops=0, bytes_accessed=1 << 22, transcendentals=0),
    )(*matrices)


def local_call(kernel, outs, scratch, *args, far=0, micros=10):
    near = [pl.BlockSpec(memory_space=pltpu.VMEM)] * (len(args) - far)
    return pl.pallas_call(
        kernel,
        out_shape=outs,
        in_specs=near + [pl.BlockSpec(memory_space=pl.ANY)] * far,
        out_specs=[pl.BlockSpec(memory_space=pltpu.VMEM)] * len(outs),
        scratch_shapes=scratch,
        compiler_params=pltpu.CompilerParams(vmem_limit_bytes=56 << 20),
        cost_estimate=pl.CostEstimate(
            flops=micros * 900_000_000, bytes_accessed=1 << 20, transcendentals=0
        ),
    )(*args)


def on_device(
    block_input,
    attention_gain,
    query_weight,
    keyvalue_weight,
    output_weight,
    feedforward_gain,
    gate_weight,
    up_weight,
    down_weight,
    document_lengths,
    piece_order,
    output_grad,
    shared_grad,
):
    y, h, l, m, x, c = (lax.axis_index(a) for a in AXES)
    M = lax.axis_size("m")
    tokens, width = block_input.shape[1:]
    rows = query_weight.shape[0]
    query_width = query_weight.shape[1]
    half_width = query_width // 2
    heads = half_width // HEAD_DIM
    hidden_units = gate_weight.shape[1]
    part = hidden_units // 4
    piece_len = tokens // 2

    def inward(value):
        value = value.reshape(tokens, 2, 2, 2, M, 2, 2, rows)
        value = value.transpose(0, 6, 1, 2, 4, 3, 5, 7)
        value = jnp.where(c == 0, value, value[:, ::-1])
        value = jnp.where(y == 0, value, value[:, :, ::-1])
        value = jnp.where(h == 0, value, value[:, :, :, ::-1])
        return value.reshape(tokens, width)

    def outward(value):
        value = value.reshape(tokens, 2, 2, 2, M, 2, 2, rows)
        value = jnp.where(h == 0, value, value[:, :, :, ::-1])
        value = jnp.where(y == 0, value, value[:, :, ::-1])
        value = jnp.where(c == 0, value, value[:, ::-1])
        return value.transpose(0, 2, 3, 5, 4, 6, 1, 7).reshape(tokens, width)

    finish = jnp.cumsum(document_lengths[0])
    starts = finish - document_lengths[0]

    def places(slots):
        order = piece_order[(slots[:, None] * 2 + jnp.arange(2)[None, :]).reshape(-1)]
        return (
            order[:, None] * piece_len + jnp.arange(piece_len, dtype=jnp.int32)[None, :]
        ).reshape(-1)

    def slot(h_at, l_at, m_at, x_at, c_at):
        return (((h_at * 2 + l_at) * M + m_at) * 2 + x_at) * 2 + c_at

    position = places(jnp.stack([slot(h, l, m, x, c), slot(h, l, m, 1 - x, c)]))
    begins = jnp.max(
        jnp.where(starts[None, :] <= position[:, None], starts[None, :], 0), axis=1
    )
    key_position = places(
        jnp.stack(
            [
                slot(h ^ i, l ^ j, m_at, x ^ k, c ^ n)
                for n in range(2)
                for k in range(2)
                for j in range(2)
                for m_at in range(M)
                for i in range(2)
            ]
        )
    )[:, None]
    query_place, query_start = position[None, :], begins[None, :]
    cosine, sine_part = angles(position - begins)

    gains = jnp.stack([attention_gain, feedforward_gain])
    gains = jnp.pad(gains, ((0, 14), (0, 2 * HEAD_DIM - rows)))
    small = jnp.concatenate([keyvalue_weight, gains])
    small_steps = [swap(small, "h")]
    small = jnp.stack([small, small_steps[-1]])
    small_steps.append(swap(small, "l"))
    small = pair(small, small_steps[-1], l, 1)
    small_steps.append(swap(small, "x"))
    small = pair(small, small_steps[-1], x, 2)
    small = gather_m(small, 1)
    small_steps.append(swap(small, "y"))
    small = jnp.stack([small, small_steps[-1]])
    small_steps.append(swap(small, "c"))
    small = jnp.stack([small, small_steps[-1]])
    small = small.reshape(width // rows, rows + 16, 2 * HEAD_DIM)
    keyvalue_full = small[:, :rows].reshape(width, 2 * HEAD_DIM)
    gain_one = small[:, rows, :rows].reshape(1, width).astype(F32)
    gain_two = small[:, rows + 1, :rows].reshape(1, width).astype(F32)

    def halves(weight):
        parts = weight.reshape(rows, 2, half_width).transpose(1, 0, 2)
        return pick(parts, x), pick(parts, 1 - x)

    def gather_heads(weight, ahead=None):
        ahead = ahead or [()] * 5
        mine, sent = halves(weight)
        steps = [swap(after(sent, *ahead[0]), "x")]
        got = pair(mine, steps[-1], x)
        steps.append(swap(after(got, *ahead[1]), "h"))
        got = jnp.stack([got, steps[-1]])
        steps.append(swap(after(got, *ahead[2]), "l"))
        got = pair(got, steps[-1], l, 1)
        got = gather_m(got, 1).reshape(-1, half_width)
        steps.append(swap(after(got, *ahead[3]), "y"))
        got = jnp.concatenate([got, steps[-1]])
        steps.append(swap(after(got, *ahead[4]), "c"))
        return jnp.concatenate([got, steps[-1]]), [(step,) for step in steps]

    def scatter_heads(grad):
        grad = fold(fold(low(grad), "c"), "y")
        grad = scatter_m(grad.reshape(2, M, 2, 2, rows, half_width), 1)
        grad = pick(grad, l, 1) + swap(low(pick(grad, 1 - l, 1)), "l").astype(F32)
        grad = grad[0] + swap(low(grad[1]), "h").astype(F32)
        other = swap(low(pick(grad, 1 - x)), "x").astype(F32)
        return pair(pick(grad, x), other, x, 1).reshape(rows, query_width)

    query_full, query_steps = gather_heads(query_weight)
    output_full, output_steps = gather_heads(output_weight, query_steps)

    def exchange(parts):
        got = lax.all_to_all(parts, ("l", "x"), 0, 0)
        got = gather_m(got, 0)
        return got.reshape(M * 4, -1, rows, part)

    both = exchange(after(split(gate_weight, up_weight), small_steps[0]))
    both = after(both, small_steps[3])
    both_h = swap(both, "h")
    both_y = swap(both, "y")
    down = exchange(after(split(down_weight), both, small_steps[4]))

    input_mine = inward(block_input[0])
    inputs = jnp.concatenate([input_mine, swap(input_mine, "x")]).astype(F32)
    scale_one = lax.rsqrt(jnp.mean(inputs * inputs, axis=-1, keepdims=True) + EPSILON)
    normed_one = inputs * scale_one
    normed_one_low = low(normed_one * gain_one)
    keyvalue_sum = dot(normed_one_low[:tokens], keyvalue_full)
    shared_mine = low(
        jnp.concatenate(
            [
                rotate(keyvalue_sum[:, :HEAD_DIM], cosine[:tokens], sine_part[:tokens]),
                keyvalue_sum[:, HEAD_DIM:],
            ],
            -1,
        )
    )
    gathered = jnp.stack([shared_mine, swap(shared_mine, "h")])
    gathered = gather_m(gathered, 0)
    for axis in "lxc":
        gathered = jnp.stack([gathered, swap(gathered, axis)])
    gathered = gathered.reshape(-1, 2 * HEAD_DIM)
    stream_len = gathered.shape[0]
    key, value = gathered[:, :HEAD_DIM], gathered[:, HEAD_DIM:]
    query_sum = lax.dot_general(
        query_full, normed_one_low, (((0,), (1,)), ((), ())), preferred_element_type=F32
    )
    cosine_t, sine_t = cosine.T, sine_part.T
    wide = (half_width, 2 * tokens)
    places_used = (key_position, query_place, query_start)
    query_rot, attended, attended_low, lse = local_call(
        attend_kernel,
        [
            jax.ShapeDtypeStruct(wide, BF16),
            jax.ShapeDtypeStruct(wide, F32),
            jax.ShapeDtypeStruct(wide, BF16),
            jax.ShapeDtypeStruct((heads, 2 * tokens), F32),
        ],
        [pltpu.VMEM((stream_len, 2 * tokens), F32)],
        query_sum, key, value.T, cosine_t, sine_t, *places_used,
    )
    branch = lax.dot_general(
        attended_low, output_full, (((0,), (1,)), ((), ())), preferred_element_type=F32
    )
    branch_sent = low(branch[tokens:])
    hidden = inputs[:tokens] + (branch[:tokens] + swap(branch_sent, "x").astype(F32))

    grad_mine = inward(output_grad[0])
    down = after(down, query_sum)
    down_y = swap(after(down, both_y), "y")
    both_h = after(both_h, branch_sent)
    down_h = swap(after(down, both_h), "h")
    both_far = swap(both_h, "y")
    down_far = swap(after(down_h, both_far), "y")
    both_all = [both, both_h, both_y, both_far]
    down_all = [down, down_h, down_y, down_far]
    both_all = both_all + [swap(piece, "c") for piece in both_all]
    down_all = down_all + [swap(piece, "c") for piece in down_all]
    grad_low = gather_group(after(grad_mine, down, query_sum)).reshape(-1, width)

    scale_two = lax.rsqrt(jnp.mean(hidden * hidden, axis=-1, keepdims=True) + EPSILON)
    normed_two = hidden * scale_two
    normed_two_low = gather_group(low(normed_two * gain_two)).reshape(-1, width)
    group = 4 * tokens
    units = jax.ShapeDtypeStruct((group, part), BF16)
    features = jax.ShapeDtypeStruct((group, width), BF16)
    held = pltpu.VMEM((3, 8, M * 4, rows, part), BF16)
    wide_sum = pltpu.VMEM((group, part), F32)
    mixed_low, grad_gate, grad_up, grad_two = local_call(
        feed_kernel,
        [units, units, units, features],
        [held, wide_sum, wide_sum, pltpu.SemaphoreType.DMA((3, 8))],
        normed_two_low, grad_low, *both_all, *down_all,
        far=16, micros=22,
    )
    grad_two = scatter_group(grad_two.reshape(4, tokens, width))
    outers = (normed_two_low, grad_low, mixed_low, grad_gate, grad_up)
    half_rows = jax.ShapeDtypeStruct((width // 2, part), BF16)
    far_parts = local_call(outer_far_kernel, [half_rows] * 3, [], *outers, micros=8)
    *near_parts, feed_out = local_call(
        outer_near_kernel,
        [half_rows] * 3 + [features],
        [pltpu.VMEM((1, 8, M * 4, rows, part), BF16), pltpu.SemaphoreType.DMA((1, 8))],
        *(after(o, *far_parts) for o in outers), *down_all,
        far=8, micros=12,
    )
    feed_out = scatter_group(after(feed_out, grad_two).reshape(4, tokens, width))
    block_output = outward(low(hidden + feed_out))[None]
    gain_two_grad = jnp.sum(grad_two * normed_two, axis=0)
    grad_hidden = grad_mine.astype(F32) + norm_back(grad_two * gain_two, normed_two, scale_two)

    grad_hidden_low = low(grad_hidden)
    grad_hidden_low = jnp.concatenate([grad_hidden_low, swap(grad_hidden_low, "x")])
    grad_heads = low(
        lax.dot_general(
            output_full, grad_hidden_low, (((0,), (1,)), ((), ())), preferred_element_type=F32
        )
    )
    query_grad_low, kv_grad = local_call(
        attend_back_kernel,
        [
            jax.ShapeDtypeStruct(wide, BF16),
            jax.ShapeDtypeStruct((stream_len, 2 * HEAD_DIM), F32),
        ],
        [pltpu.VMEM((stream_len, 2 * tokens), F32)],
        query_rot, key, key.T, value, grad_heads, attended, lse, cosine_t, sine_t, *places_used,
    )
    kv_grad = kv_first = fold(kv_grad, "c")
    for axis in "xl":
        kv_grad = fold(kv_grad, axis)
    kv_grad = scatter_m(kv_grad.reshape(M, 2 * tokens, 2 * HEAD_DIM), 0)
    kv_mine = fold(kv_grad, "h") + shared_grad[0].astype(F32)
    keyvalue_grad_low = low(
        jnp.concatenate(
            [
                rotate(kv_mine[:, :HEAD_DIM], cosine[:tokens], -sine_part[:tokens]),
                kv_mine[:, HEAD_DIM:],
            ],
            -1,
        )
    )
    grad_one = lax.dot_general(
        query_grad_low, query_full, (((0,), (1,)), ((), ())), preferred_element_type=F32
    )
    grad_one = fold(grad_one, "x") + contract_last(keyvalue_grad_low, keyvalue_full)
    normed_mine = normed_one[:tokens]
    gain_one_grad = jnp.sum(grad_one * normed_mine, axis=0)
    input_grad = outward(
        grad_hidden + norm_back(grad_one * gain_one, normed_mine, scale_one[:tokens])
    )[None]

    block = width // 8

    def fold_y(near, far):
        got = swap(far, "c")

        def total(i):
            at = slice(i * block, (i + 1) * block)
            return near[at].astype(F32) + got[at].astype(F32)

        return total, swap(low(total(3)), "y")

    def finish_feed(total, by_y, event):
        by_h = swap(low(total(1) + after(by_y, *event).astype(F32)), "h")
        own = total(0) + swap(low(total(2)), "y").astype(F32)
        own = own + by_h.astype(F32)
        own = low(scatter_m(own.reshape(M, 4, rows, part), 0))
        got = lax.all_to_all(own, ("l", "x"), 0, 0)
        return got.transpose(1, 0, 2).reshape(rows, hidden_units).astype(F32)

    totals = [fold_y(n, f) for n, f in zip(near_parts, far_parts)]
    events = [(grad_two,), (grad_heads,), (kv_first,)]
    down_weight_grad, gate_weight_grad, up_weight_grad = (
        finish_feed(*total, event) for total, event in zip(totals, events)
    )
    across = (((0,), (1,)), ((), ()))
    output_weight_grad = scatter_heads(
        lax.dot_general(grad_hidden_low, attended_low, across, preferred_element_type=F32)
    )
    query_weight_grad = scatter_heads(
        lax.dot_general(normed_one_low, query_grad_low, across, preferred_element_type=F32)
    )

    small_grad = contract_first(normed_one_low[:tokens], keyvalue_grad_low)
    small_gains = jnp.stack([gain_one_grad, gain_two_grad], -1)
    small_gains = jnp.pad(small_gains, ((0, 0), (0, HEAD_DIM - 2)))
    small_grad = jnp.concatenate([small_grad, small_gains], -1)
    small_grad = fold(fold(small_grad, "c"), "y")
    small_grad = fold(small_grad, "h").reshape(M, 2, 2, rows, 3 * HEAD_DIM)
    small_grad = pick(small_grad, l, 1) + swap(low(pick(small_grad, 1 - l, 1)), "l").astype(F32)
    small_grad = pick(small_grad, x, 1) + swap(low(pick(small_grad, 1 - x, 1)), "x").astype(F32)
    small_grad = scatter_m(small_grad, 0)
    keyvalue_weight_grad = small_grad[:, : 2 * HEAD_DIM]
    gain_one_mine = small_grad[:, 2 * HEAD_DIM]
    gain_two_mine = small_grad[:, 2 * HEAD_DIM + 1]
    return (
        block_output,
        shared_mine[None],
        input_grad,
        gain_one_mine,
        query_weight_grad,
        keyvalue_weight_grad,
        output_weight_grad,
        gain_two_mine,
        gate_weight_grad,
        up_weight_grad,
        down_weight_grad,
    )


def solution(mesh):
    streams, seq = mesh.shape["dp"], mesh.shape["seq"]
    fine = Mesh(mesh.devices.reshape(streams, 2, 2, seq // 16, 2, 2), tuple(AXES))
    stream = P("y", tuple(AXES[1:]), None)
    vector, matrix = P(tuple(AXES)), P(tuple(AXES), None)
    return jax.shard_map(
        on_device,
        mesh=fine,
        in_specs=(
            stream,
            vector,
            matrix,
            matrix,
            matrix,
            vector,
            matrix,
            matrix,
            matrix,
            P("y", None),
            P(),
            stream,
            stream,
        ),
        out_specs=(
            stream,
            stream,
            stream,
            vector,
            matrix,
            matrix,
            matrix,
            vector,
            matrix,
            matrix,
            matrix,
        ),
        check_vma=False,
    )
```

```python
import functools
import math

import jax
import jax.numpy as jnp
from jax import lax
from jax.experimental import pallas as pl
from jax.experimental.pallas import tpu as pltpu
from jax.sharding import Mesh
from jax.sharding import PartitionSpec as P

HEAD_DIM = 128
EPSILON = 1e-05
NEGATIVE = -1e30
AXES = "yhlmxc"
BF16 = jnp.bfloat16
F32 = jnp.float32


def angles(offset):
    half_dim = HEAD_DIM // 2
    frequency = jnp.exp(
        jnp.arange(half_dim, dtype=F32) * (-2.0 * math.log(10000.0) / HEAD_DIM)
    )
    phases = offset.astype(F32)[:, None] * frequency[None, :]
    return (jnp.cos(phases), jnp.sin(phases))


def rotate(vectors, cosine, sine_part):
    half_dim = vectors.shape[-1] // 2
    first, second = vectors[..., :half_dim], vectors[..., half_dim:]
    return jnp.concatenate(
        [first * cosine - second * sine_part, second * cosine + first * sine_part], -1
    )


def dot(left, right):
    return jnp.dot(left, right, preferred_element_type=F32)


def contract_last(left, right):
    return lax.dot_general(left, right, (((1,), (1,)), ((), ())), preferred_element_type=F32)


def contract_first(left, right):
    return lax.dot_general(left, right, (((0,), (0,)), ((), ())), preferred_element_type=F32)


def norm_back(grad_normed, normed, scale_rows):
    return scale_rows * (
        grad_normed - normed * jnp.mean(grad_normed * normed, axis=-1, keepdims=True)
    )


def swap(value, axis):
    return lax.ppermute(value, axis, [(0, 1), (1, 0)])


def swap_core(value):
    size = value.shape[0] // 4
    parts = [value[i * size : (i + 1) * size] for i in range(4)]
    return jnp.concatenate([swap(part, "c") for part in parts])


def low(value):
    return value.astype(BF16)


def sync(*values):
    return lax.optimization_barrier(values)


def pick(stacked, index, axis=0):
    return lax.dynamic_index_in_dim(stacked, index, axis, keepdims=False)


def pair(own, other, index, axis=0):
    return jnp.where(
        index == 0, jnp.stack([own, other], axis), jnp.stack([other, own], axis)
    )


def gather_m(value, axis):
    if lax.axis_size("m") > 1:
        return lax.all_gather(value, "m", axis=axis)
    return jnp.expand_dims(value, axis)


def scatter_m(value, axis):
    if lax.axis_size("m") > 1:
        return lax.psum_scatter(value, "m", scatter_dimension=axis)
    return lax.squeeze(value, (axis,))


def fold(total, axis):
    half = total.shape[0] // 2
    return total[:half].astype(F32) + swap(low(total[half:]), axis).astype(F32)


def gather_group(value):
    return lax.all_to_all(jnp.broadcast_to(value, (4, *value.shape)), ("l", "x"), 0, 0)


def scatter_group(value):
    return jnp.sum(lax.all_to_all(low(value), ("l", "x"), 0, 0).astype(F32), axis=0)


LOG2E = math.log2(math.e)
SCALE = 1.0 / math.sqrt(HEAD_DIM)
NT = (((1,), (1,)), ((), ()))
NN = (((1,), (0,)), ((), ()))


def mxu(left, right, dims):
    return lax.dot_general(left, right, dims, preferred_element_type=F32)


def turn(vectors, cosine, sine_part):
    half = HEAD_DIM // 2
    first, second = vectors[:half], vectors[half:]
    return jnp.concatenate(
        [first * cosine - second * sine_part, second * cosine + first * sine_part], 0
    )


def fill_bias(bias, key_place, query_place, query_start):
    keys = bias.shape[0]
    block = 256
    for i in range(keys // block):
        at = key_place[i * block : (i + 1) * block, :]
        fits = (at <= query_place[...]) & (at >= query_start[...])
        bias[i * block : (i + 1) * block, :] = jnp.where(fits, 0.0, NEGATIVE)


def attend_kernel(
    query_sum, key, value_t, cosine, sine_part, key_place, query_place, query_start,
    query_rot, attended, attended_low, lse, bias,
):
    fill_bias(bias, key_place, query_place, query_start)

    def one(head, unused):
        at = pl.ds(pl.multiple_of(head * HEAD_DIM, HEAD_DIM), HEAD_DIM)
        query = turn(query_sum[at, :], cosine[...], sine_part[...]).astype(BF16)
        query_rot[at, :] = query
        scores = mxu(key[...], query, NN) * (SCALE * LOG2E) + bias[...]
        top = jnp.max(scores, axis=0, keepdims=True)
        weights = jnp.exp2(scores - top)
        total = jnp.sum(weights, axis=0, keepdims=True)
        result = mxu(value_t[...], weights.astype(BF16), NN) / total
        attended[at, :] = result
        attended_low[at, :] = result.astype(BF16)
        lse[pl.ds(head, 1), :] = top + jnp.log2(total)
        return unused

    each_head(one, query_sum, key)


def each_head(one, heads_ref, key):
    count = heads_ref.shape[0] // HEAD_DIM
    if key.shape[0] > 2048:
        lax.fori_loop(0, count, one, 0)
    else:
        for head in range(count):
            one(head, 0)


def attend_back_kernel(
    query_rot, key, key_t, value, grad, attended, lse, cosine, sine_part, key_place,
    query_place, query_start, query_grad, kv_grad, bias,
):
    fill_bias(bias, key_place, query_place, query_start)
    kv_grad[...] = jnp.zeros_like(kv_grad)

    def one(head, unused):
        at = pl.ds(pl.multiple_of(head * HEAD_DIM, HEAD_DIM), HEAD_DIM)
        query = query_rot[at, :]
        grad_head = grad[at, :]
        delta = jnp.sum(grad_head.astype(F32) * attended[at, :], axis=0, keepdims=True)
        scores = mxu(key[...], query, NN) * (SCALE * LOG2E) + bias[...]
        probs = jnp.exp2(scores - lse[pl.ds(head, 1), :])
        grad_probs = mxu(value[...], grad_head, NN)
        grad_scores = (probs * (grad_probs - delta)).astype(BF16)
        kv_grad[:, :HEAD_DIM] += mxu(grad_scores, query, NT) * SCALE
        kv_grad[:, HEAD_DIM:] += mxu(probs.astype(BF16), grad_head, NT)
        grad_query = mxu(key_t[...], grad_scores, NN) * SCALE
        query_grad[at, :] = turn(grad_query, cosine[...], -sine_part[...]).astype(BF16)
        return unused

    each_head(one, query_rot, key)


def columns_of(width):
    return width // 256, width % 256


def each_block(width, body):
    full, rest = columns_of(width)

    def step(i, unused):
        body(pl.ds(pl.multiple_of(i * 256, 256), 256))
        return unused

    lax.fori_loop(0, full, step, 0)
    if rest:
        body(pl.ds(full * 256, rest))


def load_pieces(pieces, parts, held, sems):
    waits = []
    half = held.shape[2] // 2
    for slot, matrix in enumerate(parts):
        copies = []
        for core in range(2):
            for i, (p, first, count) in enumerate(
                ((0, 0, 2), (1, 0, 1), (1, 1, 1), (2, 0, 1), (2, 1, 1), (3, 0, 1), (3, 1, 1))
            ):
                copies.append(
                    pltpu.make_async_copy(
                        pieces[core * 7 + i].at[:, matrix],
                        held.at[slot, core * 4 + p, pl.ds(first * half, count * half)],
                        sems.at[slot, core * 7 + i],
                    )
                )
        for copy in copies:
            copy.start()
        waits.append(copies)

    def wait(slot):
        for copy in waits[slot]:
            copy.wait()

    return wait


def feed_kernel(normed, grad, *refs):
    pieces = refs[:14]
    mixed, grad_gate, grad_up, grad_two, held, gate_sum, up_sum, sems = refs[14:]
    wait = load_pieces(pieces, range(3), held, sems)
    width, part = normed.shape[1], mixed.shape[1]

    def block(slot, at):
        return held[slot, :, :, :, at].reshape(width, at.size)

    for slot, result in enumerate((gate_sum, up_sum)):
        wait(slot)

        def step(at):
            result[:, at] = mxu(normed[...], block(slot, at), NN)

        each_block(part, step)
    wait(2)

    def down_step(at):
        grad_mixed = mxu(grad[...], block(2, at), NN)
        gate, up = gate_sum[:, at], up_sum[:, at]
        sigmoid_gate = jax.nn.sigmoid(gate)
        silu_gate = gate * sigmoid_gate
        mixed[:, at] = (silu_gate * up).astype(BF16)
        grad_up[:, at] = (grad_mixed * silu_gate).astype(BF16)
        grad_gate[:, at] = (
            grad_mixed * up * sigmoid_gate * (1.0 + gate * (1.0 - sigmoid_gate))
        ).astype(BF16)

    each_block(part, down_step)

    def two_step(p, unused):
        at = pl.ds(pl.multiple_of(p * (width // 8), width // 8), width // 8)
        grad_two[:, at] = (
            mxu(grad_gate[...], held[0, p].reshape(width // 8, part), NT)
            + mxu(grad_up[...], held[1, p].reshape(width // 8, part), NT)
        ).astype(BF16)
        return unused

    lax.fori_loop(0, 8, two_step, 0)


def outer_kernel(left, *refs):
    count = len(refs) // 3
    rights, results = refs[:count], refs[count:]
    rows = left.shape[1] // 8

    def step(p, unused):
        to = pl.ds(pl.multiple_of(p * rows, rows), rows)
        for part in range(2):
            first = 4 * (1 - part)
            at = pl.ds(pl.multiple_of((first + p) * rows, rows), rows)
            turned = left[:, at].T
            for i, right in enumerate(rights):
                result = results[2 * i + part]
                result[to, :] = mxu(turned, right[...], NN).astype(result.dtype)
        return unused

    lax.fori_loop(0, 4, step, 0)


def outer_all_kernel(order, left, *refs):
    *rights, result = refs
    rows = left.shape[1] // 8

    def step(p, unused):
        at = pl.ds(pl.multiple_of(p * rows, rows), rows)
        turned = left[:, at].T
        for i, right in enumerate(rights):
            result[order[p], i] = mxu(turned, right[...], NN).astype(result.dtype)
        return unused

    lax.fori_loop(0, 8, step, 0)


def feed_out_kernel(mixed, *refs):
    pieces = refs[:14]
    feed, held, sems = refs[14:]
    wait = load_pieces(pieces, [2], held, sems)
    wait(0)
    width, part = feed.shape[1], mixed.shape[1]

    def feed_step(p, unused):
        at = pl.ds(pl.multiple_of(p * (width // 8), width // 8), width // 8)
        feed[:, at] = mxu(
            mixed[...], held[0, p].reshape(width // 8, part), NT
        ).astype(BF16)
        return unused

    lax.fori_loop(0, 8, feed_step, 0)


def split_kernel(*refs):
    result = refs[-1]
    for i, matrix in enumerate(refs[:-1]):
        result[0, i] = matrix[...]


def split(*matrices):
    rows, columns = matrices[0].shape
    count, part = len(matrices), columns // 4
    return pl.pallas_call(
        split_kernel,
        out_shape=jax.ShapeDtypeStruct((4, count, rows, part), matrices[0].dtype),
        grid=(4,),
        in_specs=[pl.BlockSpec((rows, part), lambda i: (0, i))] * count,
        out_specs=pl.BlockSpec((1, count, rows, part), lambda i: (i, 0, 0, 0)),
        cost_estimate=NO_COST,
    )(*matrices)


def merge_kernel(parts, result):
    result[...] = parts[0].astype(F32)


def merge(parts):
    _, rows, part = parts.shape
    return pl.pallas_call(
        merge_kernel,
        out_shape=jax.ShapeDtypeStruct((rows, 4 * part), F32),
        grid=(4,),
        in_specs=[pl.BlockSpec((1, rows, part), lambda i: (i, 0, 0))],
        out_specs=pl.BlockSpec((rows, part), lambda i: (0, i)),
        cost_estimate=NO_COST,
    )(parts)


NO_COST = pl.CostEstimate(flops=1, bytes_accessed=1, transcendentals=0)


def local_call(kernel, outs, scratch, *args, far=0, scalars=0):
    near = [pl.BlockSpec(memory_space=pltpu.SMEM)] * scalars
    near = near + [pl.BlockSpec(memory_space=pltpu.VMEM)] * (len(args) - far - scalars)
    return pl.pallas_call(
        kernel,
        out_shape=outs,
        in_specs=near + [pl.BlockSpec(memory_space=pl.ANY)] * far,
        out_specs=[pl.BlockSpec(memory_space=pltpu.VMEM)] * len(outs),
        scratch_shapes=scratch,
        compiler_params=pltpu.CompilerParams(vmem_limit_bytes=56 << 20),
        cost_estimate=NO_COST,
    )(*args)


def on_device(
    block_input,
    attention_gain,
    query_weight,
    keyvalue_weight,
    output_weight,
    feedforward_gain,
    gate_weight,
    up_weight,
    down_weight,
    document_lengths,
    piece_order,
    output_grad,
    shared_grad,
):
    y, h, l, m, x, c = (lax.axis_index(a) for a in AXES)
    M = lax.axis_size("m")
    tokens, width = block_input.shape[1:]
    rows = query_weight.shape[0]
    query_width = query_weight.shape[1]
    half_width = query_width // 2
    heads = half_width // HEAD_DIM
    hidden_units = gate_weight.shape[1]
    part = hidden_units // 4
    piece_len = tokens // 2

    def inward(value):
        value = value.reshape(tokens, 2, 2, 2, M, 2, 2, rows)
        value = value.transpose(0, 6, 1, 2, 4, 3, 5, 7)
        value = jnp.where(c == 0, value, value[:, ::-1])
        value = jnp.where(y == 0, value, value[:, :, ::-1])
        value = jnp.where(h == 0, value, value[:, :, :, ::-1])
        return value.reshape(tokens, width)

    def outward(value):
        value = value.reshape(tokens, 2, 2, 2, M, 2, 2, rows)
        value = jnp.where(h == 0, value, value[:, :, :, ::-1])
        value = jnp.where(y == 0, value, value[:, :, ::-1])
        value = jnp.where(c == 0, value, value[:, ::-1])
        return value.transpose(0, 2, 3, 5, 4, 6, 1, 7).reshape(tokens, width)

    finish = jnp.cumsum(document_lengths[0])
    starts = finish - document_lengths[0]

    def places(slots):
        order = piece_order[(slots[:, None] * 2 + jnp.arange(2)[None, :]).reshape(-1)]
        return (
            order[:, None] * piece_len + jnp.arange(piece_len, dtype=jnp.int32)[None, :]
        ).reshape(-1)

    def slot(h_at, l_at, m_at, x_at, c_at):
        return (((h_at * 2 + l_at) * M + m_at) * 2 + x_at) * 2 + c_at

    position = places(jnp.stack([slot(h, l, m, x, c), slot(h, l, m, 1 - x, c)]))
    begins = jnp.max(
        jnp.where(starts[None, :] <= position[:, None], starts[None, :], 0), axis=1
    )
    key_position = places(
        jnp.stack(
            [
                slot(h ^ i, l ^ j, m_at, x ^ k, c ^ n)
                for n in range(2)
                for k in range(2)
                for j in range(2)
                for m_at in range(M)
                for i in range(2)
            ]
        )
    )[:, None]
    query_place, query_start = position[None, :], begins[None, :]
    cosine, sine_part = angles(position - begins)

    gains = jnp.stack([attention_gain, feedforward_gain])
    gains = jnp.pad(gains, ((0, 14), (0, 2 * HEAD_DIM - rows)))
    small = jnp.concatenate([keyvalue_weight, gains])

    def halves(weight):
        parts = weight.reshape(rows, 2, half_width).transpose(1, 0, 2)
        return pick(parts, x), pick(parts, 1 - x)

    query_mine, query_sent = halves(query_weight)
    output_mine, output_sent = halves(output_weight)

    small_x, query_x, output_x = sync(
        swap(small, "x"), swap(query_sent, "x"), swap(output_sent, "x")
    )
    small = pair(small, small_x, x)
    query_part, output_part = pair(query_mine, query_x, x), pair(output_mine, output_x, x)
    input_mine, small, gate_weight, up_weight, down_weight = sync(
        inward(block_input[0]), small, gate_weight, up_weight, down_weight
    )
    feed_parts = split(gate_weight, up_weight, down_weight)
    small_l, query_l, output_l, input_other = sync(
        swap(small, "l"), swap(query_part, "l"), swap(output_part, "l"), swap(input_mine, "x")
    )
    small = gather_m(pair(small, small_l, l), 0)
    query_part = gather_m(pair(query_part, query_l, l), 0)
    output_part = gather_m(pair(output_part, output_l, l), 0)
    small, query_part, feed_parts = sync(small, query_part, feed_parts)
    feed = gather_m(lax.all_to_all(feed_parts, ("l", "x"), 0, 0), 0)
    feed = feed.reshape(M * 4, 3, rows, part)
    query_h = swap(query_part, "h")
    small_h = sync(swap(small, "h"))[0]
    small = jnp.stack([small, small_h])
    small_y = sync(swap(small, "y"))[0]
    small = jnp.stack([small, small_y])
    small_c = sync(swap(small, "c"), input_other)[0]
    small = jnp.stack([small, small_c])
    small = small.reshape(width // rows, rows + 16, 2 * HEAD_DIM)
    keyvalue_full = small[:, :rows].reshape(width, 2 * HEAD_DIM)
    gain_one = small[:, rows, :rows].reshape(1, width).astype(F32)
    gain_two = small[:, rows + 1, :rows].reshape(1, width).astype(F32)
    def normalize(value):
        value = value.astype(F32)
        scale = lax.rsqrt(jnp.mean(value * value, axis=-1, keepdims=True) + EPSILON)
        normed = value * scale
        return value, scale, normed, low(normed * gain_one)

    inputs, scale_one, normed_one, normed_mine_low = normalize(input_mine)
    keyvalue_sum = dot(normed_mine_low, keyvalue_full)
    shared_mine = low(
        jnp.concatenate(
            [
                rotate(keyvalue_sum[:, :HEAD_DIM], cosine[:tokens], sine_part[:tokens]),
                keyvalue_sum[:, HEAD_DIM:],
            ],
            -1,
        )
    )
    shared_h, feed, input_other, query_h = sync(
        swap(shared_mine, "h"), feed, input_other, query_h
    )
    gathered = gather_m(jnp.stack([shared_mine, shared_h]), 0)
    gathered, input_other, output_part = sync(gathered, input_other, output_part)
    query_y = swap(jnp.stack([query_part, query_h]), "y")
    output_h = swap(output_part, "h")
    normed_one_low = jnp.concatenate([normed_mine_low, normalize(input_other)[3]])
    shared_l, normed_one_low = sync(swap(gathered, "l"), normed_one_low)
    gathered = jnp.stack([gathered, shared_l])
    shared_x, output_h, query_y = sync(swap(gathered, "x"), output_h, query_y)
    gathered = jnp.stack([gathered, shared_x])
    query_part = jnp.stack([query_part, query_h])
    query_part = jnp.stack([query_part, query_y]).reshape(-1, half_width)
    query_part, gathered = sync(query_part, gathered)
    query_c = swap_core(query_part)
    output_part = jnp.stack([output_part, output_h])
    output_part, gathered, feed = sync(output_part, gathered, feed)
    output_y = swap(output_part, "y")
    quarters = [feed[i * M : (i + 1) * M] for i in range(4)]
    middle = 2 * M
    feed_h = [swap(quarters[0], "h")]
    shared_c, query_c = sync(swap(gathered, "c"), query_c)
    query_full = jnp.concatenate([query_part, query_c])
    gathered = jnp.stack([gathered, shared_c]).reshape(-1, 2 * HEAD_DIM)
    stream_len = gathered.shape[0]
    grad_mine, gathered = sync(inward(output_grad[0]), gathered)
    grad_low = gather_group(grad_mine).reshape(-1, width)
    key, value = gathered[:, :HEAD_DIM], gathered[:, HEAD_DIM:]
    query_sum = lax.dot_general(
        query_full, normed_one_low, (((0,), (1,)), ((), ())), preferred_element_type=F32
    )
    cosine_t, sine_t = cosine.T, sine_part.T
    wide = (half_width, 2 * tokens)
    places_used = (key_position, query_place, query_start)
    query_rot, attended, attended_low, lse = local_call(
        attend_kernel,
        [
            jax.ShapeDtypeStruct(wide, BF16),
            jax.ShapeDtypeStruct(wide, F32),
            jax.ShapeDtypeStruct(wide, BF16),
            jax.ShapeDtypeStruct((heads, 2 * tokens), F32),
        ],
        [pltpu.VMEM((stream_len, 2 * tokens), F32)],
        query_sum, key, value.T, cosine_t, sine_t, *places_used,
    )
    attended_low, output_y, output_part, feed_h[0] = sync(
        attended_low, output_y, output_part, feed_h[0]
    )
    output_part = jnp.stack([output_part, output_y]).reshape(-1, half_width)
    output_c = swap_core(output_part)
    sent, feed_sent = sync(quarters[1], feed[:middle], attended_low)[:2]
    feed_h.append(swap(sent, "h"))
    feed_y = [swap(feed_sent, "y")]
    output_part, output_c, attended_low = sync(output_part, output_c, attended_low)
    output_full = jnp.concatenate([output_part, output_c])
    branch = lax.dot_general(
        attended_low, output_full, (((0,), (1,)), ((), ())), preferred_element_type=F32
    )
    branch_x, feed_h[1], feed_y[0], grad_low = sync(
        swap(low(branch[tokens:]), "x"), feed_h[1], feed_y[0], grad_low
    )
    hidden = inputs + (branch[:tokens] + branch_x.astype(F32))

    feed_h = [jnp.concatenate(feed_h)]
    sent2, sent3, feed_sent, branch_x = sync(quarters[2], quarters[3], feed[middle:], branch_x)
    sent2, sent3 = swap(sent2, "h"), swap(sent3, "h")
    feed_far = [swap(feed_h[0], "y")]
    scale_two = lax.rsqrt(jnp.mean(hidden * hidden, axis=-1, keepdims=True) + EPSILON)
    normed_two = hidden * scale_two
    normed_two_low = low(normed_two * gain_two)
    normed_two_low = gather_group(normed_two_low).reshape(-1, width)
    normed_two_low, sent2, sent3, feed_far[0] = sync(normed_two_low, sent2, sent3, feed_far[0])
    feed_h.append(jnp.concatenate([sent2, sent3]))
    feed_far.append(swap(feed_h[1], "y"))
    feed_y.append(swap(feed_sent, "y"))
    early = [feed, *feed_h, feed_y[0], feed_far[0]]
    early_c = [swap(piece, "c") for piece in early]
    feed_y[1], feed_far[1], *early_c = sync(feed_y[1], feed_far[1], *early_c)
    feed_all = [feed, *feed_h, *feed_y, *feed_far]
    feed_all = feed_all + [*early_c[:4], swap(feed_y[1], "c"), early_c[4]]
    feed_all = feed_all + [swap(feed_far[1], "c")]
    order = jnp.stack(
        [
            ((y ^ j) * 2 + (h ^ k)) * 2 + (c ^ i)
            for i in range(2)
            for j in range(2)
            for k in range(2)
        ]
    )
    group = 4 * tokens
    units = jax.ShapeDtypeStruct((group, part), BF16)
    features = jax.ShapeDtypeStruct((group, width), BF16)

    def held(count):
        return pltpu.VMEM((count, 8, M * 4, rows, part), BF16)

    wide_sum = pltpu.VMEM((group, part), F32)
    mixed_low, grad_gate, grad_up, grad_two = local_call(
        feed_kernel,
        [units, units, units, features],
        [held(3), wide_sum, wide_sum, pltpu.SemaphoreType.DMA((3, 14))],
        normed_two_low, grad_low, *feed_all,
        far=14,
    )

    half, block = width // 2, width // 8
    half_rows = jax.ShapeDtypeStruct((half, part), BF16)
    mixed_low, grad_gate, grad_up, grad_two = sync(mixed_low, grad_gate, grad_up, grad_two)
    grad_two = scatter_group(grad_two.reshape(4, tokens, width))
    both_grad = local_call(
        outer_all_kernel,
        [jax.ShapeDtypeStruct((8, 2, block, part), BF16)],
        [],
        order, normed_two_low, grad_gate, grad_up,
        scalars=1,
    )[0]
    mixed_low, both_grad = sync(mixed_low, both_grad)
    both_grad = lax.psum_scatter(both_grad, ("y", "h", "c"), scatter_dimension=0)
    down_far_half, down_near = local_call(
        outer_kernel, [half_rows] * 2, [], grad_low, mixed_low
    )
    mixed_low, down_far_half = sync(mixed_low, down_far_half)
    down_got = swap(down_far_half, "c")
    feed_out = local_call(
        feed_out_kernel,
        [features],
        [held(1), pltpu.SemaphoreType.DMA((1, 14))],
        mixed_low, *feed_all,
        far=14,
    )[0]

    def quarter(i, *more):
        at = slice(i * block, (i + 1) * block)
        total = down_near[at].astype(F32) + down_got[at].astype(F32)
        for other in more:
            total = total + other.astype(F32)
        return low(total)

    grad_two, down_got, feed_out = sync(grad_two, down_got, feed_out)
    across = (((0,), (1,)), ((), ()))
    grad_hidden = grad_mine.astype(F32) + norm_back(grad_two * gain_two, normed_two, scale_two)
    grad_hidden_low, grad_two = sync(low(grad_hidden), grad_two)
    hidden_x = swap(grad_hidden_low, "x")
    down_y3, down_y2 = swap(quarter(3), "y"), swap(quarter(2), "y")
    hidden_x, feed_out = sync(hidden_x, feed_out)
    feed_out = scatter_group(feed_out.reshape(4, tokens, width))
    grad_hidden_low = jnp.concatenate([grad_hidden_low, hidden_x])
    output_term = low(
        lax.dot_general(grad_hidden_low, attended_low, across, preferred_element_type=F32)
    )
    output_got = swap(output_term[half:], "c")
    grad_heads = low(
        lax.dot_general(
            output_full, grad_hidden_low, (((0,), (1,)), ((), ())), preferred_element_type=F32
        )
    )
    grad_heads, output_got, output_term = sync(grad_heads, output_got, output_term)
    query_grad_low, kv_grad = local_call(
        attend_back_kernel,
        [
            jax.ShapeDtypeStruct(wide, BF16),
            jax.ShapeDtypeStruct((stream_len, 2 * HEAD_DIM), F32),
        ],
        [pltpu.VMEM((stream_len, 2 * tokens), F32)],
        query_rot, key, key.T, value, grad_heads, attended, lse, cosine_t, sine_t, *places_used,
    )
    query_grad_low, kv_grad, down_y3 = sync(query_grad_low, kv_grad, down_y3)

    def fold_l(total):
        total = total.reshape(2, 2, M, 2, 2, rows, -1)
        return pick(total, l, 3), swap(low(pick(total, 1 - l, 3)), "l")

    def give_x(total, got):
        total = total + got.astype(F32)
        return pick(total, x, 3), swap(low(pick(total, 1 - x, 3)), "x")

    def take_x(total, got):
        got = got.astype(F32)
        both = pair(total[..., :half_width], got[..., :half_width], x, 4)
        both = both.reshape(2, 2, M, rows, query_width)
        return jnp.concatenate([both, (total + got)[..., half_width:]], -1)

    def next_fold(total, axis):
        return total[0], swap(low(total[1]), axis)

    kv_half = kv_grad.shape[0] // 2
    kv_sent = low(kv_grad[kv_half:])
    kv_got, feed_out, query_grad_low = sync(swap(kv_sent, "c"), feed_out, query_grad_low)
    kv_grad = (kv_grad[:kv_half] + kv_got.astype(F32)).reshape(4, M, 2, tokens, 2 * HEAD_DIM)
    kv_got = swap(low(kv_grad[2:]), "x")
    query_term = low(
        lax.dot_general(normed_one_low, query_grad_low, across, preferred_element_type=F32)
    )
    kv_got, query_term = sync(kv_got, query_term)
    kv_grad = kv_grad[:2] + kv_got.astype(F32)
    kv_got = swap(low(kv_grad[1]), "l")
    grad_one = lax.dot_general(
        query_grad_low, query_full, (((0,), (1,)), ((), ())), preferred_element_type=F32
    )
    kv_got, grad_one = sync(kv_got, grad_one)
    grad_one_x = swap(low(grad_one[tokens:]), "x")
    output_total, output_got = fold_l(
        output_term[:half].astype(F32) + output_got.astype(F32)
    )
    kv_grad = kv_grad[0] + kv_got.astype(F32)
    kv_got, grad_one_x = sync(swap(low(kv_grad[:, 1]), "h"), grad_one_x)
    down_h1 = swap(quarter(1, down_y3), "h")
    kv_mine = scatter_m(kv_grad[:, 0] + kv_got.astype(F32), 0) + shared_grad[0].astype(F32)
    keyvalue_grad_low = low(
        jnp.concatenate(
            [
                rotate(kv_mine[:, :HEAD_DIM], cosine[:tokens], -sine_part[:tokens]),
                kv_mine[:, HEAD_DIM:],
            ],
            -1,
        )
    )
    grad_one = grad_one[:tokens] + grad_one_x.astype(F32)
    grad_one = grad_one + contract_last(keyvalue_grad_low, keyvalue_full)
    gain_one_grad = jnp.sum(grad_one * normed_one, axis=0)
    gain_two_grad = jnp.sum(grad_two * normed_two, axis=0)
    small_grad = contract_first(normed_mine_low, keyvalue_grad_low)
    small_gains = jnp.stack([gain_one_grad, gain_two_grad], -1)
    small_gains = jnp.pad(small_gains, ((0, 0), (0, HEAD_DIM - 2)))
    query_total = jnp.concatenate([query_term, low(small_grad), low(small_gains)], -1)
    query_got = swap_core(query_total[half:])
    query_got, output_got, query_total = sync(query_got, output_got, query_total)
    query_total, query_got = fold_l(query_total[:half].astype(F32) + query_got.astype(F32))
    output_total, output_got = give_x(output_total, output_got)
    input_grad = outward(
        grad_hidden + norm_back(grad_one * gain_one, normed_one, scale_one)
    )[None]
    block_output = outward(low(hidden + feed_out))[None]
    output_got, down_y2 = sync(output_got, down_y2)
    output_total, output_got = next_fold(take_x(output_total, output_got), "y")
    query_got, output_got = sync(query_got, output_got)
    query_total, query_got = give_x(query_total, query_got)
    output_total, output_got = next_fold(output_total + output_got.astype(F32), "h")
    query_got, output_got, down_h1, both_grad = sync(query_got, output_got, down_h1, both_grad)
    query_total, query_got = next_fold(take_x(query_total, query_got), "y")
    output_weight_grad = scatter_m(output_total + output_got.astype(F32), 0)

    def finish_feed(own):
        own = low(scatter_m(own, 0))
        got = lax.all_to_all(own, ("l", "x"), 0, 0)
        return [merge(got[:, i]) for i in range(own.shape[1])]

    (down_weight_grad,) = finish_feed(
        quarter(0, down_h1, down_y2).reshape(M, 4, 1, rows, part)
    )
    query_got, down_weight_grad = sync(query_got, down_weight_grad)
    query_total, query_got = next_fold(query_total + query_got.astype(F32), "h")
    both_grad = both_grad.reshape(2, M, 4, rows, part).transpose(1, 2, 0, 3, 4)
    gate_weight_grad, up_weight_grad = finish_feed(both_grad)
    query_total = scatter_m(query_total + query_got.astype(F32), 0)
    query_weight_grad = query_total[:, :query_width]
    keyvalue_weight_grad = query_total[:, query_width : query_width + 2 * HEAD_DIM]
    gain_one_mine = query_total[:, query_width + 2 * HEAD_DIM]
    gain_two_mine = query_total[:, query_width + 2 * HEAD_DIM + 1]
    return (
        block_output,
        shared_mine[None],
        input_grad,
        gain_one_mine,
        query_weight_grad,
        keyvalue_weight_grad,
        output_weight_grad,
        gain_two_mine,
        gate_weight_grad,
        up_weight_grad,
        down_weight_grad,
    )


def solution(mesh):
    streams, seq = mesh.shape["dp"], mesh.shape["seq"]
    fine = Mesh(mesh.devices.reshape(streams, 2, 2, seq // 16, 2, 2), tuple(AXES))
    stream = P("y", tuple(AXES[1:]), None)
    vector, matrix = P(tuple(AXES)), P(tuple(AXES), None)
    return jax.shard_map(
        on_device,
        mesh=fine,
        in_specs=(
            stream,
            vector,
            matrix,
            matrix,
            matrix,
            vector,
            matrix,
            matrix,
            matrix,
            P("y", None),
            P(),
            stream,
            stream,
        ),
        out_specs=(
            stream,
            stream,
            stream,
            vector,
            matrix,
            matrix,
            matrix,
            vector,
            matrix,
            matrix,
            matrix,
        ),
        check_vma=False,
    )
```

```python
import functools
import math

import jax
import jax.numpy as jnp
from jax import lax
from jax.experimental import pallas as pl
from jax.experimental.pallas import tpu as pltpu
from jax.sharding import Mesh
from jax.sharding import PartitionSpec as P

HEAD_DIM = 128
EPSILON = 1e-05
NEGATIVE = -1e30
AXES = "yhlmxc"
BF16 = jnp.bfloat16
F32 = jnp.float32


def angles(offset):
    half_dim = HEAD_DIM // 2
    frequency = jnp.exp(
        jnp.arange(half_dim, dtype=F32) * (-2.0 * math.log(10000.0) / HEAD_DIM)
    )
    phases = offset.astype(F32)[:, None] * frequency[None, :]
    return (jnp.cos(phases), jnp.sin(phases))


def rotate(vectors, cosine, sine_part):
    half_dim = vectors.shape[-1] // 2
    first, second = vectors[..., :half_dim], vectors[..., half_dim:]
    return jnp.concatenate(
        [first * cosine - second * sine_part, second * cosine + first * sine_part], -1
    )


def dot(left, right):
    return jnp.dot(left, right, preferred_element_type=F32)


def contract_last(left, right):
    return lax.dot_general(left, right, (((1,), (1,)), ((), ())), preferred_element_type=F32)


def contract_first(left, right):
    return lax.dot_general(left, right, (((0,), (0,)), ((), ())), preferred_element_type=F32)


def norm_back(grad_normed, normed, scale_rows):
    return scale_rows * (
        grad_normed - normed * jnp.mean(grad_normed * normed, axis=-1, keepdims=True)
    )


def swap(value, axis):
    return lax.ppermute(value, axis, [(0, 1), (1, 0)])


def swap_core(value):
    return jnp.concatenate(core_parts(value))


def core_parts(value):
    size = value.shape[0] // 4
    return [swap(value[i * size : (i + 1) * size], "c") for i in range(4)]


def low(value):
    return value.astype(BF16)


def sync(*values):
    return lax.optimization_barrier(values)


def pick(stacked, index, axis=0):
    return lax.dynamic_index_in_dim(stacked, index, axis, keepdims=False)


def pair(own, other, index, axis=0):
    return jnp.where(
        index == 0, jnp.stack([own, other], axis), jnp.stack([other, own], axis)
    )


def gather_m(value, axis):
    if lax.axis_size("m") > 1:
        return lax.all_gather(value, "m", axis=axis)
    return jnp.expand_dims(value, axis)


def scatter_m(value, axis):
    if lax.axis_size("m") > 1:
        return lax.psum_scatter(value, "m", scatter_dimension=axis)
    return lax.squeeze(value, (axis,))


def fold(total, axis):
    half = total.shape[0] // 2
    return total[:half].astype(F32) + swap(low(total[half:]), axis).astype(F32)


def gather_group(value):
    return lax.all_to_all(jnp.broadcast_to(value, (4, *value.shape)), ("l", "x"), 0, 0)


def scatter_group(value):
    return jnp.sum(lax.all_to_all(low(value), ("l", "x"), 0, 0).astype(F32), axis=0)


LOG2E = math.log2(math.e)
SCALE = 1.0 / math.sqrt(HEAD_DIM)
NT = (((1,), (1,)), ((), ()))
NN = (((1,), (0,)), ((), ()))


def mxu(left, right, dims):
    return lax.dot_general(left, right, dims, preferred_element_type=F32)


def turn(vectors, cosine, sine_part):
    half = HEAD_DIM // 2
    first, second = vectors[:half], vectors[half:]
    return jnp.concatenate(
        [first * cosine - second * sine_part, second * cosine + first * sine_part], 0
    )


def fill_bias(bias, key_place, query_place, query_start):
    keys = bias.shape[0]
    block = 256
    for i in range(keys // block):
        at = key_place[i * block : (i + 1) * block, :]
        fits = (at <= query_place[...]) & (at >= query_start[...])
        bias[i * block : (i + 1) * block, :] = jnp.where(fits, 0.0, NEGATIVE)


def each_pair(one, count, keys):
    def step(pair, unused):
        one(pair * 2, pl.ds(pl.multiple_of(pair * 2 * HEAD_DIM, 2 * HEAD_DIM), 2 * HEAD_DIM))
        return unused

    if keys > 2048:
        lax.fori_loop(0, count // 2, step, 0)
    else:
        for pair in range(count // 2):
            step(pair, 0)


def rows_of(head):
    return pl.ds(pl.multiple_of(head * HEAD_DIM, HEAD_DIM), HEAD_DIM)


def attend_kernel(
    normed, near, far_0, far_1, far_2, far_3, keyvalue, cosine, sine_part, key_place,
    query_place, query_start, query_rot, attended, attended_low, lse, bias, value_t,
):
    fill_bias(bias, key_place, query_place, query_start)
    value_t[...] = keyvalue[:, HEAD_DIM:].T
    parts = [(0, near)]
    for part in (far_0, far_1, far_2, far_3):
        parts.append((parts[-1][0] + parts[-1][1].shape[0], part))

    def one(first, columns):
        total = sum(
            mxu(normed[:, at : at + part.shape[0]], part[:, columns], NN) for at, part in parts
        )
        turned = total.T
        for i in range(2):
            at = rows_of(first + i)
            query = turn(
                turned[i * HEAD_DIM : (i + 1) * HEAD_DIM], cosine[...], sine_part[...]
            ).astype(BF16)
            query_rot[at, :] = query
            scores = mxu(keyvalue[:, :HEAD_DIM], query, NN) * (SCALE * LOG2E) + bias[...]
            top = jnp.max(scores, axis=0, keepdims=True)
            weights = jnp.exp2(scores - top)
            total = jnp.sum(weights, axis=0, keepdims=True)
            result = mxu(value_t[...], weights.astype(BF16), NN) / total
            attended[at, :] = result
            attended_low[at, :] = result.astype(BF16)
            lse[pl.ds(first + i, 1), :] = top + jnp.log2(total)

    each_pair(one, query_rot.shape[0] // HEAD_DIM, keyvalue.shape[0])


def attend_back_kernel(
    query_rot, keyvalue, grad_hidden, output_weight, attended, lse, cosine, sine_part,
    key_place, query_place, query_start, query_grad, kv_grad, bias, key_t,
):
    fill_bias(bias, key_place, query_place, query_start)
    kv_grad[...] = jnp.zeros_like(kv_grad)
    key_t[...] = keyvalue[:, :HEAD_DIM].T

    def one(first, columns):
        turned = mxu(grad_hidden[...], output_weight[:, columns], NN).T.astype(BF16)
        for i in range(2):
            at = rows_of(first + i)
            query = query_rot[at, :]
            grad_head = turned[i * HEAD_DIM : (i + 1) * HEAD_DIM]
            delta = jnp.sum(grad_head.astype(F32) * attended[at, :], axis=0, keepdims=True)
            scores = mxu(keyvalue[:, :HEAD_DIM], query, NN) * (SCALE * LOG2E) + bias[...]
            probs = jnp.exp2(scores - lse[pl.ds(first + i, 1), :])
            grad_probs = mxu(keyvalue[:, HEAD_DIM:], grad_head, NN)
            grad_scores = (probs * (grad_probs - delta)).astype(BF16)
            kv_grad[:, :HEAD_DIM] += mxu(grad_scores, query, NT) * SCALE
            kv_grad[:, HEAD_DIM:] += mxu(probs.astype(BF16), grad_head, NT)
            grad_query = mxu(key_t[...], grad_scores, NN) * SCALE
            query_grad[at, :] = turn(grad_query, cosine[...], -sine_part[...]).astype(BF16)

    each_pair(one, query_rot.shape[0] // HEAD_DIM, keyvalue.shape[0])


def columns_of(width):
    return width // 256, width % 256


def each_block(width, body):
    full, rest = columns_of(width)

    def step(i, unused):
        body(pl.ds(pl.multiple_of(i * 256, 256), 256))
        return unused

    lax.fori_loop(0, full, step, 0)
    if rest:
        body(pl.ds(full * 256, rest))


def load_pieces(pieces, held, slot, sems):
    copies = [
        pltpu.make_async_copy(piece, held.at[slot, p], sems.at[slot, p])
        for p, piece in enumerate(pieces)
    ]
    for copy in copies:
        copy.start()

    def wait():
        for copy in copies:
            copy.wait()

    return wait


def gate_up_kernel(normed, *refs):
    gate_sum, up_sum, held, sems = refs[16:]
    waits = [load_pieces(refs[8 * i : 8 * i + 8], held, i, sems) for i in range(2)]
    width, part = normed.shape[1], gate_sum.shape[1]
    for slot, result in enumerate((gate_sum, up_sum)):
        waits[slot]()

        def step(at):
            result[:, at] = mxu(
                normed[...], held[slot, :, :, :, at].reshape(width, at.size), NN
            )

        each_block(part, step)


def feed_kernel(grad, gate_sum, up_sum, *refs):
    mixed, grad_gate, grad_up, grad_two, held, sems = refs[24:]
    waits = [load_pieces(refs[8 * i : 8 * i + 8], held, i, sems) for i in range(3)]
    width, part = grad.shape[1], mixed.shape[1]
    waits[0]()

    def down_step(at):
        grad_mixed = mxu(grad[...], held[0, :, :, :, at].reshape(width, at.size), NN)
        gate, up = gate_sum[:, at], up_sum[:, at]
        sigmoid_gate = jax.nn.sigmoid(gate)
        silu_gate = gate * sigmoid_gate
        mixed[:, at] = (silu_gate * up).astype(BF16)
        grad_up[:, at] = (grad_mixed * silu_gate).astype(BF16)
        grad_gate[:, at] = (
            grad_mixed * up * sigmoid_gate * (1.0 + gate * (1.0 - sigmoid_gate))
        ).astype(BF16)

    each_block(part, down_step)
    waits[1]()
    waits[2]()

    def two_step(p, unused):
        at = pl.ds(pl.multiple_of(p * (width // 8), width // 8), width // 8)
        grad_two[:, at] = (
            mxu(grad_gate[...], held[1, p].reshape(width // 8, part), NT)
            + mxu(grad_up[...], held[2, p].reshape(width // 8, part), NT)
        ).astype(BF16)
        return unused

    lax.fori_loop(0, 8, two_step, 0)


def outer_kernel(left, *refs):
    count = len(refs) // 3
    rights, results = refs[:count], refs[count:]
    rows = left.shape[1] // 8

    def step(p, unused):
        to = pl.ds(pl.multiple_of(p * rows, rows), rows)
        for part in range(2):
            first = 4 * (1 - part)
            at = pl.ds(pl.multiple_of((first + p) * rows, rows), rows)
            turned = left[:, at].T
            for i, right in enumerate(rights):
                result = results[2 * i + part]
                result[to, :] = mxu(turned, right[...], NN).astype(result.dtype)
        return unused

    lax.fori_loop(0, 4, step, 0)


def outer_all_kernel(order, left, *refs):
    *rights, result = refs
    rows = left.shape[1] // 8

    def step(p, unused):
        at = pl.ds(pl.multiple_of(p * rows, rows), rows)
        turned = left[:, at].T
        for i, right in enumerate(rights):
            result[order[p], i] = mxu(turned, right[...], NN).astype(result.dtype)
        return unused

    lax.fori_loop(0, 8, step, 0)


def feed_out_kernel(mixed, *refs):
    feed, held, sems = refs[8:]
    load_pieces(refs[:8], held, 0, sems)()
    width, part = feed.shape[1], mixed.shape[1]

    def feed_step(p, unused):
        at = pl.ds(pl.multiple_of(p * (width // 8), width // 8), width // 8)
        feed[:, at] = mxu(
            mixed[...], held[0, p].reshape(width // 8, part), NT
        ).astype(BF16)
        return unused

    lax.fori_loop(0, 8, feed_step, 0)


def split_kernel(*refs):
    result = refs[-1]
    for i, matrix in enumerate(refs[:-1]):
        result[0, i] = matrix[...]


def split(*matrices):
    rows, columns = matrices[0].shape
    count, part = len(matrices), columns // 4
    return pl.pallas_call(
        split_kernel,
        out_shape=jax.ShapeDtypeStruct((4, count, rows, part), matrices[0].dtype),
        grid=(4,),
        in_specs=[pl.BlockSpec((rows, part), lambda i: (0, i))] * count,
        out_specs=pl.BlockSpec((1, count, rows, part), lambda i: (i, 0, 0, 0)),
        cost_estimate=NO_COST,
    )(*matrices)


def merge_kernel(parts, result):
    result[...] = parts[0].astype(F32)


def merge(parts):
    _, rows, part = parts.shape
    return pl.pallas_call(
        merge_kernel,
        out_shape=jax.ShapeDtypeStruct((rows, 4 * part), F32),
        grid=(4,),
        in_specs=[pl.BlockSpec((1, rows, part), lambda i: (i, 0, 0))],
        out_specs=pl.BlockSpec((rows, part), lambda i: (0, i)),
        cost_estimate=NO_COST,
    )(parts)


NO_COST = pl.CostEstimate(flops=1, bytes_accessed=1, transcendentals=0)


def local_call(kernel, outs, scratch, *args, far=0, scalars=0):
    near = [pl.BlockSpec(memory_space=pltpu.SMEM)] * scalars
    near = near + [pl.BlockSpec(memory_space=pltpu.VMEM)] * (len(args) - far - scalars)
    return pl.pallas_call(
        kernel,
        out_shape=outs,
        in_specs=near + [pl.BlockSpec(memory_space=pl.ANY)] * far,
        out_specs=[pl.BlockSpec(memory_space=pltpu.VMEM)] * len(outs),
        scratch_shapes=scratch,
        compiler_params=pltpu.CompilerParams(vmem_limit_bytes=56 << 20),
        cost_estimate=NO_COST,
    )(*args)


def on_device(
    block_input,
    attention_gain,
    query_weight,
    keyvalue_weight,
    output_weight,
    feedforward_gain,
    gate_weight,
    up_weight,
    down_weight,
    document_lengths,
    piece_order,
    output_grad,
    shared_grad,
):
    y, h, l, m, x, c = (lax.axis_index(a) for a in AXES)
    M = lax.axis_size("m")
    tokens, width = block_input.shape[1:]
    rows = query_weight.shape[0]
    query_width = query_weight.shape[1]
    half_width = query_width // 2
    heads = half_width // HEAD_DIM
    hidden_units = gate_weight.shape[1]
    part = hidden_units // 4
    piece_len = tokens // 2

    def inward(value):
        value = value.reshape(tokens, 2, 2, 2, M, 2, 2, rows)
        value = value.transpose(0, 6, 1, 2, 4, 3, 5, 7)
        value = jnp.where(c == 0, value, value[:, ::-1])
        value = jnp.where(y == 0, value, value[:, :, ::-1])
        value = jnp.where(h == 0, value, value[:, :, :, ::-1])
        return value.reshape(tokens, width)

    def outward(value):
        value = value.reshape(tokens, 2, 2, 2, M, 2, 2, rows)
        value = jnp.where(h == 0, value, value[:, :, :, ::-1])
        value = jnp.where(y == 0, value, value[:, :, ::-1])
        value = jnp.where(c == 0, value, value[:, ::-1])
        return value.transpose(0, 2, 3, 5, 4, 6, 1, 7).reshape(tokens, width)

    finish = jnp.cumsum(document_lengths[0])
    starts = finish - document_lengths[0]

    def places(slots):
        order = piece_order[(slots[:, None] * 2 + jnp.arange(2)[None, :]).reshape(-1)]
        return (
            order[:, None] * piece_len + jnp.arange(piece_len, dtype=jnp.int32)[None, :]
        ).reshape(-1)

    def slot(h_at, l_at, m_at, x_at, c_at):
        return (((h_at * 2 + l_at) * M + m_at) * 2 + x_at) * 2 + c_at

    position = places(jnp.stack([slot(h, l, m, x, c), slot(h, l, m, 1 - x, c)]))
    begins = jnp.max(
        jnp.where(starts[None, :] <= position[:, None], starts[None, :], 0), axis=1
    )
    key_position = places(
        jnp.stack(
            [
                slot(h ^ i, l ^ j, m_at, x ^ k, c ^ n)
                for n in range(2)
                for k in range(2)
                for j in range(2)
                for m_at in range(M)
                for i in range(2)
            ]
        )
    )[:, None]
    query_place, query_start = position[None, :], begins[None, :]
    cosine, sine_part = angles(position - begins)

    gains = jnp.stack([attention_gain, feedforward_gain])
    gains = jnp.pad(gains, ((0, 14), (0, 2 * HEAD_DIM - rows)))
    small = jnp.concatenate([keyvalue_weight, gains])

    def halves(weight):
        parts = weight.reshape(rows, 2, half_width).transpose(1, 0, 2)
        return pick(parts, x), pick(parts, 1 - x)

    query_mine, query_sent = halves(query_weight)
    output_mine, output_sent = halves(output_weight)

    small_x, query_x, output_x = sync(
        swap(small, "x"), swap(query_sent, "x"), swap(output_sent, "x")
    )
    small = pair(small, small_x, x)
    query_part, output_part = pair(query_mine, query_x, x), pair(output_mine, output_x, x)
    input_mine, small, gate_weight, up_weight, down_weight = sync(
        inward(block_input[0]), small, gate_weight, up_weight, down_weight
    )
    feed_parts = split(gate_weight, up_weight, down_weight)
    small_l, query_l, output_l, input_other = sync(
        swap(small, "l"), swap(query_part, "l"), swap(output_part, "l"), swap(input_mine, "x")
    )
    small = gather_m(pair(small, small_l, l), 0)
    query_part = gather_m(pair(query_part, query_l, l), 0)
    output_part = gather_m(pair(output_part, output_l, l), 0)
    small, query_part, feed_parts = sync(small, query_part, feed_parts)
    query_h = swap(query_part, "h")
    small_h = sync(swap(small, "h"))[0]
    small, feed_parts = sync(jnp.stack([small, small_h]), feed_parts)
    feed = gather_m(lax.all_to_all(feed_parts, ("l", "x"), 0, 0), 0)
    feed = feed.reshape(M * 4, 3, rows, part)
    small_y = sync(swap(small, "y"))[0]
    small = jnp.stack([small, small_y]).reshape(4, M * 4, rows + 16, 2 * HEAD_DIM)
    small_c, input_other, query_h = sync(swap_core(small), input_other, query_h)
    small = jnp.stack([small, small_c])
    small = small.reshape(width // rows, rows + 16, 2 * HEAD_DIM)
    keyvalue_full = small[:, :rows].reshape(width, 2 * HEAD_DIM)
    gain_one = small[:, rows, :rows].reshape(1, width).astype(F32)
    gain_two = small[:, rows + 1, :rows].reshape(1, width).astype(F32)
    def normalize(value):
        value = value.astype(F32)
        scale = lax.rsqrt(jnp.mean(value * value, axis=-1, keepdims=True) + EPSILON)
        normed = value * scale
        return value, scale, normed, low(normed * gain_one)

    inputs, scale_one, normed_one, normed_mine_low = normalize(input_mine)
    keyvalue_sum = dot(normed_mine_low, keyvalue_full)
    shared_mine = low(
        jnp.concatenate(
            [
                rotate(keyvalue_sum[:, :HEAD_DIM], cosine[:tokens], sine_part[:tokens]),
                keyvalue_sum[:, HEAD_DIM:],
            ],
            -1,
        )
    )
    query_part, keyvalue_sum, key_position, query_place, query_start, cosine_t, sine_t = sync(
        jnp.stack([query_part, query_h]),
        keyvalue_sum,
        key_position,
        query_place,
        query_start,
        cosine.T,
        sine_part.T,
    )
    query_y = swap(query_part, "y")
    shared_h, input_other = sync(swap(shared_mine, "h"), input_other)
    gathered = gather_m(jnp.stack([shared_mine, shared_h]), 0)
    gathered, input_other, output_part = sync(gathered, input_other, output_part)
    output_h = swap(output_part, "h")
    normed_one_low = jnp.concatenate([normed_mine_low, normalize(input_other)[3]])
    shared_l, normed_one_low, feed = sync(swap(gathered, "l"), normed_one_low, feed)
    gate, up, down, gathered = sync(
        *(feed[:, i] for i in range(3)), jnp.stack([gathered, shared_l])
    )
    shared_x, query_y, output_h = sync(swap(gathered, "x"), query_y, output_h)
    gathered = jnp.stack([gathered, shared_x]).reshape(4, -1, 2 * HEAD_DIM)
    query_part = jnp.stack([query_part, query_y]).reshape(-1, half_width)
    query_part, gathered = sync(query_part, gathered)
    query_c = core_parts(query_part)
    shared_c, *query_c = sync(swap_core(gathered), *query_c)
    output_part = jnp.stack([output_part, output_h])
    output_part, gate, shared_c = sync(output_part, gate, shared_c)
    output_y = swap(output_part, "y")
    gate_h = swap(gate, "h")
    gate_sent, query_place = sync(gate, query_place, *query_c)[:2]
    gate_y = swap(gate_sent, "y")
    gathered = jnp.stack([gathered, shared_c]).reshape(-1, 2 * HEAD_DIM)
    stream_len = gathered.shape[0]
    grad_mine = inward(output_grad[0])
    wide = (half_width, 2 * tokens)
    places_used = (key_position, query_place, query_start)
    query_rot, attended, attended_low, lse = local_call(
        attend_kernel,
        [
            jax.ShapeDtypeStruct(wide, BF16),
            jax.ShapeDtypeStruct(wide, F32),
            jax.ShapeDtypeStruct(wide, BF16),
            jax.ShapeDtypeStruct((heads, 2 * tokens), F32),
        ],
        [
            pltpu.VMEM((stream_len, 2 * tokens), F32),
            pltpu.VMEM((HEAD_DIM, stream_len), BF16),
        ],
        normed_one_low, query_part, *query_c, gathered, cosine_t, sine_t, *places_used,
    )
    attended_low, output_y, output_part, gate_h, gate_y = sync(
        attended_low, output_y, output_part, gate_h, gate_y
    )
    output_part = jnp.stack([output_part, output_y]).reshape(-1, half_width)
    output_c = swap_core(output_part)
    up_sent, attended_low = sync(up, attended_low)
    up_h, up_y = swap(up_sent, "h"), swap(up_sent, "y")
    output_part, output_c, attended_low = sync(output_part, output_c, attended_low)
    output_full = jnp.concatenate([output_part, output_c])
    branch = lax.dot_general(
        attended_low, output_full, (((0,), (1,)), ((), ())), preferred_element_type=F32
    )
    branch, gate_h = sync(branch, gate_h)
    gate_far = swap(gate_h, "y")
    branch_x, up_h, up_y, gate_far, grad_mine = sync(
        swap(low(branch[tokens:]), "x"), up_h, up_y, gate_far, grad_mine
    )
    hidden = inputs + (branch[:tokens] + branch_x.astype(F32))

    down_sent, branch_x = sync(down, branch_x)
    down_h, up_far, down_y = swap(down_sent, "h"), swap(up_h, "y"), swap(down_sent, "y")
    scale_two = lax.rsqrt(jnp.mean(hidden * hidden, axis=-1, keepdims=True) + EPSILON)
    normed_two = hidden * scale_two
    normed_two_low = low(normed_two * gain_two)
    normed_two_low = gather_group(normed_two_low).reshape(-1, width)
    up_far, *sent = sync(up_far, gate, gate_h, gate_y, gate_far, up, up_h, up_y)
    near_c = [swap(piece, "c") for piece in sent]
    normed_two_low, down_h, down_y, *near_c = sync(normed_two_low, down_h, down_y, *near_c)
    down_far = swap(down_h, "y")
    gate_c = near_c[:4]
    up_sent, grad_sent = sync(up_far, grad_mine, normed_two_low)[:2]
    late_c = [swap(up_sent, "c")]
    up_c = near_c[4:] + late_c
    grad_low = gather_group(grad_sent).reshape(-1, width)
    gate_all = [gate, gate_h, gate_y, gate_far, *gate_c]
    up_all = [up, up_h, up_y, up_far, *up_c]
    group = 4 * tokens
    units = jax.ShapeDtypeStruct((group, part), BF16)
    unit_sums = jax.ShapeDtypeStruct((group, part), F32)
    features = jax.ShapeDtypeStruct((group, width), BF16)

    def held(count):
        return [
            pltpu.VMEM((count, 8, M * 4, rows, part), BF16),
            pltpu.SemaphoreType.DMA((count, 8)),
        ]

    down_c = [swap(piece, "c") for piece in (down, down_h, down_y)]
    gate_sum, up_sum = local_call(
        gate_up_kernel, [unit_sums] * 2, held(2), normed_two_low, *gate_all, *up_all, far=16
    )
    down_far, gate_sum, *down_c = sync(down_far, gate_sum, *down_c)
    down_all = [down, down_h, down_y, down_far, *down_c, swap(down_far, "c")]
    order = jnp.stack(
        [
            ((y ^ j) * 2 + (h ^ k)) * 2 + (c ^ i)
            for i in range(2)
            for j in range(2)
            for k in range(2)
        ]
    )
    mixed_low, grad_gate, grad_up, grad_two = local_call(
        feed_kernel,
        [units, units, units, features],
        held(3),
        grad_low, gate_sum, up_sum, *down_all, *gate_all, *up_all,
        far=24,
    )

    half, block = width // 2, width // 8
    half_rows = jax.ShapeDtypeStruct((half, part), BF16)
    mixed_low, grad_gate, grad_up, grad_two = sync(mixed_low, grad_gate, grad_up, grad_two)
    grad_two = scatter_group(grad_two.reshape(4, tokens, width))
    both_grad = local_call(
        outer_all_kernel,
        [jax.ShapeDtypeStruct((8, 2, block, part), BF16)],
        [],
        order, normed_two_low, grad_gate, grad_up,
        scalars=1,
    )[0]
    mixed_low, both_grad = sync(mixed_low, both_grad)
    both_grad = lax.psum_scatter(both_grad, ("y", "h", "c"), scatter_dimension=0)
    down_far_half, down_near = local_call(
        outer_kernel, [half_rows] * 2, [], grad_low, mixed_low
    )
    mixed_low, down_far_half = sync(mixed_low, down_far_half)
    down_got = swap(down_far_half, "c")
    def quarter(i, *more):
        at = slice(i * block, (i + 1) * block)
        total = down_near[at].astype(F32) + down_got[at].astype(F32)
        for other in more:
            total = total + other.astype(F32)
        return low(total)

    grad_two, down_got = sync(grad_two, down_got)
    across = (((0,), (1,)), ((), ()))
    grad_hidden = grad_mine.astype(F32) + norm_back(grad_two * gain_two, normed_two, scale_two)
    grad_hidden_low, grad_two = sync(low(grad_hidden), grad_two)
    hidden_x = swap(grad_hidden_low, "x")
    down_y3, down_y2 = swap(quarter(3), "y"), swap(quarter(2), "y")
    mixed_low = sync(mixed_low, grad_hidden_low)[0]
    feed_out = local_call(
        feed_out_kernel,
        [features],
        held(1),
        mixed_low, *down_all,
        far=8,
    )[0]
    hidden_x, feed_out = sync(hidden_x, feed_out)
    feed_out = scatter_group(feed_out.reshape(4, tokens, width))
    grad_hidden_low = jnp.concatenate([grad_hidden_low, hidden_x])
    query_grad_low, kv_grad = local_call(
        attend_back_kernel,
        [
            jax.ShapeDtypeStruct(wide, BF16),
            jax.ShapeDtypeStruct((stream_len, 2 * HEAD_DIM), F32),
        ],
        [
            pltpu.VMEM((stream_len, 2 * tokens), F32),
            pltpu.VMEM((HEAD_DIM, stream_len), BF16),
        ],
        query_rot, gathered, grad_hidden_low, output_full, attended, lse, cosine_t, sine_t,
        *places_used,
    )
    query_grad_low, kv_grad, grad_hidden_low = sync(query_grad_low, kv_grad, grad_hidden_low)

    def fold_l(total):
        total = total.reshape(2, 2, M, 2, 2, rows, -1)
        return pick(total, l, 3), swap(low(pick(total, 1 - l, 3)), "l")

    def give_x(total, got):
        total = total + got.astype(F32)
        return pick(total, x, 3), swap(low(pick(total, 1 - x, 3)), "x")

    def take_x(total, got):
        got = got.astype(F32)
        both = pair(total[..., :half_width], got[..., :half_width], x, 4)
        both = both.reshape(2, 2, M, rows, query_width)
        return jnp.concatenate([both, (total + got)[..., half_width:]], -1)

    def next_fold(total, axis):
        return total[0], swap(low(total[1]), axis)

    kv_half = kv_grad.shape[0] // 2
    kv_sent = low(kv_grad[kv_half:]).reshape(4, -1, 2 * HEAD_DIM)
    output_term = low(
        lax.dot_general(grad_hidden_low, attended_low, across, preferred_element_type=F32)
    )
    kv_got, query_grad_low, output_term, feed_out, down_y3 = sync(
        swap_core(kv_sent), query_grad_low, output_term, feed_out, down_y3
    )
    output_got = swap_core(output_term[half:])
    kv_grad = kv_grad[:kv_half].reshape(4, M, 2, tokens, 2 * HEAD_DIM)
    kv_grad = kv_grad + kv_got.astype(F32).reshape(kv_grad.shape)
    kv_got = swap(low(kv_grad[2:]), "x")
    query_term = low(
        lax.dot_general(normed_one_low, query_grad_low, across, preferred_element_type=F32)
    )
    down_h1 = swap(quarter(1, down_y3), "h")
    kv_got, query_term, output_got = sync(kv_got, query_term, output_got)
    kv_grad = kv_grad[:2] + kv_got.astype(F32)
    kv_got = swap(low(kv_grad[1]), "l")
    query_full = jnp.concatenate([query_part, *query_c])
    grad_one = lax.dot_general(
        query_grad_low, query_full, (((0,), (1,)), ((), ())), preferred_element_type=F32
    )
    kv_got, grad_one = sync(kv_got, grad_one)
    grad_one_x = swap(low(grad_one[tokens:]), "x")
    output_total, output_got = fold_l(
        output_term[:half].astype(F32) + output_got.astype(F32)
    )
    kv_grad = kv_grad[0] + kv_got.astype(F32)
    kv_got, grad_one_x = sync(swap(low(kv_grad[:, 1]), "h"), grad_one_x)
    kv_mine = scatter_m(kv_grad[:, 0] + kv_got.astype(F32), 0) + shared_grad[0].astype(F32)
    keyvalue_grad_low = low(
        jnp.concatenate(
            [
                rotate(kv_mine[:, :HEAD_DIM], cosine[:tokens], -sine_part[:tokens]),
                kv_mine[:, HEAD_DIM:],
            ],
            -1,
        )
    )
    grad_one = grad_one[:tokens] + grad_one_x.astype(F32)
    grad_one = grad_one + contract_last(keyvalue_grad_low, keyvalue_full)
    gain_one_grad = jnp.sum(grad_one * normed_one, axis=0)
    gain_two_grad = jnp.sum(grad_two * normed_two, axis=0)
    small_grad = contract_first(normed_mine_low, keyvalue_grad_low)
    small_gains = jnp.stack([gain_one_grad, gain_two_grad], -1)
    small_gains = jnp.pad(small_gains, ((0, 0), (0, HEAD_DIM - 2)))
    query_total = jnp.concatenate([query_term, low(small_grad), low(small_gains)], -1)
    query_got = swap_core(query_total[half:])
    query_got, output_got, query_total = sync(query_got, output_got, query_total)
    query_total, query_got = fold_l(query_total[:half].astype(F32) + query_got.astype(F32))
    output_total, output_got = give_x(output_total, output_got)
    input_grad = outward(
        grad_hidden + norm_back(grad_one * gain_one, normed_one, scale_one)
    )[None]
    block_output = outward(low(hidden + feed_out))[None]
    output_got, down_y2 = sync(output_got, down_y2)
    output_total, output_got = next_fold(take_x(output_total, output_got), "y")
    query_got, output_got = sync(query_got, output_got)
    query_total, query_got = give_x(query_total, query_got)
    output_total, output_got = next_fold(output_total + output_got.astype(F32), "h")
    query_got, output_got, down_h1, both_grad = sync(query_got, output_got, down_h1, both_grad)
    query_total, query_got = next_fold(take_x(query_total, query_got), "y")
    output_weight_grad = scatter_m(output_total + output_got.astype(F32), 0)
    def finish_feed(own):
        own = low(scatter_m(own, 0))
        got = lax.all_to_all(own, ("l", "x"), 0, 0)
        return [merge(got[:, i]) for i in range(own.shape[1])]

    (down_weight_grad,) = finish_feed(
        quarter(0, down_h1, down_y2).reshape(M, 4, 1, rows, part)
    )
    query_got, down_weight_grad = sync(query_got, down_weight_grad)
    query_total, query_got = next_fold(query_total + query_got.astype(F32), "h")
    both_grad = both_grad.reshape(2, M, 4, rows, part).transpose(1, 2, 0, 3, 4)
    gate_weight_grad, up_weight_grad = finish_feed(both_grad)
    query_total = scatter_m(query_total + query_got.astype(F32), 0)
    query_weight_grad = query_total[:, :query_width]
    keyvalue_weight_grad = query_total[:, query_width : query_width + 2 * HEAD_DIM]
    gain_one_mine = query_total[:, query_width + 2 * HEAD_DIM]
    gain_two_mine = query_total[:, query_width + 2 * HEAD_DIM + 1]
    return (
        block_output,
        shared_mine[None],
        input_grad,
        gain_one_mine,
        query_weight_grad,
        keyvalue_weight_grad,
        output_weight_grad,
        gain_two_mine,
        gate_weight_grad,
        up_weight_grad,
        down_weight_grad,
    )


def solution(mesh):
    streams, seq = mesh.shape["dp"], mesh.shape["seq"]
    fine = Mesh(mesh.devices.reshape(streams, 2, 2, seq // 16, 2, 2), tuple(AXES))
    stream = P("y", tuple(AXES[1:]), None)
    vector, matrix = P(tuple(AXES)), P(tuple(AXES), None)
    return jax.shard_map(
        on_device,
        mesh=fine,
        in_specs=(
            stream,
            vector,
            matrix,
            matrix,
            matrix,
            vector,
            matrix,
            matrix,
            matrix,
            P("y", None),
            P(),
            stream,
            stream,
        ),
        out_specs=(
            stream,
            stream,
            stream,
            vector,
            matrix,
            matrix,
            matrix,
            vector,
            matrix,
            matrix,
            matrix,
        ),
        check_vma=False,
    )
```

```python
import functools
import math

import jax
import jax.numpy as jnp
from jax import lax
from jax.experimental import pallas as pl
from jax.experimental.pallas import tpu as pltpu
from jax.sharding import Mesh
from jax.sharding import PartitionSpec as P

HEAD_DIM = 128
EPSILON = 1e-05
NEGATIVE = -1e30
AXES = "yhlmxc"
BF16 = jnp.bfloat16
F32 = jnp.float32


def angles(offset):
    half_dim = HEAD_DIM // 2
    frequency = jnp.exp(
        jnp.arange(half_dim, dtype=F32) * (-2.0 * math.log(10000.0) / HEAD_DIM)
    )
    phases = offset.astype(F32)[:, None] * frequency[None, :]
    return (jnp.cos(phases), jnp.sin(phases))


def rotate(vectors, cosine, sine_part):
    half_dim = vectors.shape[-1] // 2
    first, second = vectors[..., :half_dim], vectors[..., half_dim:]
    return jnp.concatenate(
        [first * cosine - second * sine_part, second * cosine + first * sine_part], -1
    )


def dot(left, right):
    return jnp.dot(left, right, preferred_element_type=F32)


def contract_last(left, right):
    return lax.dot_general(left, right, (((1,), (1,)), ((), ())), preferred_element_type=F32)


def contract_first(left, right):
    return lax.dot_general(left, right, (((0,), (0,)), ((), ())), preferred_element_type=F32)


def norm_back(grad_normed, normed, scale_rows):
    return scale_rows * (
        grad_normed - normed * jnp.mean(grad_normed * normed, axis=-1, keepdims=True)
    )


def swap(value, axis):
    return lax.ppermute(value, axis, [(0, 1), (1, 0)])


def swap_core(value):
    return jnp.concatenate(core_parts(value))


def core_parts(value):
    size = value.shape[0] // 4
    return [swap(value[i * size : (i + 1) * size], "c") for i in range(4)]


def low(value):
    return value.astype(BF16)


def sync(*values):
    return lax.optimization_barrier(values)


def pick(stacked, index, axis=0):
    return lax.dynamic_index_in_dim(stacked, index, axis, keepdims=False)


def pair(own, other, index, axis=0):
    return jnp.where(
        index == 0, jnp.stack([own, other], axis), jnp.stack([other, own], axis)
    )


def gather_m(value, axis):
    if lax.axis_size("m") > 1:
        return lax.all_gather(value, "m", axis=axis)
    return jnp.expand_dims(value, axis)


def scatter_m(value, axis):
    if lax.axis_size("m") > 1:
        return lax.psum_scatter(value, "m", scatter_dimension=axis)
    return lax.squeeze(value, (axis,))


def fold(total, axis):
    half = total.shape[0] // 2
    return total[:half].astype(F32) + swap(low(total[half:]), axis).astype(F32)


def gather_group(value):
    return lax.all_to_all(jnp.broadcast_to(value, (4, *value.shape)), ("l", "x"), 0, 0)


def scatter_group(value):
    return jnp.sum(lax.all_to_all(low(value), ("l", "x"), 0, 0).astype(F32), axis=0)


LOG2E = math.log2(math.e)
SCALE = 1.0 / math.sqrt(HEAD_DIM)
NT = (((1,), (1,)), ((), ()))
NN = (((1,), (0,)), ((), ()))


def mxu(left, right, dims):
    return lax.dot_general(left, right, dims, preferred_element_type=F32)


def turn(vectors, cosine, sine_part):
    half = HEAD_DIM // 2
    first, second = vectors[:half], vectors[half:]
    return jnp.concatenate(
        [first * cosine - second * sine_part, second * cosine + first * sine_part], 0
    )


def fill_bias(bias, key_place, query_place, query_start):
    keys = bias.shape[0]
    block = 256
    for i in range(keys // block):
        at = key_place[i * block : (i + 1) * block, :]
        fits = (at <= query_place[...]) & (at >= query_start[...])
        bias[i * block : (i + 1) * block, :] = jnp.where(fits, 0.0, NEGATIVE)


def each_pair(one, count, keys):
    def step(pair, unused):
        one(pair * 2, pl.ds(pl.multiple_of(pair * 2 * HEAD_DIM, 2 * HEAD_DIM), 2 * HEAD_DIM))
        return unused

    if keys > 2048:
        lax.fori_loop(0, count // 2, step, 0)
    else:
        for pair in range(count // 2):
            step(pair, 0)


def rows_of(head):
    return pl.ds(pl.multiple_of(head * HEAD_DIM, HEAD_DIM), HEAD_DIM)


def attend_kernel(
    normed, near, far_0, far_1, far_2, far_3, keyvalue, cosine, sine_part, key_place,
    query_place, query_start, query_rot, attended, attended_low, lse, bias, value_t,
):
    fill_bias(bias, key_place, query_place, query_start)
    value_t[...] = keyvalue[:, HEAD_DIM:].T
    parts = [(0, near)]
    for part in (far_0, far_1, far_2, far_3):
        parts.append((parts[-1][0] + parts[-1][1].shape[0], part))

    def one(first, columns):
        total = sum(
            mxu(normed[:, at : at + part.shape[0]], part[:, columns], NN) for at, part in parts
        )
        turned = total.T
        for i in range(2):
            at = rows_of(first + i)
            query = turn(
                turned[i * HEAD_DIM : (i + 1) * HEAD_DIM], cosine[...], sine_part[...]
            ).astype(BF16)
            query_rot[at, :] = query
            scores = mxu(keyvalue[:, :HEAD_DIM], query, NN) * (SCALE * LOG2E) + bias[...]
            top = jnp.max(scores, axis=0, keepdims=True)
            weights = jnp.exp2(scores - top)
            total = jnp.sum(weights, axis=0, keepdims=True)
            result = mxu(value_t[...], weights.astype(BF16), NN) / total
            attended[at, :] = result
            attended_low[at, :] = result.astype(BF16)
            lse[pl.ds(first + i, 1), :] = top + jnp.log2(total)

    each_pair(one, query_rot.shape[0] // HEAD_DIM, keyvalue.shape[0])


def attend_back_kernel(
    query_rot, keyvalue, grad_hidden, output_weight, attended, lse, cosine, sine_part,
    key_place, query_place, query_start, query_grad, kv_grad, bias, key_t,
):
    fill_bias(bias, key_place, query_place, query_start)
    kv_grad[...] = jnp.zeros_like(kv_grad)
    key_t[...] = keyvalue[:, :HEAD_DIM].T

    def one(first, columns):
        turned = mxu(grad_hidden[...], output_weight[:, columns], NN).T.astype(BF16)
        for i in range(2):
            at = rows_of(first + i)
            query = query_rot[at, :]
            grad_head = turned[i * HEAD_DIM : (i + 1) * HEAD_DIM]
            delta = jnp.sum(grad_head.astype(F32) * attended[at, :], axis=0, keepdims=True)
            scores = mxu(keyvalue[:, :HEAD_DIM], query, NN) * (SCALE * LOG2E) + bias[...]
            probs = jnp.exp2(scores - lse[pl.ds(first + i, 1), :])
            grad_probs = mxu(keyvalue[:, HEAD_DIM:], grad_head, NN)
            grad_scores = (probs * (grad_probs - delta)).astype(BF16)
            kv_grad[:, :HEAD_DIM] += mxu(grad_scores, query, NT) * SCALE
            kv_grad[:, HEAD_DIM:] += mxu(probs.astype(BF16), grad_head, NT)
            grad_query = mxu(key_t[...], grad_scores, NN) * SCALE
            query_grad[at, :] = turn(grad_query, cosine[...], -sine_part[...]).astype(BF16)

    each_pair(one, query_rot.shape[0] // HEAD_DIM, keyvalue.shape[0])


def columns_of(width):
    return width // 256, width % 256


def each_block(width, body):
    full, rest = columns_of(width)

    def step(i, unused):
        body(pl.ds(pl.multiple_of(i * 256, 256), 256))
        return unused

    lax.fori_loop(0, full, step, 0)
    if rest:
        body(pl.ds(full * 256, rest))


def load_pieces(pieces, held, slot, sems):
    copies = [
        pltpu.make_async_copy(piece, held.at[slot, p], sems.at[slot, p])
        for p, piece in enumerate(pieces)
    ]
    for copy in copies:
        copy.start()

    def wait():
        for copy in copies:
            copy.wait()

    return wait


def gate_up_kernel(normed, *refs):
    gate_sum, up_sum, held, sems = refs[16:]
    waits = [load_pieces(refs[8 * i : 8 * i + 8], held, i, sems) for i in range(2)]
    width, part = normed.shape[1], gate_sum.shape[1]
    for slot, result in enumerate((gate_sum, up_sum)):
        waits[slot]()

        def step(at):
            result[:, at] = mxu(
                normed[...], held[slot, :, :, :, at].reshape(width, at.size), NN
            )

        each_block(part, step)


def feed_kernel(grad, gate_sum, up_sum, *refs):
    mixed, grad_gate, grad_up, grad_two, held, sems = refs[24:]
    waits = [load_pieces(refs[8 * i : 8 * i + 8], held, i, sems) for i in range(3)]
    width, part = grad.shape[1], mixed.shape[1]
    waits[0]()

    def down_step(at):
        grad_mixed = mxu(grad[...], held[0, :, :, :, at].reshape(width, at.size), NN)
        gate, up = gate_sum[:, at], up_sum[:, at]
        sigmoid_gate = jax.nn.sigmoid(gate)
        silu_gate = gate * sigmoid_gate
        mixed[:, at] = (silu_gate * up).astype(BF16)
        grad_up[:, at] = (grad_mixed * silu_gate).astype(BF16)
        grad_gate[:, at] = (
            grad_mixed * up * sigmoid_gate * (1.0 + gate * (1.0 - sigmoid_gate))
        ).astype(BF16)

    each_block(part, down_step)
    waits[1]()
    waits[2]()

    def two_step(p, unused):
        at = pl.ds(pl.multiple_of(p * (width // 8), width // 8), width // 8)
        grad_two[:, at] = (
            mxu(grad_gate[...], held[1, p].reshape(width // 8, part), NT)
            + mxu(grad_up[...], held[2, p].reshape(width // 8, part), NT)
        ).astype(BF16)
        return unused

    lax.fori_loop(0, 8, two_step, 0)


def outer_kernel(left, *refs):
    count = len(refs) // 3
    rights, results = refs[:count], refs[count:]
    rows = left.shape[1] // 8

    def step(p, unused):
        to = pl.ds(pl.multiple_of(p * rows, rows), rows)
        for part in range(2):
            first = 4 * (1 - part)
            at = pl.ds(pl.multiple_of((first + p) * rows, rows), rows)
            turned = left[:, at].T
            for i, right in enumerate(rights):
                result = results[2 * i + part]
                result[to, :] = mxu(turned, right[...], NN).astype(result.dtype)
        return unused

    lax.fori_loop(0, 4, step, 0)


def outer_all_kernel(order, left, *refs):
    *rights, result = refs
    rows = left.shape[1] // 8

    def step(p, unused):
        at = pl.ds(pl.multiple_of(p * rows, rows), rows)
        turned = left[:, at].T
        for i, right in enumerate(rights):
            result[order[p], i] = mxu(turned, right[...], NN).astype(result.dtype)
        return unused

    lax.fori_loop(0, 8, step, 0)


def feed_out_kernel(mixed, *refs):
    feed, held, sems = refs[8:]
    load_pieces(refs[:8], held, 0, sems)()
    width, part = feed.shape[1], mixed.shape[1]

    def feed_step(p, unused):
        at = pl.ds(pl.multiple_of(p * (width // 8), width // 8), width // 8)
        feed[:, at] = mxu(
            mixed[...], held[0, p].reshape(width // 8, part), NT
        ).astype(BF16)
        return unused

    lax.fori_loop(0, 8, feed_step, 0)


def split_kernel(*refs):
    result = refs[-1]
    for i, matrix in enumerate(refs[:-1]):
        result[0, i] = matrix[...]


def split(*matrices):
    rows, columns = matrices[0].shape
    count, part = len(matrices), columns // 4
    return pl.pallas_call(
        split_kernel,
        out_shape=jax.ShapeDtypeStruct((4, count, rows, part), matrices[0].dtype),
        grid=(4,),
        in_specs=[pl.BlockSpec((rows, part), lambda i: (0, i))] * count,
        out_specs=pl.BlockSpec((1, count, rows, part), lambda i: (i, 0, 0, 0)),
        cost_estimate=NO_COST,
    )(*matrices)


def merge_kernel(parts, result):
    result[...] = parts[0].astype(F32)


def merge(parts):
    _, rows, part = parts.shape
    return pl.pallas_call(
        merge_kernel,
        out_shape=jax.ShapeDtypeStruct((rows, 4 * part), F32),
        grid=(4,),
        in_specs=[pl.BlockSpec((1, rows, part), lambda i: (i, 0, 0))],
        out_specs=pl.BlockSpec((rows, part), lambda i: (0, i)),
        cost_estimate=NO_COST,
    )(parts)


NO_COST = pl.CostEstimate(flops=1, bytes_accessed=1, transcendentals=0)


def local_call(kernel, outs, scratch, *args, far=0, scalars=0):
    near = [pl.BlockSpec(memory_space=pltpu.SMEM)] * scalars
    near = near + [pl.BlockSpec(memory_space=pltpu.VMEM)] * (len(args) - far - scalars)
    return pl.pallas_call(
        kernel,
        out_shape=outs,
        in_specs=near + [pl.BlockSpec(memory_space=pl.ANY)] * far,
        out_specs=[pl.BlockSpec(memory_space=pltpu.VMEM)] * len(outs),
        scratch_shapes=scratch,
        compiler_params=pltpu.CompilerParams(vmem_limit_bytes=56 << 20),
        cost_estimate=NO_COST,
    )(*args)


def on_device(
    block_input,
    attention_gain,
    query_weight,
    keyvalue_weight,
    output_weight,
    feedforward_gain,
    gate_weight,
    up_weight,
    down_weight,
    document_lengths,
    piece_order,
    output_grad,
    shared_grad,
):
    y, h, l, m, x, c = (lax.axis_index(a) for a in AXES)
    M = lax.axis_size("m")
    tokens, width = block_input.shape[1:]
    rows = query_weight.shape[0]
    query_width = query_weight.shape[1]
    half_width = query_width // 2
    heads = half_width // HEAD_DIM
    hidden_units = gate_weight.shape[1]
    part = hidden_units // 4
    piece_len = tokens // 2

    def inward(value):
        value = value.reshape(tokens, 2, 2, 2, M, 2, 2, rows)
        value = value.transpose(0, 6, 1, 2, 4, 3, 5, 7)
        value = jnp.where(c == 0, value, value[:, ::-1])
        value = jnp.where(y == 0, value, value[:, :, ::-1])
        value = jnp.where(h == 0, value, value[:, :, :, ::-1])
        return value.reshape(tokens, width)

    def outward(value):
        value = value.reshape(tokens, 2, 2, 2, M, 2, 2, rows)
        value = jnp.where(h == 0, value, value[:, :, :, ::-1])
        value = jnp.where(y == 0, value, value[:, :, ::-1])
        value = jnp.where(c == 0, value, value[:, ::-1])
        return value.transpose(0, 2, 3, 5, 4, 6, 1, 7).reshape(tokens, width)

    finish = jnp.cumsum(document_lengths[0])
    starts = finish - document_lengths[0]

    def places(slots):
        order = piece_order[(slots[:, None] * 2 + jnp.arange(2)[None, :]).reshape(-1)]
        return (
            order[:, None] * piece_len + jnp.arange(piece_len, dtype=jnp.int32)[None, :]
        ).reshape(-1)

    def slot(h_at, l_at, m_at, x_at, c_at):
        return (((h_at * 2 + l_at) * M + m_at) * 2 + x_at) * 2 + c_at

    position = places(jnp.stack([slot(h, l, m, x, c), slot(h, l, m, 1 - x, c)]))
    begins = jnp.max(
        jnp.where(starts[None, :] <= position[:, None], starts[None, :], 0), axis=1
    )
    key_position = places(
        jnp.stack(
            [
                slot(h ^ i, l ^ j, m_at, x ^ k, c ^ n)
                for n in range(2)
                for k in range(2)
                for j in range(2)
                for m_at in range(M)
                for i in range(2)
            ]
        )
    )[:, None]
    query_place, query_start = position[None, :], begins[None, :]
    cosine, sine_part = angles(position - begins)

    gains = jnp.stack([attention_gain, feedforward_gain])
    gains = jnp.pad(gains, ((0, 14), (0, 2 * HEAD_DIM - rows)))
    small = jnp.concatenate([keyvalue_weight, gains])

    def halves(weight):
        parts = weight.reshape(rows, 2, half_width).transpose(1, 0, 2)
        return pick(parts, x), pick(parts, 1 - x)

    query_mine, query_sent = halves(query_weight)
    output_mine, output_sent = halves(output_weight)

    small_x, query_x, output_x = sync(
        swap(small, "x"), swap(query_sent, "x"), swap(output_sent, "x")
    )
    small = pair(small, small_x, x)
    query_part, output_part = pair(query_mine, query_x, x), pair(output_mine, output_x, x)
    input_mine, small, gate_weight, up_weight, down_weight = sync(
        inward(block_input[0]), small, gate_weight, up_weight, down_weight
    )
    feed_parts = split(gate_weight, up_weight, down_weight)
    small_l, query_l, output_l, input_other = sync(
        swap(small, "l"), swap(query_part, "l"), swap(output_part, "l"), swap(input_mine, "x")
    )
    small = gather_m(pair(small, small_l, l), 0)
    query_part = gather_m(pair(query_part, query_l, l), 0)
    output_part = gather_m(pair(output_part, output_l, l), 0)
    small, query_part, feed_parts = sync(small, query_part, feed_parts)
    query_h = swap(query_part, "h")
    small_h = sync(swap(small, "h"))[0]
    small, feed_parts = sync(jnp.stack([small, small_h]), feed_parts)
    feed = gather_m(lax.all_to_all(feed_parts, ("l", "x"), 0, 0), 0)
    feed = feed.reshape(M * 4, 3, rows, part)
    small_y = sync(swap(small, "y"))[0]
    small = jnp.stack([small, small_y]).reshape(4, M * 4, rows + 16, 2 * HEAD_DIM)
    small_c, input_other, query_h = sync(swap_core(small), input_other, query_h)
    small = jnp.stack([small, small_c])
    small = small.reshape(width // rows, rows + 16, 2 * HEAD_DIM)
    keyvalue_full = small[:, :rows].reshape(width, 2 * HEAD_DIM)
    gain_one = small[:, rows, :rows].reshape(1, width).astype(F32)
    gain_two = small[:, rows + 1, :rows].reshape(1, width).astype(F32)
    def normalize(value):
        value = value.astype(F32)
        scale = lax.rsqrt(jnp.mean(value * value, axis=-1, keepdims=True) + EPSILON)
        normed = value * scale
        return value, scale, normed, low(normed * gain_one)

    inputs, scale_one, normed_one, normed_mine_low = normalize(input_mine)
    keyvalue_sum = dot(normed_mine_low, keyvalue_full)
    shared_mine = low(
        jnp.concatenate(
            [
                rotate(keyvalue_sum[:, :HEAD_DIM], cosine[:tokens], sine_part[:tokens]),
                keyvalue_sum[:, HEAD_DIM:],
            ],
            -1,
        )
    )
    query_part, keyvalue_sum, key_position, query_place, query_start, cosine_t, sine_t = sync(
        jnp.stack([query_part, query_h]),
        keyvalue_sum,
        key_position,
        query_place,
        query_start,
        cosine.T,
        sine_part.T,
    )
    query_y = swap(query_part, "y")
    shared_h, input_other = sync(swap(shared_mine, "h"), input_other)
    gathered = gather_m(jnp.stack([shared_mine, shared_h]), 0)
    gathered, input_other, output_part = sync(gathered, input_other, output_part)
    output_h = swap(output_part, "h")
    normed_one_low = jnp.concatenate([normed_mine_low, normalize(input_other)[3]])
    shared_l, normed_one_low, feed = sync(swap(gathered, "l"), normed_one_low, feed)
    gate, up, down, gathered = sync(
        *(feed[:, i] for i in range(3)), jnp.stack([gathered, shared_l])
    )
    shared_x, query_y, output_h = sync(swap(gathered, "x"), query_y, output_h)
    gathered = jnp.stack([gathered, shared_x]).reshape(4, -1, 2 * HEAD_DIM)
    query_part = jnp.stack([query_part, query_y]).reshape(-1, half_width)
    query_part, gathered = sync(query_part, gathered)
    query_c = core_parts(query_part)
    shared_c, *query_c = sync(swap_core(gathered), *query_c)
    output_part = jnp.stack([output_part, output_h])
    output_part, gate, shared_c = sync(output_part, gate, shared_c)
    output_y = swap(output_part, "y")
    gate_h = swap(gate, "h")
    gate_sent, query_place = sync(gate, query_place, *query_c)[:2]
    gate_y = swap(gate_sent, "y")
    gathered = jnp.stack([gathered, shared_c]).reshape(-1, 2 * HEAD_DIM)
    stream_len = gathered.shape[0]
    grad_mine = inward(output_grad[0])
    wide = (half_width, 2 * tokens)
    places_used = (key_position, query_place, query_start)
    query_rot, attended, attended_low, lse = local_call(
        attend_kernel,
        [
            jax.ShapeDtypeStruct(wide, BF16),
            jax.ShapeDtypeStruct(wide, F32),
            jax.ShapeDtypeStruct(wide, BF16),
            jax.ShapeDtypeStruct((heads, 2 * tokens), F32),
        ],
        [
            pltpu.VMEM((stream_len, 2 * tokens), F32),
            pltpu.VMEM((HEAD_DIM, stream_len), BF16),
        ],
        normed_one_low, query_part, *query_c, gathered, cosine_t, sine_t, *places_used,
    )
    attended_low, output_y, output_part, gate_h, gate_y = sync(
        attended_low, output_y, output_part, gate_h, gate_y
    )
    output_part = jnp.stack([output_part, output_y]).reshape(-1, half_width)
    output_c = swap_core(output_part)
    up_sent, attended_low = sync(up, attended_low)
    up_h, up_y = swap(up_sent, "h"), swap(up_sent, "y")
    output_part, output_c, attended_low = sync(output_part, output_c, attended_low)
    output_full = jnp.concatenate([output_part, output_c])
    branch = lax.dot_general(
        attended_low, output_full, (((0,), (1,)), ((), ())), preferred_element_type=F32
    )
    branch, gate_h = sync(branch, gate_h)
    gate_far = swap(gate_h, "y")
    branch_x, up_h, up_y, gate_far, grad_mine = sync(
        swap(low(branch[tokens:]), "x"), up_h, up_y, gate_far, grad_mine
    )
    hidden = inputs + (branch[:tokens] + branch_x.astype(F32))

    down_sent, branch_x = sync(down, branch_x)
    down_h, up_far, down_y = swap(down_sent, "h"), swap(up_h, "y"), swap(down_sent, "y")
    scale_two = lax.rsqrt(jnp.mean(hidden * hidden, axis=-1, keepdims=True) + EPSILON)
    normed_two = hidden * scale_two
    normed_two_low = low(normed_two * gain_two)
    normed_two_low = gather_group(normed_two_low).reshape(-1, width)
    up_far, *sent = sync(up_far, gate, gate_h, gate_y, gate_far, up, up_h, up_y)
    near_c = [swap(piece, "c") for piece in sent]
    normed_two_low, down_h, down_y, *near_c = sync(normed_two_low, down_h, down_y, *near_c)
    down_far = swap(down_h, "y")
    gate_c = near_c[:4]
    up_sent, grad_sent = sync(up_far, grad_mine, normed_two_low)[:2]
    late_c = [swap(up_sent, "c")]
    up_c = near_c[4:] + late_c
    grad_low = gather_group(grad_sent).reshape(-1, width)
    gate_all = [gate, gate_h, gate_y, gate_far, *gate_c]
    up_all = [up, up_h, up_y, up_far, *up_c]
    group = 4 * tokens
    units = jax.ShapeDtypeStruct((group, part), BF16)
    unit_sums = jax.ShapeDtypeStruct((group, part), F32)
    features = jax.ShapeDtypeStruct((group, width), BF16)

    def held(count):
        return [
            pltpu.VMEM((count, 8, M * 4, rows, part), BF16),
            pltpu.SemaphoreType.DMA((count, 8)),
        ]

    down_c = [swap(piece, "c") for piece in (down, down_h, down_y)]
    gate_sum, up_sum = local_call(
        gate_up_kernel, [unit_sums] * 2, held(2), normed_two_low, *gate_all, *up_all, far=16
    )
    down_far, gate_sum, *down_c = sync(down_far, gate_sum, *down_c)
    down_all = [down, down_h, down_y, down_far, *down_c, swap(down_far, "c")]
    order = jnp.stack(
        [
            ((y ^ j) * 2 + (h ^ k)) * 2 + (c ^ i)
            for i in range(2)
            for j in range(2)
            for k in range(2)
        ]
    )
    mixed_low, grad_gate, grad_up, grad_two = local_call(
        feed_kernel,
        [units, units, units, features],
        held(3),
        grad_low, gate_sum, up_sum, *down_all, *gate_all, *up_all,
        far=24,
    )

    half, block = width // 2, width // 8
    half_rows = jax.ShapeDtypeStruct((half, part), BF16)
    mixed_low, grad_gate, grad_up, grad_two = sync(mixed_low, grad_gate, grad_up, grad_two)
    grad_two = scatter_group(grad_two.reshape(4, tokens, width))
    both_grad = local_call(
        outer_all_kernel,
        [jax.ShapeDtypeStruct((8, 2, block, part), BF16)],
        [],
        order, normed_two_low, grad_gate, grad_up,
        scalars=1,
    )[0]
    mixed_low, both_grad = sync(mixed_low, both_grad)
    both_grad = lax.psum_scatter(both_grad, ("y", "h", "c"), scatter_dimension=0)
    down_far_half, down_near = local_call(
        outer_kernel, [half_rows] * 2, [], grad_low, mixed_low
    )
    mixed_low, down_far_half = sync(mixed_low, down_far_half)
    down_got = swap(down_far_half, "c")
    def quarter(i, *more):
        at = slice(i * block, (i + 1) * block)
        total = down_near[at].astype(F32) + down_got[at].astype(F32)
        for other in more:
            total = total + other.astype(F32)
        return low(total)

    grad_two, down_got = sync(grad_two, down_got)
    across = (((0,), (1,)), ((), ()))
    grad_hidden = grad_mine.astype(F32) + norm_back(grad_two * gain_two, normed_two, scale_two)
    grad_hidden_low, grad_two = sync(low(grad_hidden), grad_two)
    hidden_x = swap(grad_hidden_low, "x")
    down_y3, down_y2 = swap(quarter(3), "y"), swap(quarter(2), "y")
    mixed_low = sync(mixed_low, grad_hidden_low)[0]
    feed_out = local_call(
        feed_out_kernel,
        [features],
        held(1),
        mixed_low, *down_all,
        far=8,
    )[0]
    hidden_x, feed_out = sync(hidden_x, feed_out)
    feed_out = scatter_group(feed_out.reshape(4, tokens, width))
    grad_hidden_low = jnp.concatenate([grad_hidden_low, hidden_x])
    query_grad_low, kv_grad = local_call(
        attend_back_kernel,
        [
            jax.ShapeDtypeStruct(wide, BF16),
            jax.ShapeDtypeStruct((stream_len, 2 * HEAD_DIM), F32),
        ],
        [
            pltpu.VMEM((stream_len, 2 * tokens), F32),
            pltpu.VMEM((HEAD_DIM, stream_len), BF16),
        ],
        query_rot, gathered, grad_hidden_low, output_full, attended, lse, cosine_t, sine_t,
        *places_used,
    )
    query_grad_low, kv_grad, grad_hidden_low = sync(query_grad_low, kv_grad, grad_hidden_low)

    def fold_l(total):
        total = total.reshape(2, 2, M, 2, 2, rows, -1)
        return pick(total, l, 3), swap(low(pick(total, 1 - l, 3)), "l")

    def give_x(total, got):
        total = total + got.astype(F32)
        return pick(total, x, 3), swap(low(pick(total, 1 - x, 3)), "x")

    def take_x(total, got):
        got = got.astype(F32)
        both = pair(total[..., :half_width], got[..., :half_width], x, 4)
        both = both.reshape(2, 2, M, rows, query_width)
        return jnp.concatenate([both, (total + got)[..., half_width:]], -1)

    def next_fold(total, axis):
        return total[0], swap(low(total[1]), axis)

    kv_half = kv_grad.shape[0] // 2
    kv_sent = low(kv_grad[kv_half:]).reshape(4, -1, 2 * HEAD_DIM)
    output_term = low(
        lax.dot_general(grad_hidden_low, attended_low, across, preferred_element_type=F32)
    )
    kv_got, query_grad_low, output_term = sync(
        swap_core(kv_sent), query_grad_low, output_term
    )
    output_got = swap_core(output_term[half:])
    kv_grad = kv_grad[:kv_half].reshape(4, M, 2, tokens, 2 * HEAD_DIM)
    kv_grad = kv_grad + kv_got.astype(F32).reshape(kv_grad.shape)
    kv_got = swap(low(kv_grad[2:]), "x")
    query_term = low(
        lax.dot_general(normed_one_low, query_grad_low, across, preferred_element_type=F32)
    )
    kv_got, query_term, output_got = sync(kv_got, query_term, output_got)
    kv_grad = kv_grad[:2] + kv_got.astype(F32)
    kv_got = swap(low(kv_grad[1]), "l")
    query_full = jnp.concatenate([query_part, *query_c])
    grad_one = lax.dot_general(
        query_grad_low, query_full, (((0,), (1,)), ((), ())), preferred_element_type=F32
    )
    kv_got, grad_one, feed_out = sync(kv_got, grad_one, feed_out)
    grad_one_x = swap(low(grad_one[tokens:]), "x")
    output_total, output_got = fold_l(
        output_term[:half].astype(F32) + output_got.astype(F32)
    )
    kv_grad = kv_grad[0] + kv_got.astype(F32)
    kv_got, grad_one_x, down_y3 = sync(swap(low(kv_grad[:, 1]), "h"), grad_one_x, down_y3)
    down_h1 = swap(quarter(1, down_y3), "h")
    kv_mine = scatter_m(kv_grad[:, 0] + kv_got.astype(F32), 0) + shared_grad[0].astype(F32)
    keyvalue_grad_low = low(
        jnp.concatenate(
            [
                rotate(kv_mine[:, :HEAD_DIM], cosine[:tokens], -sine_part[:tokens]),
                kv_mine[:, HEAD_DIM:],
            ],
            -1,
        )
    )
    grad_one = grad_one[:tokens] + grad_one_x.astype(F32)
    grad_one = grad_one + contract_last(keyvalue_grad_low, keyvalue_full)
    gain_one_grad = jnp.sum(grad_one * normed_one, axis=0)
    gain_two_grad = jnp.sum(grad_two * normed_two, axis=0)
    small_grad = contract_first(normed_mine_low, keyvalue_grad_low)
    small_gains = jnp.stack([gain_one_grad, gain_two_grad], -1)
    small_gains = jnp.pad(small_gains, ((0, 0), (0, HEAD_DIM - 2)))
    query_total = jnp.concatenate([query_term, low(small_grad), low(small_gains)], -1)
    query_got = swap_core(query_total[half:])
    query_got, output_got, query_total = sync(query_got, output_got, query_total)
    query_total, query_got = fold_l(query_total[:half].astype(F32) + query_got.astype(F32))
    output_total, output_got = give_x(output_total, output_got)
    input_grad = outward(
        grad_hidden + norm_back(grad_one * gain_one, normed_one, scale_one)
    )[None]
    block_output = outward(low(hidden + feed_out))[None]
    output_got, down_y2 = sync(output_got, down_y2)
    output_total, output_got = next_fold(take_x(output_total, output_got), "y")
    query_got, output_got = sync(query_got, output_got)
    query_total, query_got = give_x(query_total, query_got)
    output_total, output_got = next_fold(output_total + output_got.astype(F32), "h")
    query_got, output_got, down_h1, both_grad = sync(query_got, output_got, down_h1, both_grad)
    query_total, query_got = next_fold(take_x(query_total, query_got), "y")
    output_weight_grad = scatter_m(output_total + output_got.astype(F32), 0)
    def finish_feed(own):
        own = low(scatter_m(own, 0))
        got = lax.all_to_all(own, ("l", "x"), 0, 0)
        return [merge(got[:, i]) for i in range(own.shape[1])]

    both_grad = both_grad.reshape(2, M, 4, rows, part).transpose(1, 2, 0, 3, 4)
    gate_weight_grad, up_weight_grad = finish_feed(both_grad)
    query_total, query_got = next_fold(query_total + query_got.astype(F32), "h")
    down_own = sync(quarter(0, down_h1, down_y2), gate_weight_grad)[0]
    (down_weight_grad,) = finish_feed(down_own.reshape(M, 4, 1, rows, part))
    query_total = scatter_m(query_total + query_got.astype(F32), 0)
    query_weight_grad = query_total[:, :query_width]
    keyvalue_weight_grad = query_total[:, query_width : query_width + 2 * HEAD_DIM]
    gain_one_mine = query_total[:, query_width + 2 * HEAD_DIM]
    gain_two_mine = query_total[:, query_width + 2 * HEAD_DIM + 1]
    return (
        block_output,
        shared_mine[None],
        input_grad,
        gain_one_mine,
        query_weight_grad,
        keyvalue_weight_grad,
        output_weight_grad,
        gain_two_mine,
        gate_weight_grad,
        up_weight_grad,
        down_weight_grad,
    )


def solution(mesh):
    streams, seq = mesh.shape["dp"], mesh.shape["seq"]
    fine = Mesh(mesh.devices.reshape(streams, 2, 2, seq // 16, 2, 2), tuple(AXES))
    stream = P("y", tuple(AXES[1:]), None)
    vector, matrix = P(tuple(AXES)), P(tuple(AXES), None)
    return jax.shard_map(
        on_device,
        mesh=fine,
        in_specs=(
            stream,
            vector,
            matrix,
            matrix,
            matrix,
            vector,
            matrix,
            matrix,
            matrix,
            P("y", None),
            P(),
            stream,
            stream,
        ),
        out_specs=(
            stream,
            stream,
            stream,
            vector,
            matrix,
            matrix,
            matrix,
            vector,
            matrix,
            matrix,
            matrix,
        ),
        check_vma=False,
    )
```

```python
import functools
import math

import jax
import jax.numpy as jnp
from jax import lax
from jax.experimental import pallas as pl
from jax.experimental.pallas import tpu as pltpu
from jax.sharding import Mesh
from jax.sharding import PartitionSpec as P

HEAD_DIM = 128
EPSILON = 1e-05
NEGATIVE = -1e30
AXES = "yhlmxc"
BF16 = jnp.bfloat16
F32 = jnp.float32


def angles(offset):
    half_dim = HEAD_DIM // 2
    frequency = jnp.exp(
        jnp.arange(half_dim, dtype=F32) * (-2.0 * math.log(10000.0) / HEAD_DIM)
    )
    phases = offset.astype(F32)[:, None] * frequency[None, :]
    return (jnp.cos(phases), jnp.sin(phases))


def rotate(vectors, cosine, sine_part):
    half_dim = vectors.shape[-1] // 2
    first, second = vectors[..., :half_dim], vectors[..., half_dim:]
    return jnp.concatenate(
        [first * cosine - second * sine_part, second * cosine + first * sine_part], -1
    )


def dot(left, right):
    return jnp.dot(left, right, preferred_element_type=F32)


def contract_last(left, right):
    return lax.dot_general(left, right, (((1,), (1,)), ((), ())), preferred_element_type=F32)


def contract_first(left, right):
    return lax.dot_general(left, right, (((0,), (0,)), ((), ())), preferred_element_type=F32)


def norm_back(grad_normed, normed, scale_rows):
    return scale_rows * (
        grad_normed - normed * jnp.mean(grad_normed * normed, axis=-1, keepdims=True)
    )


def swap(value, axis):
    return lax.ppermute(value, axis, [(0, 1), (1, 0)])


def swap_core(value):
    return jnp.concatenate(core_parts(value))


def core_parts(value):
    size = value.shape[0] // 4
    return [swap(value[i * size : (i + 1) * size], "c") for i in range(4)]


def low(value):
    return value.astype(BF16)


def sync(*values):
    return lax.optimization_barrier(values)


def pick(stacked, index, axis=0):
    return lax.dynamic_index_in_dim(stacked, index, axis, keepdims=False)


def pair(own, other, index, axis=0):
    return jnp.where(
        index == 0, jnp.stack([own, other], axis), jnp.stack([other, own], axis)
    )


def gather_m(value, axis):
    if lax.axis_size("m") > 1:
        return lax.all_gather(value, "m", axis=axis)
    return jnp.expand_dims(value, axis)


def scatter_m(value, axis):
    if lax.axis_size("m") > 1:
        return lax.psum_scatter(value, "m", scatter_dimension=axis)
    return lax.squeeze(value, (axis,))


def fold(total, axis):
    half = total.shape[0] // 2
    return total[:half].astype(F32) + swap(low(total[half:]), axis).astype(F32)


def four_of(value):
    return jnp.broadcast_to(value, (4, *value.shape))


def gather_group(copies):
    return lax.all_to_all(copies, ("l", "x"), 0, 0)


def scatter_group(value):
    return jnp.sum(lax.all_to_all(low(value), ("l", "x"), 0, 0).astype(F32), axis=0)


LOG2E = math.log2(math.e)
SCALE = 1.0 / math.sqrt(HEAD_DIM)
NT = (((1,), (1,)), ((), ()))
NN = (((1,), (0,)), ((), ()))


def mxu(left, right, dims):
    return lax.dot_general(left, right, dims, preferred_element_type=F32)


def turn(vectors, cosine, sine_part):
    half = HEAD_DIM // 2
    first, second = vectors[:half], vectors[half:]
    return jnp.concatenate(
        [first * cosine - second * sine_part, second * cosine + first * sine_part], 0
    )


def fill_bias(bias, key_place, query_place, query_start):
    keys = bias.shape[0]
    block = 256
    for i in range(keys // block):
        at = key_place[i * block : (i + 1) * block, :]
        fits = (at <= query_place[...]) & (at >= query_start[...])
        bias[i * block : (i + 1) * block, :] = jnp.where(fits, 0.0, NEGATIVE)


def each_pair(one, count, keys):
    def step(pair, unused):
        one(pair * 2, pl.ds(pl.multiple_of(pair * 2 * HEAD_DIM, 2 * HEAD_DIM), 2 * HEAD_DIM))
        return unused

    if keys > 2048:
        lax.fori_loop(0, count // 2, step, 0)
    else:
        for pair in range(count // 2):
            step(pair, 0)


def rows_of(head):
    return pl.ds(pl.multiple_of(head * HEAD_DIM, HEAD_DIM), HEAD_DIM)


def attend_kernel(
    normed, near, far_0, far_1, far_2, far_3, keyvalue, cosine, sine_part, key_place,
    query_place, query_start, query_rot, attended, attended_low, lse, bias, value_t,
):
    fill_bias(bias, key_place, query_place, query_start)
    value_t[...] = keyvalue[:, HEAD_DIM:].T
    parts = [(0, near)]
    for part in (far_0, far_1, far_2, far_3):
        parts.append((parts[-1][0] + parts[-1][1].shape[0], part))

    def one(first, columns):
        total = sum(
            mxu(normed[:, at : at + part.shape[0]], part[:, columns], NN) for at, part in parts
        )
        turned = total.T
        for i in range(2):
            at = rows_of(first + i)
            query = turn(
                turned[i * HEAD_DIM : (i + 1) * HEAD_DIM], cosine[...], sine_part[...]
            ).astype(BF16)
            query_rot[at, :] = query
            scores = mxu(keyvalue[:, :HEAD_DIM], query, NN) * (SCALE * LOG2E) + bias[...]
            top = jnp.max(scores, axis=0, keepdims=True)
            weights = jnp.exp2(scores - top)
            total = jnp.sum(weights, axis=0, keepdims=True)
            result = mxu(value_t[...], weights.astype(BF16), NN) / total
            attended[at, :] = result
            attended_low[at, :] = result.astype(BF16)
            lse[pl.ds(first + i, 1), :] = top + jnp.log2(total)

    each_pair(one, query_rot.shape[0] // HEAD_DIM, keyvalue.shape[0])


def attend_back_kernel(
    query_rot, keyvalue, grad_hidden, output_weight, attended, lse, cosine, sine_part,
    key_place, query_place, query_start, query_grad, kv_grad, bias, key_t,
):
    fill_bias(bias, key_place, query_place, query_start)
    kv_grad[...] = jnp.zeros_like(kv_grad)
    key_t[...] = keyvalue[:, :HEAD_DIM].T

    def one(first, columns):
        turned = mxu(grad_hidden[...], output_weight[:, columns], NN).T.astype(BF16)
        for i in range(2):
            at = rows_of(first + i)
            query = query_rot[at, :]
            grad_head = turned[i * HEAD_DIM : (i + 1) * HEAD_DIM]
            delta = jnp.sum(grad_head.astype(F32) * attended[at, :], axis=0, keepdims=True)
            scores = mxu(keyvalue[:, :HEAD_DIM], query, NN) * (SCALE * LOG2E) + bias[...]
            probs = jnp.exp2(scores - lse[pl.ds(first + i, 1), :])
            grad_probs = mxu(keyvalue[:, HEAD_DIM:], grad_head, NN)
            grad_scores = (probs * (grad_probs - delta)).astype(BF16)
            kv_grad[:, :HEAD_DIM] += mxu(grad_scores, query, NT) * SCALE
            kv_grad[:, HEAD_DIM:] += mxu(probs.astype(BF16), grad_head, NT)
            grad_query = mxu(key_t[...], grad_scores, NN) * SCALE
            query_grad[at, :] = turn(grad_query, cosine[...], -sine_part[...]).astype(BF16)

    each_pair(one, query_rot.shape[0] // HEAD_DIM, keyvalue.shape[0])


def columns_of(width):
    return width // 256, width % 256


def each_block(width, body):
    full, rest = columns_of(width)

    def step(i, unused):
        body(pl.ds(pl.multiple_of(i * 256, 256), 256))
        return unused

    lax.fori_loop(0, full, step, 0)
    if rest:
        body(pl.ds(full * 256, rest))


def load_pieces(pieces, held, slot, sems):
    copies = [
        pltpu.make_async_copy(piece, held.at[slot, p], sems.at[slot, p])
        for p, piece in enumerate(pieces)
    ]
    for copy in copies:
        copy.start()

    def wait():
        for copy in copies:
            copy.wait()

    return wait


def gate_up_kernel(normed, *refs):
    gate_sum, up_sum, held, sems = refs[16:]
    waits = [load_pieces(refs[8 * i : 8 * i + 8], held, i, sems) for i in range(2)]
    width, part = normed.shape[1], gate_sum.shape[1]
    for slot, result in enumerate((gate_sum, up_sum)):
        waits[slot]()

        def step(at):
            result[:, at] = mxu(
                normed[...], held[slot, :, :, :, at].reshape(width, at.size), NN
            )

        each_block(part, step)


def feed_kernel(grad, gate_sum, up_sum, *refs):
    mixed, grad_gate, grad_up, grad_two, held, sems = refs[24:]
    waits = [load_pieces(refs[8 * i : 8 * i + 8], held, i, sems) for i in range(3)]
    width, part = grad.shape[1], mixed.shape[1]
    waits[0]()

    def down_step(at):
        grad_mixed = mxu(grad[...], held[0, :, :, :, at].reshape(width, at.size), NN)
        gate, up = gate_sum[:, at], up_sum[:, at]
        sigmoid_gate = jax.nn.sigmoid(gate)
        silu_gate = gate * sigmoid_gate
        mixed[:, at] = (silu_gate * up).astype(BF16)
        grad_up[:, at] = (grad_mixed * silu_gate).astype(BF16)
        grad_gate[:, at] = (
            grad_mixed * up * sigmoid_gate * (1.0 + gate * (1.0 - sigmoid_gate))
        ).astype(BF16)

    each_block(part, down_step)
    waits[1]()
    waits[2]()

    def two_step(p, unused):
        at = pl.ds(pl.multiple_of(p * (width // 8), width // 8), width // 8)
        grad_two[:, at] = (
            mxu(grad_gate[...], held[1, p].reshape(width // 8, part), NT)
            + mxu(grad_up[...], held[2, p].reshape(width // 8, part), NT)
        ).astype(BF16)
        return unused

    lax.fori_loop(0, 8, two_step, 0)


def outer_kernel(left, *refs):
    count = len(refs) // 3
    rights, results = refs[:count], refs[count:]
    rows = left.shape[1] // 8

    def step(p, unused):
        to = pl.ds(pl.multiple_of(p * rows, rows), rows)
        for part in range(2):
            first = 4 * (1 - part)
            at = pl.ds(pl.multiple_of((first + p) * rows, rows), rows)
            turned = left[:, at].T
            for i, right in enumerate(rights):
                result = results[2 * i + part]
                result[to, :] = mxu(turned, right[...], NN).astype(result.dtype)
        return unused

    lax.fori_loop(0, 4, step, 0)


def outer_all_kernel(order, left, *refs):
    *rights, result = refs
    rows = left.shape[1] // 8

    def step(p, unused):
        at = pl.ds(pl.multiple_of(p * rows, rows), rows)
        turned = left[:, at].T
        for i, right in enumerate(rights):
            result[order[p], i] = mxu(turned, right[...], NN).astype(result.dtype)
        return unused

    lax.fori_loop(0, 8, step, 0)


def feed_out_kernel(mixed, *refs):
    feed, held, sems = refs[8:]
    load_pieces(refs[:8], held, 0, sems)()
    width, part = feed.shape[1], mixed.shape[1]

    def feed_step(p, unused):
        at = pl.ds(pl.multiple_of(p * (width // 8), width // 8), width // 8)
        feed[:, at] = mxu(
            mixed[...], held[0, p].reshape(width // 8, part), NT
        ).astype(BF16)
        return unused

    lax.fori_loop(0, 8, feed_step, 0)


def split_kernel(*refs):
    result = refs[-1]
    for i, matrix in enumerate(refs[:-1]):
        result[0, i] = matrix[...]


def split(*matrices):
    rows, columns = matrices[0].shape
    count, part = len(matrices), columns // 4
    return pl.pallas_call(
        split_kernel,
        out_shape=jax.ShapeDtypeStruct((4, count, rows, part), matrices[0].dtype),
        grid=(4,),
        in_specs=[pl.BlockSpec((rows, part), lambda i: (0, i))] * count,
        out_specs=pl.BlockSpec((1, count, rows, part), lambda i: (i, 0, 0, 0)),
        cost_estimate=NO_COST,
    )(*matrices)


def merge_kernel(parts, result):
    result[...] = parts[0].astype(F32)


def merge(parts):
    _, rows, part = parts.shape
    return pl.pallas_call(
        merge_kernel,
        out_shape=jax.ShapeDtypeStruct((rows, 4 * part), F32),
        grid=(4,),
        in_specs=[pl.BlockSpec((1, rows, part), lambda i: (i, 0, 0))],
        out_specs=pl.BlockSpec((rows, part), lambda i: (0, i)),
        cost_estimate=NO_COST,
    )(parts)


NO_COST = pl.CostEstimate(flops=1, bytes_accessed=1, transcendentals=0)


def local_call(kernel, outs, scratch, *args, far=0, scalars=0):
    near = [pl.BlockSpec(memory_space=pltpu.SMEM)] * scalars
    near = near + [pl.BlockSpec(memory_space=pltpu.VMEM)] * (len(args) - far - scalars)
    return pl.pallas_call(
        kernel,
        out_shape=outs,
        in_specs=near + [pl.BlockSpec(memory_space=pl.ANY)] * far,
        out_specs=[pl.BlockSpec(memory_space=pltpu.VMEM)] * len(outs),
        scratch_shapes=scratch,
        compiler_params=pltpu.CompilerParams(vmem_limit_bytes=56 << 20),
        cost_estimate=NO_COST,
    )(*args)


def on_device(
    block_input,
    attention_gain,
    query_weight,
    keyvalue_weight,
    output_weight,
    feedforward_gain,
    gate_weight,
    up_weight,
    down_weight,
    document_lengths,
    piece_order,
    output_grad,
    shared_grad,
):
    y, h, l, m, x, c = (lax.axis_index(a) for a in AXES)
    M = lax.axis_size("m")
    tokens, width = block_input.shape[1:]
    rows = query_weight.shape[0]
    query_width = query_weight.shape[1]
    half_width = query_width // 2
    heads = half_width // HEAD_DIM
    hidden_units = gate_weight.shape[1]
    part = hidden_units // 4
    piece_len = tokens // 2

    def inward(value):
        value = value.reshape(tokens, 2, 2, 2, M, 2, 2, rows)
        value = value.transpose(0, 6, 1, 2, 4, 3, 5, 7)
        value = jnp.where(c == 0, value, value[:, ::-1])
        value = jnp.where(y == 0, value, value[:, :, ::-1])
        value = jnp.where(h == 0, value, value[:, :, :, ::-1])
        return value.reshape(tokens, width)

    def outward(value):
        value = value.reshape(tokens, 2, 2, 2, M, 2, 2, rows)
        value = jnp.where(h == 0, value, value[:, :, :, ::-1])
        value = jnp.where(y == 0, value, value[:, :, ::-1])
        value = jnp.where(c == 0, value, value[:, ::-1])
        return value.transpose(0, 2, 3, 5, 4, 6, 1, 7).reshape(tokens, width)

    finish = jnp.cumsum(document_lengths[0])
    starts = finish - document_lengths[0]

    def places(slots):
        order = piece_order[(slots[:, None] * 2 + jnp.arange(2)[None, :]).reshape(-1)]
        return (
            order[:, None] * piece_len + jnp.arange(piece_len, dtype=jnp.int32)[None, :]
        ).reshape(-1)

    def slot(h_at, l_at, m_at, x_at, c_at):
        return (((h_at * 2 + l_at) * M + m_at) * 2 + x_at) * 2 + c_at

    position = places(jnp.stack([slot(h, l, m, x, c), slot(h, l, m, 1 - x, c)]))
    begins = jnp.max(
        jnp.where(starts[None, :] <= position[:, None], starts[None, :], 0), axis=1
    )
    key_position = places(
        jnp.stack(
            [
                slot(h ^ i, l ^ j, m_at, x ^ k, c ^ n)
                for n in range(2)
                for k in range(2)
                for j in range(2)
                for m_at in range(M)
                for i in range(2)
            ]
        )
    )[:, None]
    query_place, query_start = position[None, :], begins[None, :]
    cosine, sine_part = angles(position - begins)

    gains = jnp.stack([attention_gain, feedforward_gain])
    gains = jnp.pad(gains, ((0, 14), (0, 2 * HEAD_DIM - rows)))
    small = jnp.concatenate([keyvalue_weight, gains])

    def halves(weight):
        parts = weight.reshape(rows, 2, half_width).transpose(1, 0, 2)
        return pick(parts, x), pick(parts, 1 - x)

    query_mine, query_sent = halves(query_weight)
    output_mine, output_sent = halves(output_weight)

    small_x, query_x, output_x = sync(
        swap(small, "x"), swap(query_sent, "x"), swap(output_sent, "x")
    )
    small = pair(small, small_x, x)
    query_part, output_part = pair(query_mine, query_x, x), pair(output_mine, output_x, x)
    input_mine, small, gate_weight, up_weight, down_weight = sync(
        inward(block_input[0]), small, gate_weight, up_weight, down_weight
    )
    feed_parts = split(gate_weight, up_weight, down_weight)
    small_l, query_l, output_l, input_other = sync(
        swap(small, "l"), swap(query_part, "l"), swap(output_part, "l"), swap(input_mine, "x")
    )
    small = gather_m(pair(small, small_l, l), 0)
    query_part = gather_m(pair(query_part, query_l, l), 0)
    output_part = gather_m(pair(output_part, output_l, l), 0)
    small, query_part, feed_parts = sync(small, query_part, feed_parts)
    query_h = swap(query_part, "h")
    small_h = sync(swap(small, "h"))[0]
    small, feed_parts = sync(jnp.stack([small, small_h]), feed_parts)
    feed = gather_m(lax.all_to_all(feed_parts, ("l", "x"), 0, 0), 0)
    feed = feed.reshape(M * 4, 3, rows, part)
    small_y = sync(swap(small, "y"))[0]
    small = jnp.stack([small, small_y]).reshape(4, M * 4, rows + 16, 2 * HEAD_DIM)
    small_c, input_other, query_h = sync(swap_core(small), input_other, query_h)
    small = jnp.stack([small, small_c])
    small = small.reshape(width // rows, rows + 16, 2 * HEAD_DIM)
    keyvalue_full = small[:, :rows].reshape(width, 2 * HEAD_DIM)
    gain_one = small[:, rows, :rows].reshape(1, width).astype(F32)
    gain_two = small[:, rows + 1, :rows].reshape(1, width).astype(F32)
    def normalize(value):
        value = value.astype(F32)
        scale = lax.rsqrt(jnp.mean(value * value, axis=-1, keepdims=True) + EPSILON)
        normed = value * scale
        return value, scale, normed, low(normed * gain_one)

    inputs, scale_one, normed_one, normed_mine_low = normalize(input_mine)
    keyvalue_sum = dot(normed_mine_low, keyvalue_full)
    shared_mine = low(
        jnp.concatenate(
            [
                rotate(keyvalue_sum[:, :HEAD_DIM], cosine[:tokens], sine_part[:tokens]),
                keyvalue_sum[:, HEAD_DIM:],
            ],
            -1,
        )
    )
    query_part, keyvalue_sum, key_position, query_place, query_start, cosine_t, sine_t = sync(
        jnp.stack([query_part, query_h]),
        keyvalue_sum,
        key_position,
        query_place,
        query_start,
        cosine.T,
        sine_part.T,
    )
    query_y = swap(query_part, "y")
    shared_h, input_other = sync(swap(shared_mine, "h"), input_other)
    gathered = gather_m(jnp.stack([shared_mine, shared_h]), 0)
    gathered, input_other, output_part = sync(gathered, input_other, output_part)
    output_h = swap(output_part, "h")
    normed_one_low = jnp.concatenate([normed_mine_low, normalize(input_other)[3]])
    shared_l, normed_one_low, feed = sync(swap(gathered, "l"), normed_one_low, feed)
    gate, up, down, gathered = sync(
        *(feed[:, i] for i in range(3)), jnp.stack([gathered, shared_l])
    )
    shared_x, query_y, output_h = sync(swap(gathered, "x"), query_y, output_h)
    gathered = jnp.stack([gathered, shared_x]).reshape(4, -1, 2 * HEAD_DIM)
    query_part = jnp.stack([query_part, query_y]).reshape(-1, half_width)
    query_part, gathered = sync(query_part, gathered)
    query_c = core_parts(query_part)
    shared_c, *query_c = sync(swap_core(gathered), *query_c)
    output_part = jnp.stack([output_part, output_h])
    output_part, gate, shared_c = sync(output_part, gate, shared_c)
    output_y = swap(output_part, "y")
    gate_h = swap(gate, "h")
    gate_sent, query_place = sync(gate, query_place, *query_c)[:2]
    gate_y = swap(gate_sent, "y")
    gathered = jnp.stack([gathered, shared_c]).reshape(-1, 2 * HEAD_DIM)
    stream_len = gathered.shape[0]
    grad_mine = inward(output_grad[0])
    wide = (half_width, 2 * tokens)
    places_used = (key_position, query_place, query_start)
    query_rot, attended, attended_low, lse = local_call(
        attend_kernel,
        [
            jax.ShapeDtypeStruct(wide, BF16),
            jax.ShapeDtypeStruct(wide, F32),
            jax.ShapeDtypeStruct(wide, BF16),
            jax.ShapeDtypeStruct((heads, 2 * tokens), F32),
        ],
        [
            pltpu.VMEM((stream_len, 2 * tokens), F32),
            pltpu.VMEM((HEAD_DIM, stream_len), BF16),
        ],
        normed_one_low, query_part, *query_c, gathered, cosine_t, sine_t, *places_used,
    )
    attended_low, output_y, output_part, gate_h, gate_y, grad_mine, grad_copies = sync(
        attended_low, output_y, output_part, gate_h, gate_y, grad_mine, four_of(grad_mine)
    )
    output_part = jnp.stack([output_part, output_y]).reshape(-1, half_width)
    output_c = swap_core(output_part)
    up_sent, attended_low = sync(up, attended_low)
    up_h, up_y = swap(up_sent, "h"), swap(up_sent, "y")
    output_part, output_c, attended_low = sync(output_part, output_c, attended_low)
    output_full = jnp.concatenate([output_part, output_c])
    branch = lax.dot_general(
        attended_low, output_full, (((0,), (1,)), ((), ())), preferred_element_type=F32
    )
    branch, gate_h = sync(branch, gate_h)
    gate_far = swap(gate_h, "y")
    branch_x, up_h, up_y, gate_far = sync(
        swap(low(branch[tokens:]), "x"), up_h, up_y, gate_far
    )
    hidden = inputs + (branch[:tokens] + branch_x.astype(F32))

    down_sent, branch_x = sync(down, branch_x)
    down_h, up_far, down_y = swap(down_sent, "h"), swap(up_h, "y"), swap(down_sent, "y")
    scale_two = lax.rsqrt(jnp.mean(hidden * hidden, axis=-1, keepdims=True) + EPSILON)
    normed_two = hidden * scale_two
    normed_two_low = low(normed_two * gain_two)
    normed_two_low = gather_group(four_of(normed_two_low)).reshape(-1, width)
    up_far, *sent = sync(up_far, gate, gate_h, gate_y, gate_far, up, up_h, up_y)
    near_c = [swap(piece, "c") for piece in sent]
    normed_two_low, down_h, down_y, *near_c = sync(normed_two_low, down_h, down_y, *near_c)
    down_far = swap(down_h, "y")
    gate_c = near_c[:4]
    up_sent, grad_sent = sync(up_far, grad_copies, normed_two_low)[:2]
    late_c = [swap(up_sent, "c")]
    up_c = near_c[4:] + late_c
    grad_low = gather_group(grad_sent).reshape(-1, width)
    gate_all = [gate, gate_h, gate_y, gate_far, *gate_c]
    up_all = [up, up_h, up_y, up_far, *up_c]
    group = 4 * tokens
    units = jax.ShapeDtypeStruct((group, part), BF16)
    unit_sums = jax.ShapeDtypeStruct((group, part), F32)
    features = jax.ShapeDtypeStruct((group, width), BF16)

    def held(count):
        return [
            pltpu.VMEM((count, 8, M * 4, rows, part), BF16),
            pltpu.SemaphoreType.DMA((count, 8)),
        ]

    down_c = [swap(piece, "c") for piece in (down, down_h, down_y)]
    gate_sum, up_sum = local_call(
        gate_up_kernel, [unit_sums] * 2, held(2), normed_two_low, *gate_all, *up_all, far=16
    )
    down_far, gate_sum, *down_c = sync(down_far, gate_sum, *down_c)
    down_all = [down, down_h, down_y, down_far, *down_c, swap(down_far, "c")]
    order = jnp.stack(
        [
            ((y ^ j) * 2 + (h ^ k)) * 2 + (c ^ i)
            for i in range(2)
            for j in range(2)
            for k in range(2)
        ]
    )
    mixed_low, grad_gate, grad_up, grad_two = local_call(
        feed_kernel,
        [units, units, units, features],
        held(3),
        grad_low, gate_sum, up_sum, *down_all, *gate_all, *up_all,
        far=24,
    )

    half, block = width // 2, width // 8
    half_rows = jax.ShapeDtypeStruct((half, part), BF16)
    mixed_low, grad_gate, grad_up, grad_two = sync(mixed_low, grad_gate, grad_up, grad_two)
    grad_two = scatter_group(grad_two.reshape(4, tokens, width))
    both_grad = local_call(
        outer_all_kernel,
        [jax.ShapeDtypeStruct((8, 2, block, part), BF16)],
        [],
        order, normed_two_low, grad_gate, grad_up,
        scalars=1,
    )[0]
    mixed_low, both_grad = sync(mixed_low, both_grad)
    both_grad = lax.psum_scatter(both_grad, ("y", "h", "c"), scatter_dimension=0)
    down_far_half, down_near = local_call(
        outer_kernel, [half_rows] * 2, [], grad_low, mixed_low
    )
    mixed_low, down_far_half = sync(mixed_low, down_far_half)
    down_got = swap(down_far_half, "c")
    def quarter(i, *more):
        at = slice(i * block, (i + 1) * block)
        total = down_near[at].astype(F32) + down_got[at].astype(F32)
        for other in more:
            total = total + other.astype(F32)
        return low(total)

    grad_two, down_got = sync(grad_two, down_got)
    across = (((0,), (1,)), ((), ()))
    grad_hidden = grad_mine.astype(F32) + norm_back(grad_two * gain_two, normed_two, scale_two)
    grad_hidden_low, grad_two = sync(low(grad_hidden), grad_two)
    hidden_x = swap(grad_hidden_low, "x")
    down_y3, down_y2 = swap(quarter(3), "y"), swap(quarter(2), "y")
    mixed_low = sync(mixed_low, grad_hidden_low)[0]
    feed_out = local_call(
        feed_out_kernel,
        [features],
        held(1),
        mixed_low, *down_all,
        far=8,
    )[0]
    hidden_x, feed_out = sync(hidden_x, feed_out)
    feed_out = scatter_group(feed_out.reshape(4, tokens, width))
    grad_hidden_low = jnp.concatenate([grad_hidden_low, hidden_x])
    query_grad_low, kv_grad = local_call(
        attend_back_kernel,
        [
            jax.ShapeDtypeStruct(wide, BF16),
            jax.ShapeDtypeStruct((stream_len, 2 * HEAD_DIM), F32),
        ],
        [
            pltpu.VMEM((stream_len, 2 * tokens), F32),
            pltpu.VMEM((HEAD_DIM, stream_len), BF16),
        ],
        query_rot, gathered, grad_hidden_low, output_full, attended, lse, cosine_t, sine_t,
        *places_used,
    )
    query_grad_low, kv_grad, grad_hidden_low = sync(query_grad_low, kv_grad, grad_hidden_low)

    def fold_l(total):
        total = total.reshape(2, 2, M, 2, 2, rows, -1)
        return pick(total, l, 3), swap(low(pick(total, 1 - l, 3)), "l")

    def give_x(total, got):
        total = total + got.astype(F32)
        return pick(total, x, 3), swap(low(pick(total, 1 - x, 3)), "x")

    def take_x(total, got):
        got = got.astype(F32)
        both = pair(total[..., :half_width], got[..., :half_width], x, 4)
        both = both.reshape(2, 2, M, rows, query_width)
        return jnp.concatenate([both, (total + got)[..., half_width:]], -1)

    def next_fold(total, axis):
        return total[0], swap(low(total[1]), axis)

    kv_half = kv_grad.shape[0] // 2
    kv_sent = low(kv_grad[kv_half:]).reshape(4, -1, 2 * HEAD_DIM)
    output_term = low(
        lax.dot_general(grad_hidden_low, attended_low, across, preferred_element_type=F32)
    )
    kv_got, query_grad_low, output_term = sync(
        swap_core(kv_sent), query_grad_low, output_term
    )
    output_got = swap_core(output_term[half:])
    kv_grad = kv_grad[:kv_half].reshape(4, M, 2, tokens, 2 * HEAD_DIM)
    kv_grad = kv_grad + kv_got.astype(F32).reshape(kv_grad.shape)
    kv_got = swap(low(kv_grad[2:]), "x")
    query_term = low(
        lax.dot_general(normed_one_low, query_grad_low, across, preferred_element_type=F32)
    )
    kv_got, query_term, output_got = sync(kv_got, query_term, output_got)
    kv_grad = kv_grad[:2] + kv_got.astype(F32)
    kv_got = swap(low(kv_grad[1]), "l")
    query_full = jnp.concatenate([query_part, *query_c])
    grad_one = lax.dot_general(
        query_grad_low, query_full, (((0,), (1,)), ((), ())), preferred_element_type=F32
    )
    kv_got, grad_one, feed_out = sync(kv_got, grad_one, feed_out)
    grad_one_x = swap(low(grad_one[tokens:]), "x")
    output_total, output_got = fold_l(
        output_term[:half].astype(F32) + output_got.astype(F32)
    )
    kv_grad = kv_grad[0] + kv_got.astype(F32)
    kv_got, grad_one_x, down_y3 = sync(swap(low(kv_grad[:, 1]), "h"), grad_one_x, down_y3)
    down_h1 = swap(quarter(1, down_y3), "h")
    kv_mine = scatter_m(kv_grad[:, 0] + kv_got.astype(F32), 0) + shared_grad[0].astype(F32)
    keyvalue_grad_low = low(
        jnp.concatenate(
            [
                rotate(kv_mine[:, :HEAD_DIM], cosine[:tokens], -sine_part[:tokens]),
                kv_mine[:, HEAD_DIM:],
            ],
            -1,
        )
    )
    grad_one = grad_one[:tokens] + grad_one_x.astype(F32)
    grad_one = grad_one + contract_last(keyvalue_grad_low, keyvalue_full)
    gain_one_grad = jnp.sum(grad_one * normed_one, axis=0)
    gain_two_grad = jnp.sum(grad_two * normed_two, axis=0)
    small_grad = contract_first(normed_mine_low, keyvalue_grad_low)
    small_gains = jnp.stack([gain_one_grad, gain_two_grad], -1)
    small_gains = jnp.pad(small_gains, ((0, 0), (0, HEAD_DIM - 2)))
    query_total = jnp.concatenate([query_term, low(small_grad), low(small_gains)], -1)
    query_got = swap_core(query_total[half:])
    query_got, output_got, query_total = sync(query_got, output_got, query_total)
    query_total, query_got = fold_l(query_total[:half].astype(F32) + query_got.astype(F32))
    output_total, output_got = give_x(output_total, output_got)
    input_grad = outward(
        grad_hidden + norm_back(grad_one * gain_one, normed_one, scale_one)
    )[None]
    block_output = outward(low(hidden + feed_out))[None]
    output_got, down_y2 = sync(output_got, down_y2)
    output_total, output_got = next_fold(take_x(output_total, output_got), "y")
    query_got, output_got = sync(query_got, output_got)
    query_total, query_got = give_x(query_total, query_got)
    output_total, output_got = next_fold(output_total + output_got.astype(F32), "h")
    query_got, output_got, down_h1, both_grad = sync(query_got, output_got, down_h1, both_grad)
    query_total, query_got = next_fold(take_x(query_total, query_got), "y")
    output_weight_grad = scatter_m(output_total + output_got.astype(F32), 0)
    def finish_feed(own):
        own = low(scatter_m(own, 0))
        got = lax.all_to_all(own, ("l", "x"), 0, 0)
        return [merge(got[:, i]) for i in range(own.shape[1])]

    both_grad = both_grad.reshape(2, M, 4, rows, part).transpose(1, 2, 0, 3, 4)
    gate_weight_grad, up_weight_grad = finish_feed(both_grad)
    query_total, query_got = next_fold(query_total + query_got.astype(F32), "h")
    down_own = sync(quarter(0, down_h1, down_y2), gate_weight_grad)[0]
    (down_weight_grad,) = finish_feed(down_own.reshape(M, 4, 1, rows, part))
    query_total = scatter_m(query_total + query_got.astype(F32), 0)
    query_weight_grad = query_total[:, :query_width]
    keyvalue_weight_grad = query_total[:, query_width : query_width + 2 * HEAD_DIM]
    gain_one_mine = query_total[:, query_width + 2 * HEAD_DIM]
    gain_two_mine = query_total[:, query_width + 2 * HEAD_DIM + 1]
    return (
        block_output,
        shared_mine[None],
        input_grad,
        gain_one_mine,
        query_weight_grad,
        keyvalue_weight_grad,
        output_weight_grad,
        gain_two_mine,
        gate_weight_grad,
        up_weight_grad,
        down_weight_grad,
    )


def solution(mesh):
    streams, seq = mesh.shape["dp"], mesh.shape["seq"]
    fine = Mesh(mesh.devices.reshape(streams, 2, 2, seq // 16, 2, 2), tuple(AXES))
    stream = P("y", tuple(AXES[1:]), None)
    vector, matrix = P(tuple(AXES)), P(tuple(AXES), None)
    return jax.shard_map(
        on_device,
        mesh=fine,
        in_specs=(
            stream,
            vector,
            matrix,
            matrix,
            matrix,
            vector,
            matrix,
            matrix,
            matrix,
            P("y", None),
            P(),
            stream,
            stream,
        ),
        out_specs=(
            stream,
            stream,
            stream,
            vector,
            matrix,
            matrix,
            matrix,
            vector,
            matrix,
            matrix,
            matrix,
        ),
        check_vma=False,
    )
```

```python
import functools
import math

import jax
import jax.numpy as jnp
from jax import lax
from jax.experimental import pallas as pl
from jax.experimental.pallas import tpu as pltpu
from jax.sharding import Mesh
from jax.sharding import PartitionSpec as P

HEAD_DIM = 128
EPSILON = 1e-05
NEGATIVE = -1e30
AXES = "yhlmxc"
BF16 = jnp.bfloat16
F32 = jnp.float32


def angles(offset):
    half_dim = HEAD_DIM // 2
    frequency = jnp.exp(
        jnp.arange(half_dim, dtype=F32) * (-2.0 * math.log(10000.0) / HEAD_DIM)
    )
    phases = offset.astype(F32)[:, None] * frequency[None, :]
    return (jnp.cos(phases), jnp.sin(phases))


def rotate(vectors, cosine, sine_part):
    half_dim = vectors.shape[-1] // 2
    first, second = vectors[..., :half_dim], vectors[..., half_dim:]
    return jnp.concatenate(
        [first * cosine - second * sine_part, second * cosine + first * sine_part], -1
    )


def dot(left, right):
    return jnp.dot(left, right, preferred_element_type=F32)


def contract_last(left, right):
    return lax.dot_general(left, right, (((1,), (1,)), ((), ())), preferred_element_type=F32)


def contract_first(left, right):
    return lax.dot_general(left, right, (((0,), (0,)), ((), ())), preferred_element_type=F32)


def norm_back(grad_normed, normed, scale_rows):
    return scale_rows * (
        grad_normed - normed * jnp.mean(grad_normed * normed, axis=-1, keepdims=True)
    )


def swap(value, axis):
    return lax.ppermute(value, axis, [(0, 1), (1, 0)])


def swap_core(value):
    return jnp.concatenate(core_parts(value))


def core_parts(value):
    size = value.shape[0] // 4
    return [swap(value[i * size : (i + 1) * size], "c") for i in range(4)]


def low(value):
    return value.astype(BF16)


def sync(*values):
    return lax.optimization_barrier(values)


def pick(stacked, index, axis=0):
    return lax.dynamic_index_in_dim(stacked, index, axis, keepdims=False)


def pair(own, other, index, axis=0):
    return jnp.where(
        index == 0, jnp.stack([own, other], axis), jnp.stack([other, own], axis)
    )


def gather_m(value, axis):
    if lax.axis_size("m") > 1:
        return lax.all_gather(value, "m", axis=axis)
    return jnp.expand_dims(value, axis)


def scatter_m(value, axis):
    if lax.axis_size("m") > 1:
        return lax.psum_scatter(value, "m", scatter_dimension=axis)
    return lax.squeeze(value, (axis,))


def fold(total, axis):
    half = total.shape[0] // 2
    return total[:half].astype(F32) + swap(low(total[half:]), axis).astype(F32)


def four_of(value):
    return jnp.broadcast_to(value, (4, *value.shape))


def gather_group(copies):
    return lax.all_to_all(copies, ("l", "x"), 0, 0)


def scatter_group(value):
    return jnp.sum(lax.all_to_all(low(value), ("l", "x"), 0, 0).astype(F32), axis=0)


LOG2E = math.log2(math.e)
SCALE = 1.0 / math.sqrt(HEAD_DIM)
NT = (((1,), (1,)), ((), ()))
NN = (((1,), (0,)), ((), ()))


def mxu(left, right, dims):
    return lax.dot_general(left, right, dims, preferred_element_type=F32)


def turn(vectors, cosine, sine_part):
    half = HEAD_DIM // 2
    first, second = vectors[:half], vectors[half:]
    return jnp.concatenate(
        [first * cosine - second * sine_part, second * cosine + first * sine_part], 0
    )


def fill_bias(bias, key_place, query_place, query_start):
    keys = bias.shape[0]
    block = 256
    for i in range(keys // block):
        at = key_place[i * block : (i + 1) * block, :]
        fits = (at <= query_place[...]) & (at >= query_start[...])
        bias[i * block : (i + 1) * block, :] = jnp.where(fits, 0.0, NEGATIVE)


def each_pair(one, count, keys):
    def step(pair, unused):
        one(pair * 2, pl.ds(pl.multiple_of(pair * 2 * HEAD_DIM, 2 * HEAD_DIM), 2 * HEAD_DIM))
        return unused

    if keys > 2048:
        lax.fori_loop(0, count // 2, step, 0)
    else:
        for pair in range(count // 2):
            step(pair, 0)


def rows_of(head):
    return pl.ds(pl.multiple_of(head * HEAD_DIM, HEAD_DIM), HEAD_DIM)


def attend_kernel(
    normed, near, far_0, far_1, far_2, far_3, keyvalue, cosine, sine_part, key_place,
    query_place, query_start, query_rot, attended, attended_low, lse, bias, value_t,
):
    fill_bias(bias, key_place, query_place, query_start)
    value_t[...] = keyvalue[:, HEAD_DIM:].T
    parts = [(0, near)]
    for part in (far_0, far_1, far_2, far_3):
        parts.append((parts[-1][0] + parts[-1][1].shape[0], part))

    def one(first, columns):
        total = sum(
            mxu(normed[:, at : at + part.shape[0]], part[:, columns], NN) for at, part in parts
        )
        turned = total.T
        for i in range(2):
            at = rows_of(first + i)
            query = turn(
                turned[i * HEAD_DIM : (i + 1) * HEAD_DIM], cosine[...], sine_part[...]
            ).astype(BF16)
            query_rot[at, :] = query
            scores = mxu(keyvalue[:, :HEAD_DIM], query, NN) * (SCALE * LOG2E) + bias[...]
            top = jnp.max(scores, axis=0, keepdims=True)
            weights = jnp.exp2(scores - top)
            total = jnp.sum(weights, axis=0, keepdims=True)
            result = mxu(value_t[...], weights.astype(BF16), NN) / total
            attended[at, :] = result
            attended_low[at, :] = result.astype(BF16)
            lse[pl.ds(first + i, 1), :] = top + jnp.log2(total)

    each_pair(one, query_rot.shape[0] // HEAD_DIM, keyvalue.shape[0])


def attend_back_kernel(
    query_rot, keyvalue, grad_hidden, output_weight, attended, lse, cosine, sine_part,
    key_place, query_place, query_start, query_grad, kv_grad, bias, key_t,
):
    fill_bias(bias, key_place, query_place, query_start)
    kv_grad[...] = jnp.zeros_like(kv_grad)
    key_t[...] = keyvalue[:, :HEAD_DIM].T

    def one(first, columns):
        turned = mxu(grad_hidden[...], output_weight[:, columns], NN).T.astype(BF16)
        for i in range(2):
            at = rows_of(first + i)
            query = query_rot[at, :]
            grad_head = turned[i * HEAD_DIM : (i + 1) * HEAD_DIM]
            delta = jnp.sum(grad_head.astype(F32) * attended[at, :], axis=0, keepdims=True)
            scores = mxu(keyvalue[:, :HEAD_DIM], query, NN) * (SCALE * LOG2E) + bias[...]
            probs = jnp.exp2(scores - lse[pl.ds(first + i, 1), :])
            grad_probs = mxu(keyvalue[:, HEAD_DIM:], grad_head, NN)
            grad_scores = (probs * (grad_probs - delta)).astype(BF16)
            kv_grad[:, :HEAD_DIM] += mxu(grad_scores, query, NT) * SCALE
            kv_grad[:, HEAD_DIM:] += mxu(probs.astype(BF16), grad_head, NT)
            grad_query = mxu(key_t[...], grad_scores, NN) * SCALE
            query_grad[at, :] = turn(grad_query, cosine[...], -sine_part[...]).astype(BF16)

    each_pair(one, query_rot.shape[0] // HEAD_DIM, keyvalue.shape[0])


def columns_of(width):
    return width // 256, width % 256


def each_block(width, body):
    full, rest = columns_of(width)

    def step(i, unused):
        body(pl.ds(pl.multiple_of(i * 256, 256), 256))
        return unused

    lax.fori_loop(0, full, step, 0)
    if rest:
        body(pl.ds(full * 256, rest))


def load_pieces(pieces, held, slot, sems):
    copies = [
        pltpu.make_async_copy(piece, held.at[slot, p], sems.at[slot, p])
        for p, piece in enumerate(pieces)
    ]
    for copy in copies:
        copy.start()

    def wait():
        for copy in copies:
            copy.wait()

    return wait


def gate_up_kernel(normed, *refs):
    gate_sum, up_sum, held, sems = refs[16:]
    waits = [load_pieces(refs[8 * i : 8 * i + 8], held, i, sems) for i in range(2)]
    width, part = normed.shape[1], gate_sum.shape[1]
    for slot, result in enumerate((gate_sum, up_sum)):
        waits[slot]()

        def step(at):
            result[:, at] = mxu(
                normed[...], held[slot, :, :, :, at].reshape(width, at.size), NN
            )

        each_block(part, step)


def feed_kernel(grad, gate_sum, up_sum, *refs):
    mixed, grad_gate, grad_up, grad_two, held, sems = refs[24:]
    waits = [load_pieces(refs[8 * i : 8 * i + 8], held, i, sems) for i in range(3)]
    width, part = grad.shape[1], mixed.shape[1]
    waits[0]()

    def down_step(at):
        grad_mixed = mxu(grad[...], held[0, :, :, :, at].reshape(width, at.size), NN)
        gate, up = gate_sum[:, at], up_sum[:, at]
        sigmoid_gate = jax.nn.sigmoid(gate)
        silu_gate = gate * sigmoid_gate
        mixed[:, at] = (silu_gate * up).astype(BF16)
        grad_up[:, at] = (grad_mixed * silu_gate).astype(BF16)
        grad_gate[:, at] = (
            grad_mixed * up * sigmoid_gate * (1.0 + gate * (1.0 - sigmoid_gate))
        ).astype(BF16)

    each_block(part, down_step)
    waits[1]()
    waits[2]()

    def two_step(p, unused):
        at = pl.ds(pl.multiple_of(p * (width // 8), width // 8), width // 8)
        grad_two[:, at] = (
            mxu(grad_gate[...], held[1, p].reshape(width // 8, part), NT)
            + mxu(grad_up[...], held[2, p].reshape(width // 8, part), NT)
        ).astype(BF16)
        return unused

    lax.fori_loop(0, 8, two_step, 0)


def outer_kernel(left, *refs):
    count = len(refs) // 3
    rights, results = refs[:count], refs[count:]
    rows = left.shape[1] // 8

    def step(p, unused):
        to = pl.ds(pl.multiple_of(p * rows, rows), rows)
        for part in range(2):
            first = 4 * (1 - part)
            at = pl.ds(pl.multiple_of((first + p) * rows, rows), rows)
            turned = left[:, at].T
            for i, right in enumerate(rights):
                result = results[2 * i + part]
                result[to, :] = mxu(turned, right[...], NN).astype(result.dtype)
        return unused

    lax.fori_loop(0, 4, step, 0)


def outer_all_kernel(order, left, *refs):
    *rights, result = refs
    rows = left.shape[1] // 8

    def step(p, unused):
        at = pl.ds(pl.multiple_of(p * rows, rows), rows)
        turned = left[:, at].T
        for i, right in enumerate(rights):
            result[order[p], i] = mxu(turned, right[...], NN).astype(result.dtype)
        return unused

    lax.fori_loop(0, 8, step, 0)


def feed_out_kernel(mixed, *refs):
    feed, held, sems = refs[8:]
    load_pieces(refs[:8], held, 0, sems)()
    width, part = feed.shape[1], mixed.shape[1]

    def feed_step(p, unused):
        at = pl.ds(pl.multiple_of(p * (width // 8), width // 8), width // 8)
        feed[:, at] = mxu(
            mixed[...], held[0, p].reshape(width // 8, part), NT
        ).astype(BF16)
        return unused

    lax.fori_loop(0, 8, feed_step, 0)


def split_kernel(*refs):
    result = refs[-1]
    for i, matrix in enumerate(refs[:-1]):
        result[0, i] = matrix[...]


def split(*matrices):
    rows, columns = matrices[0].shape
    count, part = len(matrices), columns // 4
    return pl.pallas_call(
        split_kernel,
        out_shape=jax.ShapeDtypeStruct((4, count, rows, part), matrices[0].dtype),
        grid=(4,),
        in_specs=[pl.BlockSpec((rows, part), lambda i: (0, i))] * count,
        out_specs=pl.BlockSpec((1, count, rows, part), lambda i: (i, 0, 0, 0)),
        cost_estimate=NO_COST,
    )(*matrices)


def merge_kernel(parts, result):
    result[...] = parts[0].astype(F32)


def merge(parts):
    _, rows, part = parts.shape
    return pl.pallas_call(
        merge_kernel,
        out_shape=jax.ShapeDtypeStruct((rows, 4 * part), F32),
        grid=(4,),
        in_specs=[pl.BlockSpec((1, rows, part), lambda i: (i, 0, 0))],
        out_specs=pl.BlockSpec((rows, part), lambda i: (0, i)),
        cost_estimate=NO_COST,
    )(parts)


NO_COST = pl.CostEstimate(flops=1, bytes_accessed=1, transcendentals=0)


def local_call(kernel, outs, scratch, *args, far=0, scalars=0):
    near = [pl.BlockSpec(memory_space=pltpu.SMEM)] * scalars
    near = near + [pl.BlockSpec(memory_space=pltpu.VMEM)] * (len(args) - far - scalars)
    return pl.pallas_call(
        kernel,
        out_shape=outs,
        in_specs=near + [pl.BlockSpec(memory_space=pl.ANY)] * far,
        out_specs=[pl.BlockSpec(memory_space=pltpu.VMEM)] * len(outs),
        scratch_shapes=scratch,
        compiler_params=pltpu.CompilerParams(vmem_limit_bytes=56 << 20),
        cost_estimate=NO_COST,
    )(*args)


def on_device(
    block_input,
    attention_gain,
    query_weight,
    keyvalue_weight,
    output_weight,
    feedforward_gain,
    gate_weight,
    up_weight,
    down_weight,
    document_lengths,
    piece_order,
    output_grad,
    shared_grad,
):
    y, h, l, m, x, c = (lax.axis_index(a) for a in AXES)
    M = lax.axis_size("m")
    tokens, width = block_input.shape[1:]
    rows = query_weight.shape[0]
    query_width = query_weight.shape[1]
    half_width = query_width // 2
    heads = half_width // HEAD_DIM
    hidden_units = gate_weight.shape[1]
    part = hidden_units // 4
    piece_len = tokens // 2

    def inward(value):
        value = value.reshape(tokens, 2, 2, 2, M, 2, 2, rows)
        value = value.transpose(0, 6, 1, 2, 4, 3, 5, 7)
        value = jnp.where(c == 0, value, value[:, ::-1])
        value = jnp.where(y == 0, value, value[:, :, ::-1])
        value = jnp.where(h == 0, value, value[:, :, :, ::-1])
        return value.reshape(tokens, width)

    def outward(value):
        value = value.reshape(tokens, 2, 2, 2, M, 2, 2, rows)
        value = jnp.where(h == 0, value, value[:, :, :, ::-1])
        value = jnp.where(y == 0, value, value[:, :, ::-1])
        value = jnp.where(c == 0, value, value[:, ::-1])
        return value.transpose(0, 2, 3, 5, 4, 6, 1, 7).reshape(tokens, width)

    finish = jnp.cumsum(document_lengths[0])
    starts = finish - document_lengths[0]

    def places(slots):
        order = piece_order[(slots[:, None] * 2 + jnp.arange(2)[None, :]).reshape(-1)]
        return (
            order[:, None] * piece_len + jnp.arange(piece_len, dtype=jnp.int32)[None, :]
        ).reshape(-1)

    def slot(h_at, l_at, m_at, x_at, c_at):
        return (((h_at * 2 + l_at) * M + m_at) * 2 + x_at) * 2 + c_at

    position = places(jnp.stack([slot(h, l, m, x, c), slot(h, l, m, 1 - x, c)]))
    begins = jnp.max(
        jnp.where(starts[None, :] <= position[:, None], starts[None, :], 0), axis=1
    )
    key_position = places(
        jnp.stack(
            [
                slot(h ^ i, l ^ j, m_at, x ^ k, c ^ n)
                for n in range(2)
                for k in range(2)
                for j in range(2)
                for m_at in range(M)
                for i in range(2)
            ]
        )
    )[:, None]
    query_place, query_start = position[None, :], begins[None, :]
    cosine, sine_part = angles(position - begins)

    gains = jnp.stack([attention_gain, feedforward_gain])
    gains = jnp.pad(gains, ((0, 14), (0, 2 * HEAD_DIM - rows)))
    small = jnp.concatenate([keyvalue_weight, gains])

    def halves(weight):
        parts = weight.reshape(rows, 2, half_width).transpose(1, 0, 2)
        return pick(parts, x), pick(parts, 1 - x)

    query_mine, query_sent = halves(query_weight)
    output_mine, output_sent = halves(output_weight)

    small_x, query_x, output_x = sync(
        swap(small, "x"), swap(query_sent, "x"), swap(output_sent, "x")
    )
    small = pair(small, small_x, x)
    query_part, output_part = pair(query_mine, query_x, x), pair(output_mine, output_x, x)
    input_mine, small, gate_weight, up_weight, down_weight = sync(
        inward(block_input[0]), small, gate_weight, up_weight, down_weight
    )
    feed_parts = split(gate_weight, up_weight, down_weight)
    small_l, query_l, output_l, input_other = sync(
        swap(small, "l"), swap(query_part, "l"), swap(output_part, "l"), swap(input_mine, "x")
    )
    small = gather_m(pair(small, small_l, l), 0)
    query_part = gather_m(pair(query_part, query_l, l), 0)
    output_part = gather_m(pair(output_part, output_l, l), 0)
    small, query_part, feed_parts = sync(small, query_part, feed_parts)
    query_h = swap(query_part, "h")
    small_h = sync(swap(small, "h"))[0]
    small, feed_parts = sync(jnp.stack([small, small_h]), feed_parts)
    feed = gather_m(lax.all_to_all(feed_parts, ("l", "x"), 0, 0), 0)
    feed = feed.reshape(M * 4, 3, rows, part)
    small_y = sync(swap(small, "y"))[0]
    small = jnp.stack([small, small_y]).reshape(4, M * 4, rows + 16, 2 * HEAD_DIM)
    small_c, input_other, query_h = sync(swap_core(small), input_other, query_h)
    small = jnp.stack([small, small_c])
    small = small.reshape(width // rows, rows + 16, 2 * HEAD_DIM)
    keyvalue_full = small[:, :rows].reshape(width, 2 * HEAD_DIM)
    gain_one = small[:, rows, :rows].reshape(1, width).astype(F32)
    gain_two = small[:, rows + 1, :rows].reshape(1, width).astype(F32)
    def normalize(value):
        value = value.astype(F32)
        scale = lax.rsqrt(jnp.mean(value * value, axis=-1, keepdims=True) + EPSILON)
        normed = value * scale
        return value, scale, normed, low(normed * gain_one)

    inputs, scale_one, normed_one, normed_mine_low = normalize(input_mine)
    keyvalue_sum = dot(normed_mine_low, keyvalue_full)
    shared_mine = low(
        jnp.concatenate(
            [
                rotate(keyvalue_sum[:, :HEAD_DIM], cosine[:tokens], sine_part[:tokens]),
                keyvalue_sum[:, HEAD_DIM:],
            ],
            -1,
        )
    )
    query_part, keyvalue_sum, key_position, query_place, query_start, cosine_t, sine_t = sync(
        jnp.stack([query_part, query_h]),
        keyvalue_sum,
        key_position,
        query_place,
        query_start,
        cosine.T,
        sine_part.T,
    )
    query_y = swap(query_part, "y")
    shared_h, input_other = sync(swap(shared_mine, "h"), input_other)
    gathered = gather_m(jnp.stack([shared_mine, shared_h]), 0)
    gathered, input_other, output_part = sync(gathered, input_other, output_part)
    output_h = swap(output_part, "h")
    normed_one_low = jnp.concatenate([normed_mine_low, normalize(input_other)[3]])
    shared_l, normed_one_low, feed = sync(swap(gathered, "l"), normed_one_low, feed)
    gate, up, down, gathered = sync(
        *(feed[:, i] for i in range(3)), jnp.stack([gathered, shared_l])
    )
    shared_x, query_y, output_h = sync(swap(gathered, "x"), query_y, output_h)
    gathered = jnp.stack([gathered, shared_x]).reshape(4, -1, 2 * HEAD_DIM)
    query_part = jnp.stack([query_part, query_y]).reshape(-1, half_width)
    query_part, gathered = sync(query_part, gathered)
    query_c = core_parts(query_part)
    shared_c, *query_c = sync(swap_core(gathered), *query_c)
    output_part = jnp.stack([output_part, output_h])
    output_part, gate, shared_c = sync(output_part, gate, shared_c)
    output_y = swap(output_part, "y")
    gate_h = swap(gate, "h")
    gate_sent, query_place = sync(gate, query_place, *query_c)[:2]
    gate_y = swap(gate_sent, "y")
    gathered = jnp.stack([gathered, shared_c]).reshape(-1, 2 * HEAD_DIM)
    stream_len = gathered.shape[0]
    grad_mine = inward(output_grad[0])
    wide = (half_width, 2 * tokens)
    places_used = (key_position, query_place, query_start)
    query_rot, attended, attended_low, lse = local_call(
        attend_kernel,
        [
            jax.ShapeDtypeStruct(wide, BF16),
            jax.ShapeDtypeStruct(wide, F32),
            jax.ShapeDtypeStruct(wide, BF16),
            jax.ShapeDtypeStruct((heads, 2 * tokens), F32),
        ],
        [
            pltpu.VMEM((stream_len, 2 * tokens), F32),
            pltpu.VMEM((HEAD_DIM, stream_len), BF16),
        ],
        normed_one_low, query_part, *query_c, gathered, cosine_t, sine_t, *places_used,
    )
    attended_low, output_y, output_part, gate_h, gate_y, grad_mine, grad_copies = sync(
        attended_low, output_y, output_part, gate_h, gate_y, grad_mine, four_of(grad_mine)
    )
    output_part = jnp.stack([output_part, output_y]).reshape(-1, half_width)
    output_c = swap_core(output_part)
    up_sent, attended_low = sync(up, attended_low)
    up_h, up_y = swap(up_sent, "h"), swap(up_sent, "y")
    output_part, output_c, attended_low = sync(output_part, output_c, attended_low)
    output_full = jnp.concatenate([output_part, output_c])
    branch = lax.dot_general(
        attended_low, output_full, (((0,), (1,)), ((), ())), preferred_element_type=F32
    )
    branch, gate_h = sync(branch, gate_h)
    gate_far = swap(gate_h, "y")
    branch_x, up_h, up_y, gate_far = sync(
        swap(low(branch[tokens:]), "x"), up_h, up_y, gate_far
    )
    hidden = inputs + (branch[:tokens] + branch_x.astype(F32))

    down_sent, branch_x = sync(down, branch_x)
    down_h, up_far, down_y = swap(down_sent, "h"), swap(up_h, "y"), swap(down_sent, "y")
    scale_two = lax.rsqrt(jnp.mean(hidden * hidden, axis=-1, keepdims=True) + EPSILON)
    normed_two = hidden * scale_two
    normed_two_low = low(normed_two * gain_two)
    normed_two_low = gather_group(four_of(normed_two_low)).reshape(-1, width)
    up_far, *sent = sync(up_far, gate, gate_h, gate_y, gate_far, up, up_h, up_y)
    near_c = [swap(piece, "c") for piece in sent]
    normed_two_low, down_h, down_y, *near_c = sync(normed_two_low, down_h, down_y, *near_c)
    down_far = swap(down_h, "y")
    gate_c = near_c[:4]
    up_sent, grad_sent = sync(up_far, grad_copies, normed_two_low)[:2]
    late_c = [swap(up_sent, "c")]
    up_c = near_c[4:] + late_c
    grad_low = gather_group(grad_sent).reshape(-1, width)
    gate_all = [gate, gate_h, gate_y, gate_far, *gate_c]
    up_all = [up, up_h, up_y, up_far, *up_c]
    group = 4 * tokens
    units = jax.ShapeDtypeStruct((group, part), BF16)
    unit_sums = jax.ShapeDtypeStruct((group, part), F32)
    features = jax.ShapeDtypeStruct((group, width), BF16)

    def held(count):
        return [
            pltpu.VMEM((count, 8, M * 4, rows, part), BF16),
            pltpu.SemaphoreType.DMA((count, 8)),
        ]

    down_c = [swap(piece, "c") for piece in (down, down_h, down_y)]
    gate_sum, up_sum = local_call(
        gate_up_kernel, [unit_sums] * 2, held(2), normed_two_low, *gate_all, *up_all, far=16
    )
    down_far, gate_sum, *down_c = sync(down_far, gate_sum, *down_c)
    down_all = [down, down_h, down_y, down_far, *down_c, swap(down_far, "c")]
    order = jnp.stack(
        [
            ((y ^ j) * 2 + (h ^ k)) * 2 + (c ^ i)
            for i in range(2)
            for j in range(2)
            for k in range(2)
        ]
    )
    mixed_low, grad_gate, grad_up, grad_two = local_call(
        feed_kernel,
        [units, units, units, features],
        held(3),
        grad_low, gate_sum, up_sum, *down_all, *gate_all, *up_all,
        far=24,
    )

    half, block = width // 2, width // 8
    half_rows = jax.ShapeDtypeStruct((half, part), BF16)
    mixed_low, grad_gate, grad_up, grad_two = sync(mixed_low, grad_gate, grad_up, grad_two)
    grad_two = scatter_group(grad_two.reshape(4, tokens, width))
    both_grad = local_call(
        outer_all_kernel,
        [jax.ShapeDtypeStruct((8, 2, block, part), BF16)],
        [],
        order, normed_two_low, grad_gate, grad_up,
        scalars=1,
    )[0]
    mixed_low, both_grad = sync(mixed_low, both_grad)
    both_grad = lax.psum_scatter(both_grad, ("y", "h", "c"), scatter_dimension=0)
    down_far_half, down_near = local_call(
        outer_kernel, [half_rows] * 2, [], grad_low, mixed_low
    )
    mixed_low, down_far_half = sync(mixed_low, down_far_half)
    down_got = swap(down_far_half, "c")
    def quarter(i, *more):
        at = slice(i * block, (i + 1) * block)
        total = down_near[at].astype(F32) + down_got[at].astype(F32)
        for other in more:
            total = total + other.astype(F32)
        return low(total)

    grad_two, down_got = sync(grad_two, down_got)
    across = (((0,), (1,)), ((), ()))
    grad_hidden = grad_mine.astype(F32) + norm_back(grad_two * gain_two, normed_two, scale_two)
    grad_hidden_low, grad_two = sync(low(grad_hidden), grad_two)
    hidden_x = swap(grad_hidden_low, "x")
    down_y3, down_y2 = swap(quarter(3), "y"), swap(quarter(2), "y")
    mixed_low = sync(mixed_low, grad_hidden_low)[0]
    feed_out = local_call(
        feed_out_kernel,
        [features],
        held(1),
        mixed_low, *down_all,
        far=8,
    )[0]
    hidden_x, feed_out = sync(hidden_x, feed_out)
    feed_out = scatter_group(feed_out.reshape(4, tokens, width))
    grad_hidden_low = jnp.concatenate([grad_hidden_low, hidden_x])
    query_grad_low, kv_grad = local_call(
        attend_back_kernel,
        [
            jax.ShapeDtypeStruct(wide, BF16),
            jax.ShapeDtypeStruct((stream_len, 2 * HEAD_DIM), F32),
        ],
        [
            pltpu.VMEM((stream_len, 2 * tokens), F32),
            pltpu.VMEM((HEAD_DIM, stream_len), BF16),
        ],
        query_rot, gathered, grad_hidden_low, output_full, attended, lse, cosine_t, sine_t,
        *places_used,
    )
    query_grad_low, kv_grad, grad_hidden_low = sync(query_grad_low, kv_grad, grad_hidden_low)

    def fold_l(total):
        total = total.reshape(2, 2, M, 2, 2, rows, -1)
        return pick(total, l, 3), swap(low(pick(total, 1 - l, 3)), "l")

    def give_x(total, got):
        total = total + got.astype(F32)
        return pick(total, x, 3), swap(low(pick(total, 1 - x, 3)), "x")

    def take_x(total, got):
        got = got.astype(F32)
        both = pair(total[..., :half_width], got[..., :half_width], x, 4)
        both = both.reshape(2, 2, M, rows, query_width)
        return jnp.concatenate([both, (total + got)[..., half_width:]], -1)

    def next_fold(total, axis):
        return total[0], swap(low(total[1]), axis)

    kv_half = kv_grad.shape[0] // 2
    kv_sent = low(kv_grad[kv_half:]).reshape(4, -1, 2 * HEAD_DIM)
    output_term = low(
        lax.dot_general(grad_hidden_low, attended_low, across, preferred_element_type=F32)
    )
    kv_got, query_grad_low, output_term = sync(
        swap_core(kv_sent), query_grad_low, output_term
    )
    output_got = swap_core(output_term[half:])
    kv_grad = kv_grad[:kv_half].reshape(4, M, 2, tokens, 2 * HEAD_DIM)
    kv_grad = kv_grad + kv_got.astype(F32).reshape(kv_grad.shape)
    kv_got = swap(low(kv_grad[2:]), "x")
    query_term = low(
        lax.dot_general(normed_one_low, query_grad_low, across, preferred_element_type=F32)
    )
    kv_got, query_term, output_got = sync(kv_got, query_term, output_got)
    kv_grad = kv_grad[:2] + kv_got.astype(F32)
    kv_got = swap(low(kv_grad[1]), "l")
    query_full = jnp.concatenate([query_part, *query_c])
    grad_one = lax.dot_general(
        query_grad_low, query_full, (((0,), (1,)), ((), ())), preferred_element_type=F32
    )
    kv_got, grad_one, feed_out = sync(kv_got, grad_one, feed_out)
    grad_one_x = swap(low(grad_one[tokens:]), "x")
    output_total, output_got = fold_l(
        output_term[:half].astype(F32) + output_got.astype(F32)
    )
    kv_grad = kv_grad[0] + kv_got.astype(F32)
    kv_got, grad_one_x, down_y3 = sync(swap(low(kv_grad[:, 1]), "h"), grad_one_x, down_y3)
    down_h1 = swap(quarter(1, down_y3), "h")
    kv_mine = scatter_m(kv_grad[:, 0] + kv_got.astype(F32), 0) + shared_grad[0].astype(F32)
    keyvalue_grad_low = low(
        jnp.concatenate(
            [
                rotate(kv_mine[:, :HEAD_DIM], cosine[:tokens], -sine_part[:tokens]),
                kv_mine[:, HEAD_DIM:],
            ],
            -1,
        )
    )
    grad_one = grad_one[:tokens] + grad_one_x.astype(F32)
    grad_one = grad_one + contract_last(keyvalue_grad_low, keyvalue_full)
    gain_one_grad = jnp.sum(grad_one * normed_one, axis=0)
    gain_two_grad = jnp.sum(grad_two * normed_two, axis=0)
    small_grad = contract_first(normed_mine_low, keyvalue_grad_low)
    small_gains = jnp.stack([gain_one_grad, gain_two_grad], -1)
    small_gains = jnp.pad(small_gains, ((0, 0), (0, HEAD_DIM - 2)))
    query_total = jnp.concatenate([query_term, low(small_grad), low(small_gains)], -1)
    query_got = swap_core(query_total[half:])
    query_got, output_got, query_total = sync(query_got, output_got, query_total)
    query_total, query_got = fold_l(query_total[:half].astype(F32) + query_got.astype(F32))
    output_total, output_got = give_x(output_total, output_got)
    input_grad = outward(
        grad_hidden + norm_back(grad_one * gain_one, normed_one, scale_one)
    )[None]
    block_output = outward(low(hidden + feed_out))[None]
    output_got, down_y2 = sync(output_got, down_y2)
    output_total, output_got = next_fold(take_x(output_total, output_got), "y")
    query_got, output_got = sync(query_got, output_got)
    query_total, query_got = give_x(query_total, query_got)
    output_total, output_got = next_fold(output_total + output_got.astype(F32), "h")
    query_got, output_got, down_h1, both_grad = sync(query_got, output_got, down_h1, both_grad)
    query_total, query_got = next_fold(take_x(query_total, query_got), "y")
    output_weight_grad = scatter_m(output_total + output_got.astype(F32), 0)
    def exchange_feed(own):
        return lax.all_to_all(low(scatter_m(own, 0)), ("l", "x"), 0, 0)

    both_grad = both_grad.reshape(2, M, 4, rows, part).transpose(1, 2, 0, 3, 4)
    both_parts = exchange_feed(both_grad)
    query_total, query_got = next_fold(query_total + query_got.astype(F32), "h")
    down_own, both_parts = sync(quarter(0, down_h1, down_y2), both_parts)
    down_parts = exchange_feed(down_own.reshape(M, 4, 1, rows, part))
    gate_weight_grad, up_weight_grad = (merge(both_parts[:, i]) for i in range(2))
    down_weight_grad = merge(down_parts[:, 0])
    query_total = scatter_m(query_total + query_got.astype(F32), 0)
    query_weight_grad = query_total[:, :query_width]
    keyvalue_weight_grad = query_total[:, query_width : query_width + 2 * HEAD_DIM]
    gain_one_mine = query_total[:, query_width + 2 * HEAD_DIM]
    gain_two_mine = query_total[:, query_width + 2 * HEAD_DIM + 1]
    return (
        block_output,
        shared_mine[None],
        input_grad,
        gain_one_mine,
        query_weight_grad,
        keyvalue_weight_grad,
        output_weight_grad,
        gain_two_mine,
        gate_weight_grad,
        up_weight_grad,
        down_weight_grad,
    )


def solution(mesh):
    streams, seq = mesh.shape["dp"], mesh.shape["seq"]
    fine = Mesh(mesh.devices.reshape(streams, 2, 2, seq // 16, 2, 2), tuple(AXES))
    stream = P("y", tuple(AXES[1:]), None)
    vector, matrix = P(tuple(AXES)), P(tuple(AXES), None)
    return jax.shard_map(
        on_device,
        mesh=fine,
        in_specs=(
            stream,
            vector,
            matrix,
            matrix,
            matrix,
            vector,
            matrix,
            matrix,
            matrix,
            P("y", None),
            P(),
            stream,
            stream,
        ),
        out_specs=(
            stream,
            stream,
            stream,
            vector,
            matrix,
            matrix,
            matrix,
            vector,
            matrix,
            matrix,
            matrix,
        ),
        check_vma=False,
    )
```
